32 devices in a mesh: groups: 2 (over y), wide: 4 (over z), narrow: 4 (over x, core).
Axes of the slice: x: 2, y: 2, z: 4, core: 2. Of those that a mesh axis runs over, the one named last changes fastest.
Arguments:
- grid_state: bfloat16 [128, 128, 256], P(('groups', 'wide'), 'narrow'), parts along dimension 0, may hold values from -6 to 6
- boundary_rows: bfloat16 [1024, 256], P(('groups', 'wide', 'narrow')), parts along dimension 0, may hold values from -6 to 6
- row_count: int32 [32], P(('groups', 'wide', 'narrow')), parts along dimension 0, may hold values from 24 to 32, as said below
- target_x: int32 [1024], P(('groups', 'wide', 'narrow')), parts along dimension 0, may hold values from 0 to 63, as said below
- target_y: int32 [1024], P(('groups', 'wide', 'narrow')), parts along dimension 0, may hold values from 0 to 127, as said below
- g2m_mask: int32 [36, 32, 32], P(None, ('groups', 'wide'), 'narrow'), parts along dimension 1, may hold values 0 or 1
- mesh_cotangent: bfloat16 [32, 32, 256], P(('groups', 'wide'), 'narrow'), parts along dimension 0, may hold values from -6 to 6
- w_force: bfloat16 [256, 256], replicated, may hold values from -0.375 to 0.375
- w_embed: bfloat16 [256, 256], replicated, may hold values from -0.375 to 0.375
- w_message: bfloat16 [256, 256], replicated, may hold values from -0.375 to 0.375
- w_level_one: bfloat16 [256, 256], replicated, may hold values from -0.375 to 0.375
- w_level_two: bfloat16 [256, 256], replicated, may hold values from -0.375 to 0.375
Outputs:
- grad_state: bfloat16 [128, 128, 256], P(('groups', 'wide'), 'narrow'), parts along dimension 0
- grad_rows: bfloat16 [1024, 256], P(('groups', 'wide', 'narrow')), parts along dimension 0
- weight_grads: float32 [10, 256, 256], P('groups'), parts along dimension 0
The draws below stay inside these ranges and needn't reach their ends.
There are 2 independent parts, one for each index of `groups`. The reference program is written for one: setup_inputs(seed, part) draws one part's arguments, and reference() takes and returns one part's arrays. A program takes and returns all parts, laid end to end along the dimension named above; an argument that names none is the same for every part. Nothing has to cross between parts.
Inputs may be any that keep to these rules, and one draw needn't show every extreme that they name: `row_count`: every tile has at least max(16, 24) live rows and tile 0 has 32. The rows of tile t = 4 * w + n target only cells whose second coordinate lies in [n * 32, (n + 1) * 32). Of one tile's live rows at most 16 target cells with the same value of target_x // 16, and tile 0 has exactly 16 such rows for some value. `target_y`: see target_x.
All inputs are finite; a program needn't handle non-finite values. No bound on the sum of `g2m_mask` on one device may be relied on, other than what follows from the above.
Results may differ from the reference program's by a relative error of at most 0.017.
Values may be sent and summed in bfloat16 or wider, within the bound.
No kernel may reach another device: no remote copies, remote signals or barrier semaphores. Data moves between devices by JAX's collectives and lax.ppermute only.
A program may use at most 64 MiB of HBM per device.

```python
import math
import jax
import jax.numpy as jnp

C = 256
GX = 16
GY = 32
CAP = 16
BROWS = 32
BR = 512
NX = 64
NY = 128
MESH_X = 16
MESH_Y = 32


def boundary_plan(key):
    wide_count = NX // GX
    narrow_count = NY // GY
    tiles = wide_count * narrow_count
    keys = jax.random.split(key, 5)
    column = jnp.arange(tiles) % narrow_count
    least_count = max(CAP, BROWS - BROWS // 4)
    counts = jax.random.randint(keys[0], (tiles,), least_count, BROWS + 1)
    counts = counts.at[0].set(BROWS)
    orders = jax.vmap(lambda sub_key: jax.random.permutation(sub_key, wide_count))(jax.random.split(keys[2], tiles))
    block = jnp.arange(BROWS) // CAP
    destination = orders[:, block]
    local_x = jax.random.randint(keys[3], (tiles, BROWS), 0, GX)
    local_y = jax.random.randint(keys[4], (tiles, BROWS), 0, GY)
    cell_x = (destination * GX + local_x).reshape(-1).astype(jnp.int32)
    cell_y = (column[:, None] * GY + local_y).reshape(-1).astype(jnp.int32)
    return (counts.astype(jnp.int32), cell_x, cell_y)


def draw_row_count(key, part):
    return boundary_plan(key)[0]


def draw_target_x(key, part):
    return boundary_plan(key)[1]


def draw_target_y(key, part):
    return boundary_plan(key)[2]


def touch_ends(drawn, own_key, smallest, largest):
    shape = drawn.shape
    index_at = [jax.random.randint(jax.random.fold_in(own_key, axis), (), 0, shape[axis]) for axis in range(len(shape))]
    drawn = drawn.at[tuple(index_at)].set(smallest)
    longest = shape.index(max(shape))
    index_at[longest] = (index_at[longest] + 1) % shape[longest]
    return drawn.at[tuple(index_at)].set(largest)


def block_levels(key, dims, shards, smallest, top_value):
    def one(axis_at, parts):
        heights = jax.random.uniform(jax.random.fold_in(jax.random.fold_in(key, 6), axis_at), (parts,), jnp.float32, smallest / len(shards), top_value / len(shards))
        return jnp.repeat(jnp.exp(heights), dims[axis_at] // parts).reshape((-1,) + (1,) * (len(dims) - axis_at - 1))

    loudness = one(*shards[0])
    for cut in shards[1:]:
        loudness = loudness * one(*cut)
    return loudness


def gaussian(own_key, dims, width, reach, cuts=(), dtype=jnp.bfloat16):
    result = jax.random.normal(own_key, dims, jnp.float32) * width
    if len(cuts) > 0:
        result = block_levels(own_key, dims, cuts, -0.22, 0.18) * result
    return jnp.clip(result, min=-reach, max=reach).astype(dtype)


def setup_inputs(seed: int = 0, part: int = 0) -> dict:
    arg_keys = jax.random.split(jax.random.key(seed), 13)
    own_keys = jax.random.split(jax.random.fold_in(arg_keys[12], part), 13)
    return {
        "grid_state": gaussian(own_keys[0], (NX, NY, C), 1.0, 6.0, ((0, 4), (1, 4))),
        "boundary_rows": gaussian(own_keys[1], (BR, C), 1.0, 6.0, ((0, 16),)),
        "row_count": draw_row_count(jax.random.fold_in(jax.random.fold_in(arg_keys[12], part), 71), part),
        "target_x": draw_target_x(jax.random.fold_in(jax.random.fold_in(arg_keys[12], part), 71), part),
        "target_y": draw_target_y(jax.random.fold_in(jax.random.fold_in(arg_keys[12], part), 71), part),
        "g2m_mask": touch_ends((jax.random.randint(own_keys[5], (36, MESH_X, MESH_Y), 0, 3) < 2).astype(jnp.int32), jax.random.fold_in(own_keys[5], 1), 0, 1),
        "mesh_cotangent": gaussian(own_keys[6], (MESH_X, MESH_Y, C), 1.0, 6.0, ((0, 4), (1, 4))),
        "w_force": gaussian(arg_keys[7], (C, C), C ** -0.5, 0.375),
        "w_embed": gaussian(arg_keys[8], (C, C), C ** -0.5, 0.375),
        "w_message": gaussian(arg_keys[9], (C, C), C ** -0.5, 0.375),
        "w_level_one": gaussian(arg_keys[10], (C, C), C ** -0.5, 0.375),
        "w_level_two": gaussian(arg_keys[11], (C, C), C ** -0.5, 0.375),
    }


def silu_slope(argument):
    logistic = jax.nn.sigmoid(argument)
    return logistic * (1.0 + argument * (1.0 - logistic))

def gather_window(padded, window_mask):
    node_x = window_mask.shape[1]
    node_y = window_mask.shape[2]
    accumulated = jnp.zeros((node_x, node_y, padded.shape[2]), jnp.float32)
    for shift_x in range(6):
        for shift_y in range(6):
            window_piece = padded[shift_x:shift_x + 4 * node_x - 3:4, shift_y:shift_y + 4 * node_y - 3:4]
            scale = window_mask[shift_x * 6 + shift_y].astype(jnp.float32)
            accumulated = accumulated + scale[:, :, None] * window_piece.astype(jnp.float32)
    return accumulated / 6.0

def spread_window(node_bar, window_mask):
    node_x, node_y, channels = node_bar.shape
    table = window_mask.astype(jnp.float32).reshape(6, 6, node_x, node_y)
    table = jnp.pad(table, ((0, 2), (0, 2), (0, 0), (0, 0)))
    summed = jnp.zeros((4 * node_x + 4, 4 * node_y + 4, channels), jnp.float32)
    for offset_x in range(2):
        for offset_y in range(2):
            scales = table[4 * offset_x:4 * offset_x + 4, 4 * offset_y:4 * offset_y + 4].transpose(2, 0, 3, 1)
            placed = (scales[..., None] * node_bar[:, None, :, None, :]).reshape(4 * node_x, 4 * node_y, channels)
            summed = summed + jnp.pad(placed, ((4 * offset_x, 4 - 4 * offset_x), (4 * offset_y, 4 - 4 * offset_y), (0, 0)))
    return summed[:4 * node_x + 2, :4 * node_y + 2] / 6.0

def grid_forward(blended, w_embed, w_message):
    pre_embed = jnp.dot(blended, w_embed, preferred_element_type=jnp.float32)
    latent = (blended.astype(jnp.float32) + jax.nn.silu(pre_embed)).astype(jnp.bfloat16)
    pre_message = jnp.dot(latent, w_message, preferred_element_type=jnp.float32)
    message = jax.nn.silu(pre_message).astype(jnp.bfloat16)
    return (pre_embed, latent, pre_message, message)

def grid_backward(message_bar, blended, pre_embed, latent, pre_message, w_embed, w_message):
    pre_message_bar = (message_bar * silu_slope(pre_message)).astype(jnp.bfloat16)
    grad_message = jnp.dot(latent.T, pre_message_bar, preferred_element_type=jnp.float32)
    latent_bar = jnp.dot(pre_message_bar, w_message.T, preferred_element_type=jnp.float32)
    pre_embed_bar = (latent_bar * silu_slope(pre_embed)).astype(jnp.bfloat16)
    grad_embed = jnp.dot(blended.T, pre_embed_bar, preferred_element_type=jnp.float32)
    grad_state = (latent_bar + jnp.dot(pre_embed_bar, w_embed.T, preferred_element_type=jnp.float32)).astype(jnp.bfloat16)
    return (grad_state, grad_embed, grad_message)

def mesh_backward(level_one, cotangent, w_level_one, w_level_two):
    node_x, node_y, channels = level_one.shape
    flat_one = level_one.reshape(-1, channels)
    pre_one = jnp.dot(flat_one, w_level_one, preferred_element_type=jnp.float32)
    state_one = flat_one.astype(jnp.float32) + jax.nn.silu(pre_one)
    pooled = state_one.reshape(node_x // 2, 2, node_y // 2, 2, channels).mean(axis=(1, 3)).astype(jnp.bfloat16)
    flat_two = pooled.reshape(-1, channels)
    pre_two = jnp.dot(flat_two, w_level_two, preferred_element_type=jnp.float32)
    upstream = cotangent.astype(jnp.float32).reshape(node_x // 2, 2, node_y // 2, 2, channels)
    two_bar = upstream.sum(axis=(1, 3)).reshape(-1, channels)
    pre_two_bar = (two_bar * silu_slope(pre_two)).astype(jnp.bfloat16)
    grad_two = jnp.dot(flat_two.T, pre_two_bar, preferred_element_type=jnp.float32)
    pooled_bar = two_bar + jnp.dot(pre_two_bar, w_level_two.T, preferred_element_type=jnp.float32)
    one_bar = upstream + 0.25 * pooled_bar.reshape(node_x // 2, 1, node_y // 2, 1, channels)
    one_bar = one_bar.reshape(-1, channels)
    pre_one_bar = (one_bar * silu_slope(pre_one)).astype(jnp.bfloat16)
    grad_one = jnp.dot(flat_one.T, pre_one_bar, preferred_element_type=jnp.float32)
    level_bar = one_bar + jnp.dot(pre_one_bar, w_level_one.T, preferred_element_type=jnp.float32)
    return (level_bar.reshape(node_x, node_y, channels), grad_one, grad_two)

def reference(grid_state, boundary_rows, row_count, target_x, target_y, g2m_mask, mesh_cotangent, w_force, w_embed, w_message, w_level_one, w_level_two):
    live_rows = jnp.arange(BR) % BROWS < jnp.repeat(row_count, BROWS, total_repeat_length=BR)
    target_cell = jnp.where(live_rows, target_x * NY + target_y, NX * NY).astype(jnp.int32)
    projected = jnp.dot(boundary_rows, w_force, preferred_element_type=jnp.float32).astype(jnp.bfloat16)
    force = jnp.zeros((NX * NY, C), jnp.float32).at[target_cell].add(projected.astype(jnp.float32), mode='drop')
    blended = (grid_state.reshape(NX * NY, C).astype(jnp.float32) + force).astype(jnp.bfloat16)
    pre_embed, latent, pre_message, message = grid_forward(blended, w_embed, w_message)
    padded = jnp.pad(message.reshape(NX, NY, C), ((1, 1), (1, 1), (0, 0)))
    level_one = gather_window(padded, g2m_mask).astype(jnp.bfloat16)
    level_bar, grad_one, grad_two = mesh_backward(level_one, mesh_cotangent, w_level_one, w_level_two)
    spread = spread_window(level_bar, g2m_mask)
    message_bar = spread[1:NX + 1, 1:NY + 1].reshape(NX * NY, C)
    grad_state, grad_embed, grad_message = grid_backward(message_bar, blended, pre_embed, latent, pre_message, w_embed, w_message)
    projected_bar = jnp.take(grad_state, target_cell, axis=0, mode='fill', fill_value=0)
    grad_rows = jnp.dot(projected_bar, w_force.T, preferred_element_type=jnp.float32).astype(jnp.bfloat16)
    grad_force = jnp.dot(boundary_rows.T, projected_bar, preferred_element_type=jnp.float32)
    cell_total = NX * NY
    weight_grads = jnp.stack([grad_force / math.sqrt(BR), grad_embed / math.sqrt(cell_total), grad_message / math.sqrt(cell_total), grad_one / math.sqrt(cell_total // 16), grad_two / math.sqrt(cell_total // 64)])
    return (grad_state.reshape(NX, NY, C), grad_rows, weight_grads)
```

```python
import math

import jax
import jax.numpy as jnp
from jax import lax
from jax.sharding import PartitionSpec as P

CAP = 16


def padded_2(cells, sides, width):
    for axis, dim in sides:
        count = lax.axis_size(axis)
        ends = count - 1
        head = lax.slice_in_dim(cells, 0, width, axis=dim)
        tail = lax.slice_in_dim(cells, cells.shape[dim] - width, cells.shape[dim], axis=dim)
        cells = jnp.concatenate(
            [
                lax.ppermute(tail, axis, [(i, (i + 1) % count) for i in range(ends)]),
                cells,
                lax.ppermute(head, axis, [((i + 1) % count, i) for i in range(ends)]),
            ],
            axis=dim,
        )
    return cells


def swapped(block, axis, bit):
    count = lax.axis_size(axis)
    return lax.ppermute(block, axis, [(i, i ^ bit) for i in range(count)])


def shifted(block, axis, step):
    count = lax.axis_size(axis)
    return lax.ppermute(block, axis, [(i, (i + step) % count) for i in range(count)])


def summed_over_part(terms):
    wide_count = lax.axis_size("wide")
    narrow_count = lax.axis_size("narrow")
    wide_at = lax.axis_index("wide")
    narrow_at = lax.axis_index("narrow")
    bits = []
    while 1 << len(bits) < narrow_count:
        bits.append(1 << len(bits))
    piece = terms
    for bit in bits:
        half = piece.shape[0] // 2
        upper = (narrow_at // bit) % 2
        sent = lax.dynamic_slice_in_dim(piece, (1 - upper) * half, half).astype(jnp.bfloat16)
        kept = lax.dynamic_slice_in_dim(piece, upper * half, half)
        piece = kept + swapped(sent, "narrow", bit).astype(jnp.float32)
    part = piece.shape[0] // wide_count
    rounded = piece.astype(jnp.bfloat16)
    total = lax.dynamic_slice_in_dim(piece, wide_at * part, part)
    for step in range(1, wide_count):
        target = (wide_at + step) % wide_count
        sent = lax.dynamic_slice_in_dim(rounded, target * part, part)
        total = total + shifted(sent, "wide", step).astype(jnp.float32)
    own = total.astype(jnp.bfloat16)
    gathered = jnp.zeros((wide_count * part, own.shape[1]), jnp.bfloat16)
    gathered = lax.dynamic_update_slice_in_dim(gathered, own, wide_at * part, 0)
    for step in range(1, wide_count):
        source = (wide_at - step) % wide_count
        gathered = lax.dynamic_update_slice_in_dim(
            gathered, shifted(own, "wide", step), source * part, 0
        )
    for bit in reversed(bits):
        upper = (narrow_at // bit) % 2
        other = swapped(gathered, "narrow", bit)
        gathered = jnp.where(
            upper == 0,
            jnp.concatenate([gathered, other]),
            jnp.concatenate([other, gathered]),
        )
    return gathered


def silu_slope(argument):
    logistic = jax.nn.sigmoid(argument)
    return logistic * (1.0 + argument * (1.0 - logistic))


def gather_window(padded, window_mask):
    node_x = window_mask.shape[1]
    node_y = window_mask.shape[2]
    accumulated = jnp.zeros((node_x, node_y, padded.shape[2]), jnp.float32)
    for shift_x in range(6):
        for shift_y in range(6):
            window_piece = padded[
                shift_x : shift_x + 4 * node_x - 3 : 4, shift_y : shift_y + 4 * node_y - 3 : 4
            ]
            scale = window_mask[shift_x * 6 + shift_y].astype(jnp.float32)
            accumulated = accumulated + scale[:, :, None] * window_piece.astype(jnp.float32)
    return accumulated / 6.0


def spread_window(node_bar, window_mask):
    node_x, node_y, channels = node_bar.shape
    table = window_mask.astype(jnp.float32).reshape(6, 6, node_x, node_y)
    table = jnp.pad(table, ((0, 2), (0, 2), (0, 0), (0, 0)))
    summed = jnp.zeros((4 * node_x + 4, 4 * node_y + 4, channels), jnp.float32)
    for offset_x in range(2):
        for offset_y in range(2):
            scales = table[
                4 * offset_x : 4 * offset_x + 4, 4 * offset_y : 4 * offset_y + 4
            ].transpose(2, 0, 3, 1)
            placed = (scales[..., None] * node_bar[:, None, :, None, :]).reshape(
                4 * node_x, 4 * node_y, channels
            )
            summed = summed + jnp.pad(
                placed, ((4 * offset_x, 4 - 4 * offset_x), (4 * offset_y, 4 - 4 * offset_y), (0, 0))
            )
    return summed[: 4 * node_x + 2, : 4 * node_y + 2] / 6.0


def grid_forward(blended, w_embed, w_message):
    pre_embed = jnp.dot(blended, w_embed, preferred_element_type=jnp.float32)
    latent = (blended.astype(jnp.float32) + jax.nn.silu(pre_embed)).astype(jnp.bfloat16)
    pre_message = jnp.dot(latent, w_message, preferred_element_type=jnp.float32)
    message = jax.nn.silu(pre_message).astype(jnp.bfloat16)
    return (pre_embed, latent, pre_message, message)


def grid_backward(message_bar, blended, pre_embed, latent, pre_message, w_embed, w_message):
    pre_message_bar = (message_bar * silu_slope(pre_message)).astype(jnp.bfloat16)
    grad_message = jnp.dot(latent.T, pre_message_bar, preferred_element_type=jnp.float32)
    latent_bar = jnp.dot(pre_message_bar, w_message.T, preferred_element_type=jnp.float32)
    pre_embed_bar = (latent_bar * silu_slope(pre_embed)).astype(jnp.bfloat16)
    grad_embed = jnp.dot(blended.T, pre_embed_bar, preferred_element_type=jnp.float32)
    grad_state = (
        latent_bar + jnp.dot(pre_embed_bar, w_embed.T, preferred_element_type=jnp.float32)
    ).astype(jnp.bfloat16)
    return (grad_state, grad_embed, grad_message)


def mesh_backward(level_one, cotangent, w_level_one, w_level_two):
    node_x, node_y, channels = level_one.shape
    flat_one = level_one.reshape(-1, channels)
    pre_one = jnp.dot(flat_one, w_level_one, preferred_element_type=jnp.float32)
    state_one = flat_one.astype(jnp.float32) + jax.nn.silu(pre_one)
    pooled = (
        state_one.reshape(node_x // 2, 2, node_y // 2, 2, channels)
        .mean(axis=(1, 3))
        .astype(jnp.bfloat16)
    )
    flat_two = pooled.reshape(-1, channels)
    pre_two = jnp.dot(flat_two, w_level_two, preferred_element_type=jnp.float32)
    upstream = cotangent.astype(jnp.float32).reshape(node_x // 2, 2, node_y // 2, 2, channels)
    two_bar = upstream.sum(axis=(1, 3)).reshape(-1, channels)
    pre_two_bar = (two_bar * silu_slope(pre_two)).astype(jnp.bfloat16)
    grad_two = jnp.dot(flat_two.T, pre_two_bar, preferred_element_type=jnp.float32)
    pooled_bar = two_bar + jnp.dot(pre_two_bar, w_level_two.T, preferred_element_type=jnp.float32)
    one_bar = upstream + 0.25 * pooled_bar.reshape(node_x // 2, 1, node_y // 2, 1, channels)
    one_bar = one_bar.reshape(-1, channels)
    pre_one_bar = (one_bar * silu_slope(pre_one)).astype(jnp.bfloat16)
    grad_one = jnp.dot(flat_one.T, pre_one_bar, preferred_element_type=jnp.float32)
    level_bar = one_bar + jnp.dot(pre_one_bar, w_level_one.T, preferred_element_type=jnp.float32)
    return (level_bar.reshape(node_x, node_y, channels), grad_one, grad_two)


def local(
    grid_state,
    boundary_rows,
    row_count,
    target_x,
    target_y,
    g2m_mask,
    mesh_cotangent,
    w_force,
    w_embed,
    w_message,
    w_level_one,
    w_level_two,
):
    tile_x, tile_y, channels = grid_state.shape
    wide_count = lax.axis_size("wide")
    narrow_count = lax.axis_size("narrow")
    tile_cells = tile_x * tile_y
    slot_count = wide_count * CAP
    held_rows = boundary_rows.shape[0]
    live_rows = jnp.arange(held_rows) < row_count[0]
    destination = target_x // tile_x
    target_cell = target_x % tile_x * tile_y + target_y - lax.axis_index("narrow") * tile_y
    matches = (destination[:, None] == jnp.arange(wide_count)[None, :]) & live_rows[:, None]
    running = jnp.cumsum(matches.astype(jnp.int32), axis=0) - 1
    slot_index = jnp.sum(jnp.where(matches, running, 0), axis=1)
    send_slot = jnp.where(live_rows, destination * CAP + slot_index, slot_count)
    slot_cells = (
        jnp.full((slot_count,), tile_cells, jnp.int32).at[send_slot].set(target_cell, mode="drop")
    )
    outgoing = (
        jnp.zeros((slot_count, channels), jnp.bfloat16)
        .at[send_slot]
        .set(boundary_rows, mode="drop")
    )
    arrived, arrived_cells = (
        lax.all_to_all(
            outgoing.reshape(wide_count, CAP, channels),
            "wide",
            split_axis=0,
            concat_axis=0,
            tiled=True,
        ),
        lax.all_to_all(
            slot_cells.reshape(wide_count, CAP), "wide", split_axis=0, concat_axis=0, tiled=True
        ),
    )
    arrived = arrived.reshape(slot_count, channels)
    arrived_cells = arrived_cells.reshape(slot_count)
    projected = jnp.dot(arrived, w_force, preferred_element_type=jnp.float32).astype(jnp.bfloat16)
    force = (
        jnp.zeros((tile_cells, channels), jnp.float32)
        .at[arrived_cells]
        .add(projected.astype(jnp.float32), mode="drop")
    )
    blended = (grid_state.reshape(tile_cells, channels).astype(jnp.float32) + force).astype(
        jnp.bfloat16
    )
    pre_embed, latent, pre_message, message = grid_forward(blended, w_embed, w_message)
    padded = padded_2(message.reshape(tile_x, tile_y, channels), (("wide", 0), ("narrow", 1)), 1)
    level_one = gather_window(padded, g2m_mask).astype(jnp.bfloat16)
    level_bar, grad_one, grad_two = mesh_backward(
        level_one, mesh_cotangent, w_level_one, w_level_two
    )
    spread = spread_window(level_bar, g2m_mask)
    received = padded_2(spread, (("wide", 0), ("narrow", 1)), 1)
    interior = spread[1:-1, 1:-1]
    interior = interior.at[0].add(received[0, 2:-2])
    interior = interior.at[-1].add(received[-1, 2:-2])
    interior = interior.at[:, 0].add(received[2:-2, 0])
    interior = interior.at[:, -1].add(received[2:-2, -1])
    interior = interior.at[0, 0].add(received[0, 0])
    interior = interior.at[0, -1].add(received[0, -1])
    interior = interior.at[-1, 0].add(received[-1, 0])
    interior = interior.at[-1, -1].add(received[-1, -1])
    grad_state, grad_embed, grad_message = grid_backward(
        interior.reshape(tile_cells, channels),
        blended,
        pre_embed,
        latent,
        pre_message,
        w_embed,
        w_message,
    )
    slot_bar = jnp.take(grad_state, arrived_cells, axis=0, mode="fill", fill_value=0)
    back_payload = jnp.dot(slot_bar, w_force.T, preferred_element_type=jnp.float32).astype(
        jnp.bfloat16
    )
    grad_force = jnp.dot(arrived.T, slot_bar, preferred_element_type=jnp.float32)
    returned = lax.all_to_all(
        back_payload.reshape(wide_count, CAP, channels),
        "wide",
        split_axis=0,
        concat_axis=0,
        tiled=True,
    )
    row_back = jnp.take(
        returned.reshape(slot_count, channels), send_slot, axis=0, mode="fill", fill_value=0
    )
    totals = summed_over_part(
        jnp.concatenate([grad_force, grad_embed, grad_message, grad_one, grad_two], axis=0)
    )
    cell_total = tile_cells * wide_count * narrow_count
    row_total = held_rows * wide_count * narrow_count
    scales = jnp.array(
        [
            1.0 / math.sqrt(row_total),
            1.0 / math.sqrt(cell_total),
            1.0 / math.sqrt(cell_total),
            1.0 / math.sqrt(cell_total // 16),
            1.0 / math.sqrt(cell_total // 64),
        ],
        jnp.float32,
    )
    weight_grads = totals.reshape(5, channels, channels).astype(jnp.float32) * scales[:, None, None]
    return (grad_state.reshape(tile_x, tile_y, channels), row_back, weight_grads)


def solution(mesh):
    in_specs = (
        P(("groups", "wide"), "narrow", None),
        P(("groups", "wide", "narrow"), None),
        P(("groups", "wide", "narrow")),
        P(("groups", "wide", "narrow")),
        P(("groups", "wide", "narrow")),
        P(None, ("groups", "wide"), "narrow"),
        P(("groups", "wide"), "narrow", None),
        P(),
        P(),
        P(),
        P(),
        P(),
    )
    out_specs = (
        P(("groups", "wide"), "narrow", None),
        P(("groups", "wide", "narrow"), None),
        P("groups", None, None),
    )
    return jax.shard_map(local, mesh=mesh, in_specs=in_specs, out_specs=out_specs, check_vma=False)
```

```python
import functools
import math

import jax
import jax.numpy as jnp
import numpy as np
from jax import lax
from jax.experimental import pallas as pl
from jax.experimental.pallas import tpu as pltpu
from jax.sharding import PartitionSpec as P

CAP = 16
REACH = 9
NODES_OUT = 2
SIDE = 16
SLOTS = 16
LANES = 256
VMEM_LIMIT = 48 * 1024 * 1024
F32 = jnp.float32
BF16 = jnp.bfloat16


def swapped(block, axis, bit):
    count = lax.axis_size(axis)
    return lax.ppermute(block, axis, [(i, i ^ bit) for i in range(count)])


def shifted(block, axis, step):
    count = lax.axis_size(axis)
    return lax.ppermute(block, axis, [(i, (i + step) % count) for i in range(count)])


def dot(left, right):
    return jnp.dot(left, right, preferred_element_type=F32)


def dot_right_t(left, right):
    return lax.dot_general(left, right, (((1,), (1,)), ((), ())), preferred_element_type=F32)


def dot_left_t(left, right):
    return lax.dot_general(left, right, (((0,), (0,)), ((), ())), preferred_element_type=F32)


def sigmoid(value):
    return 0.5 * jnp.tanh(0.5 * value) + 0.5


def silu_and_slope(value):
    logistic = sigmoid(value)
    return value * logistic, logistic * (1.0 + value * (1.0 - logistic))


def silu(value):
    return value * sigmoid(value)


def pieces(start, stop, size):
    return [(at, min(size, stop - at)) for at in range(start, stop, size)]


def two_halves(value):
    high = value.astype(BF16)
    low = (value - high.astype(F32)).astype(BF16)
    return jnp.concatenate([high, low], axis=0)


class Shape:
    def __init__(self, tile_x, tile_y):
        self.tile_x = tile_x
        self.tile_y = tile_y
        self.cells = tile_x * tile_y
        self.rows_x = tile_x + 2 * REACH
        self.halo = REACH * tile_y
        self.center = self.rows_x * tile_y
        self.side = self.rows_x * SIDE
        self.pitch = tile_y + 2 * SIDE
        self.node_x = tile_x // 4
        self.node_y = tile_y // 4
        self.out_x = self.node_x + 2 * NODES_OUT
        self.nodes = self.out_x * SLOTS
        self.edge = NODES_OUT * self.node_y
        self.own_nodes = self.node_x * self.node_y
        self.window = 6 * self.pitch
        self.side_nodes = NODES_OUT * self.out_x

    def center_row(self, at_x, at_y, kind):
        edge, own = self.edge, self.own_nodes
        if at_x < NODES_OUT:
            return kind * edge + at_x * self.node_y + at_y
        at_x -= NODES_OUT
        if at_x < self.node_x:
            return 2 * edge + kind * own + at_x * self.node_y + at_y
        at_x -= self.node_x
        return 2 * edge + 2 * own + kind * edge + at_x * self.node_y + at_y

    def tables(self):
        stack = 4 * self.edge + 2 * self.own_nodes
        side = self.side_nodes
        to_left = np.zeros((2 * side, stack), np.float32)
        to_right = np.zeros((2 * side, stack), np.float32)
        for kind in range(2):
            for at_x in range(self.out_x):
                for k in range(NODES_OUT):
                    row = kind * side + at_x * NODES_OUT + k
                    to_left[row, self.center_row(at_x, k, kind)] = 1
                    last = self.node_y - NODES_OUT + k
                    to_right[row, self.center_row(at_x, last, kind)] = 1
        place = np.zeros((2, self.nodes, stack + 4 * side), np.float32)
        for kind in range(2):
            for at_x in range(self.out_x):
                for slot in range(self.node_y + 2 * NODES_OUT):
                    at_y = slot - NODES_OUT
                    if at_y < 0:
                        column = stack + kind * side + at_x * NODES_OUT + slot
                    elif at_y < self.node_y:
                        column = self.center_row(at_x, at_y, kind)
                    else:
                        k = at_y - self.node_y
                        column = stack + 2 * side + kind * side + at_x * NODES_OUT + k
                    place[kind, at_x * SLOTS + slot, column] = 1
        spread = np.zeros((2, 128, self.window), np.float32)
        match = np.zeros((2, SLOTS, self.window), np.float32)
        for dx in range(6):
            for at in range(self.pitch):
                if at < self.tile_y:
                    y = at
                elif at < self.tile_y + SIDE:
                    y = at - self.tile_y - SIDE
                else:
                    y = at - SIDE
                quotient, rest = (y + REACH) // 4, (y + REACH) % 4
                lane = dx * self.pitch + at
                spread[0, dx * 6 + rest, lane] = 1
                if 0 <= quotient < SLOTS:
                    match[0, quotient, lane] = 1
                if rest < 2:
                    spread[1, dx * 6 + rest + 4, lane] = 1
                    if 0 <= quotient - 1 < SLOTS:
                        match[1, quotient - 1, lane] = 1
        node = np.arange(self.nodes)
        quad = node // SLOTS // 2 * SLOTS + node % SLOTS // 2
        same = (quad[:, None] == quad[None, :]).astype(np.float32)
        return {
            "to_left": to_left,
            "to_right": to_right,
            "place": place,
            "spread": spread,
            "match": match,
            "quad": np.concatenate([same, same], axis=1),
        }


def blend_kernel(shape, wide_count, units, unit_rows, *refs):
    (wide_ref, own_ref, mesh_ref, w_force_ref, left_ref, right_ref, own_rows_ref) = refs[:7]
    count = len(units) - 1
    arrived = refs[7 : 7 + count]
    (blended_ref, to_left_ref, to_right_ref, stack_ref, rows_ref, key_ref) = refs[7 + count : 13 + count]
    (projected_ref,) = refs[13 + count :]
    from_prev, from_next = arrived[0], arrived[-1]
    wide_at = wide_ref[0]
    held = [own_rows_ref] + list(arrived)
    total = unit_rows * len(units)
    for k, start in enumerate(units):
        rows_ref[k * unit_rows : (k + 1) * unit_rows] = held[k][start : start + unit_rows]
    blocks = []
    if total <= LANES:
        metas = [
            held[k][start + unit_rows : start + unit_rows + 16].astype(F32)
            for k, start in enumerate(units)
        ]
        blocks.append(functools.reduce(lambda a, b: a + b, metas)[:, :total])
    else:
        for k, start in enumerate(units):
            for part in range(unit_rows // LANES):
                at = start + unit_rows + 16 * part
                blocks.append(held[k][at : at + 16].astype(F32))
    keys = []
    for block in blocks:
        whole = block.astype(jnp.int32)
        at_x = whole[0:1] * shape.tile_x + whole[1:2] - wide_at * shape.tile_x + REACH
        at_y = whole[2:3]
        inside = (at_x >= 0) & (at_x < shape.rows_x) & (at_y < shape.tile_y)
        keys.append(jnp.where(inside, at_x * shape.tile_y + at_y, -1))
    width = keys[0].shape[1]
    for k, key in enumerate(keys):
        key_ref[:, k * width : (k + 1) * width] = jnp.broadcast_to(key, (8, width))
    projected_ref[...] = dot(rows_ref[...], w_force_ref[...]).astype(BF16)

    mesh = 2 * shape.edge
    keep_prev = (wide_at > 0).astype(F32)
    keep_next = (wide_at < wide_count - 1).astype(F32)
    prev_mesh = from_prev[shape.halo : shape.halo + mesh].astype(F32) * keep_prev
    next_mesh = from_next[shape.halo : shape.halo + mesh].astype(F32) * keep_next
    stack = jnp.concatenate(
        [prev_mesh.astype(BF16), mesh_ref[...], next_mesh.astype(BF16)], axis=0
    )
    stack_ref[...] = stack
    to_left_ref[shape.side :] = dot(left_ref[...], stack).astype(BF16)
    to_right_ref[shape.side :] = dot(right_ref[...], stack).astype(BF16)

    tile_y = shape.tile_y
    inner = shape.halo + shape.cells
    jobs = [(from_prev, at, n, 0, keep_prev) for at, n in pieces(0, shape.halo, 3 * tile_y)]
    jobs += [(own_ref, at, n, shape.halo, None) for at, n in pieces(0, shape.cells, 4 * tile_y)]
    jobs += [(from_next, at, n, inner, keep_next) for at, n in pieces(0, shape.halo, 3 * tile_y)]
    for ref, at, n, base, keep in jobs:
        first = base + at
        value = ref[at : at + n].astype(F32)
        if keep is not None:
            value = value * keep
        cell = lax.broadcasted_iota(jnp.int32, (n, width), 0) + first
        for k, key in enumerate(keys):
            hit = jnp.where(cell == key, 1.0, 0.0).astype(BF16)
            value = value + dot(hit, projected_ref[k * width : (k + 1) * width])
        value = value.astype(BF16)
        blended_ref[first : first + n] = value
        for t in range(n // tile_y):
            row = first // tile_y + t
            to_left_ref[row * SIDE : (row + 1) * SIDE] = value[t * tile_y : t * tile_y + SIDE]
            to_right_ref[row * SIDE : (row + 1) * SIDE] = value[
                (t + 1) * tile_y - SIDE : (t + 1) * tile_y
            ]


def forward_kernel(
    shape, blended_ref, w_embed_ref, w_message_ref, message_ref, latent_ref, embed_ref, slope_ref
):
    inner = shape.halo + shape.cells
    jobs = pieces(0, shape.halo, 96) + pieces(shape.halo, inner, 128)
    jobs += pieces(inner, shape.center, 96)
    for at, n in jobs:
        blended = blended_ref[at : at + n]
        pre_embed = dot(blended, w_embed_ref[...])
        value, slope = silu_and_slope(pre_embed)
        latent = (blended.astype(F32) + value).astype(BF16)
        pre_message = dot(latent, w_message_ref[...])
        message, message_slope = silu_and_slope(pre_message)
        message_ref[at : at + n] = message.astype(BF16)
        if shape.halo <= at < inner:
            own = at - shape.halo
            latent_ref[own : own + n] = latent
            embed_ref[own : own + n] = slope
            slope_ref[own : own + n] = message_slope


def backward_kernel(shape, total_rows, *refs):
    (
        narrow_ref,
        from_left_ref,
        from_right_ref,
        stack_ref,
        blended_ref,
        message_ref,
        latent_ref,
        embed_ref,
        slope_ref,
        rows_ref,
        key_ref,
        place_ref,
        spread_ref,
        match_ref,
        quad_ref,
        w_force_ref,
        w_embed_ref,
        w_message_ref,
        w_one_ref,
        w_two_ref,
        state_ref,
        back_ref,
        sent_ref,
        kept_ref,
        padded_ref,
        level_ref,
        cover_ref,
        pmb_ref,
        peb_ref,
        grads_ref,
    ) = refs
    tile_y, pitch = shape.tile_y, shape.pitch
    channels = blended_ref.shape[1]

    for ref, offset in ((from_left_ref, tile_y), (from_right_ref, tile_y + SIDE)):
        for at, n in pieces(0, shape.side, 8 * SIDE):
            blended = ref[at : at + n]
            latent = (blended.astype(F32) + silu(dot(blended, w_embed_ref[...]))).astype(BF16)
            message = silu(dot(latent, w_message_ref[...])).astype(BF16)
            for t in range(n // SIDE):
                row = (at // SIDE + t) * pitch + offset
                padded_ref[row : row + SIDE] = message[t * SIDE : (t + 1) * SIDE]
    for row in range(shape.rows_x):
        padded_ref[row * pitch : row * pitch + tile_y] = message_ref[
            row * tile_y : (row + 1) * tile_y
        ]

    stack = jnp.concatenate(
        [stack_ref[...], from_left_ref[shape.side :], from_right_ref[shape.side :]], axis=0
    )
    cotangent = dot(place_ref[0], stack)
    mask = dot(place_ref[1], stack[:, :128]).astype(BF16)
    near = dot(mask, spread_ref[0])
    far = dot(mask, spread_ref[1])
    windows = []
    for at_x in range(shape.out_x):
        rows = slice(at_x * SLOTS, (at_x + 1) * SLOTS)
        windows.append(near[rows] * match_ref[0] + far[rows] * match_ref[1])
        level_ref[rows] = (
            dot(
                windows[-1].astype(BF16),
                padded_ref[4 * at_x * pitch : 4 * at_x * pitch + shape.window],
            )
            / 6.0
        ).astype(BF16)
    turned = jnp.concatenate(windows, axis=0).T
    node_x = lax.broadcasted_iota(jnp.int32, (tile_y, shape.nodes), 1) // SLOTS
    for at_x in range(shape.tile_x):
        quotient, rest = (at_x + REACH) // 4, (at_x + REACH) % 4
        cover = jnp.where(node_x == quotient, turned[rest * pitch : rest * pitch + tile_y], 0.0)
        if rest < 2:
            again = (rest + 4) * pitch
            cover = cover + jnp.where(
                node_x == quotient - 1, turned[again : again + tile_y], 0.0
            )
        cover = cover.astype(BF16)
        cover_ref[at_x * tile_y : (at_x + 1) * tile_y] = jnp.concatenate([cover, cover], axis=1)

    level_one = level_ref[...]
    pre_one = dot(level_one, w_one_ref[...])
    value, slope_one = silu_and_slope(pre_one)
    state_one = level_one.astype(F32) + value
    level_two = (0.25 * dot(quad_ref[...], two_halves(state_one))).astype(BF16)
    pre_two = dot(level_two, w_two_ref[...])
    two_bar = dot(quad_ref[:, : shape.nodes], cotangent.astype(BF16))
    pre_two_bar = (two_bar * silu_and_slope(pre_two)[1]).astype(BF16)
    pooled_bar = two_bar + dot_right_t(pre_two_bar, w_two_ref[...])
    one_bar = cotangent + 0.25 * pooled_bar
    pre_one_bar = (one_bar * slope_one).astype(BF16)
    level_bar = one_bar + dot_right_t(pre_one_bar, w_one_ref[...])

    node = lax.broadcasted_iota(jnp.int32, (shape.nodes, channels), 0)
    at_x, at_y = node // SLOTS, node % SLOTS
    owned = (at_x >= NODES_OUT) & (at_x < NODES_OUT + shape.node_x)
    owned = owned & (at_y >= NODES_OUT) & (at_y < NODES_OUT + shape.node_y)
    first = owned & (at_x % 2 == 0) & (at_y % 2 == 0)
    grads_ref[3 * channels : 4 * channels] = dot_left_t(
        level_one, jnp.where(owned, pre_one_bar.astype(F32), 0.0).astype(BF16)
    )
    grads_ref[4 * channels :] = dot_left_t(
        level_two, jnp.where(first, pre_two_bar.astype(F32), 0.0).astype(BF16)
    )

    both = two_halves(level_bar)
    for at, n in pieces(0, shape.cells, 128):
        rows = slice(at, at + n)
        message_bar = dot(cover_ref[rows], both) / 6.0
        pre_message_bar = (message_bar * slope_ref[rows]).astype(BF16)
        pmb_ref[rows] = pre_message_bar
        latent_bar = dot_right_t(pre_message_bar, w_message_ref[...])
        pre_embed_bar = (latent_bar * embed_ref[rows]).astype(BF16)
        peb_ref[rows] = pre_embed_bar
        state_ref[rows] = (latent_bar + dot_right_t(pre_embed_bar, w_embed_ref[...])).astype(BF16)
    own = slice(shape.halo, shape.halo + shape.cells)
    grads_ref[channels : 2 * channels] = dot_left_t(blended_ref[own], peb_ref[...])
    grads_ref[2 * channels : 3 * channels] = dot_left_t(latent_ref[...], pmb_ref[...])

    width = min(total_rows, LANES)
    cell = lax.broadcasted_iota(jnp.int32, (shape.cells, width), 0) + shape.halo
    grad_force = None
    for at in range(0, total_rows, width):
        rows = slice(at, at + width)
        hit = jnp.where(cell == key_ref[0:1, rows], 1.0, 0.0).astype(BF16)
        slot_bar = dot_left_t(hit, state_ref[...]).astype(BF16)
        back_ref[rows] = dot_right_t(slot_bar, w_force_ref[...]).astype(BF16)
        term = dot_left_t(rows_ref[rows], slot_bar)
        grad_force = term if grad_force is None else grad_force + term
    grads_ref[:channels] = grad_force

    half = sent_ref.shape[0]
    upper = narrow_ref[0] % 2
    kept_at = pl.multiple_of(upper * half, half)
    sent_at = pl.multiple_of((1 - upper) * half, half)
    sent_ref[...] = grads_ref[pl.ds(sent_at, half)].astype(BF16)
    kept_ref[...] = grads_ref[pl.ds(kept_at, half)]


def call(kernel, out_shapes, operands, scratch=(), scalars=1, flops=0):
    specs = [pl.BlockSpec(memory_space=pltpu.SMEM)] * scalars
    specs += [pl.BlockSpec(memory_space=pltpu.VMEM)] * (len(operands) - scalars)
    moved = sum(math.prod(o.shape) * o.dtype.itemsize for o in list(operands) + list(out_shapes))
    return pl.pallas_call(
        kernel,
        out_shape=tuple(out_shapes),
        in_specs=specs,
        out_specs=tuple(pl.BlockSpec(memory_space=pltpu.VMEM) for _ in out_shapes),
        scratch_shapes=list(scratch),
        compiler_params=pltpu.CompilerParams(vmem_limit_bytes=VMEM_LIMIT),
        cost_estimate=pl.CostEstimate(flops=flops, bytes_accessed=moved, transcendentals=0),
    )(*operands)


def meta_rows(live, target_x, target_y, tile_x, unit_rows, slot, units):
    high = target_x // tile_x
    low = target_x % tile_x
    column = jnp.where(live, target_y, LANES - 1)
    fields = jnp.stack([high, low, column]).astype(F32)
    if unit_rows * units <= LANES:
        before = slot * unit_rows
        after = LANES - before - unit_rows
        return jnp.pad(fields, ((0, 13), (before, after))).astype(BF16)
    blocks = unit_rows // LANES
    fields = fields.reshape(3, blocks, LANES).transpose(1, 0, 2)
    return jnp.pad(fields, ((0, 0), (0, 13), (0, 0))).reshape(16 * blocks, LANES).astype(BF16)


def local(
    grid_state,
    boundary_rows,
    row_count,
    target_x,
    target_y,
    g2m_mask,
    mesh_cotangent,
    w_force,
    w_embed,
    w_message,
    w_level_one,
    w_level_two,
):
    tile_x, tile_y, channels = grid_state.shape
    wide_count = lax.axis_size("wide")
    narrow_count = lax.axis_size("narrow")
    wide_at = lax.axis_index("wide")
    narrow_at = lax.axis_index("narrow")
    held_rows = boundary_rows.shape[0]
    shape = Shape(tile_x, tile_y)
    table = {name: jnp.asarray(value, BF16) for name, value in shape.tables().items()}
    table["match"] = table["match"].astype(F32)

    live = jnp.arange(held_rows) < row_count[0]
    column = target_y - narrow_at * tile_y
    whole_column = held_rows * wide_count <= LANES
    if whole_column:
        units = wide_count
        unit_rows = held_rows
        rows, row_live, row_x, row_y = boundary_rows, live, target_x, column
    else:
        slot_count = wide_count * CAP
        destination = target_x // tile_x
        matches = (destination[:, None] == jnp.arange(wide_count)[None, :]) & live[:, None]
        running = jnp.cumsum(matches.astype(jnp.int32), axis=0) - 1
        slot_index = jnp.sum(jnp.where(matches, running, 0), axis=1)
        send_slot = jnp.where(live, destination * CAP + slot_index, slot_count)
        cells = jnp.full((slot_count,), -1, jnp.int32)
        cells = cells.at[send_slot].set(target_x % tile_x * tile_y + column, mode="drop")
        outgoing = jnp.zeros((slot_count, channels), BF16)
        outgoing = outgoing.at[send_slot].set(boundary_rows, mode="drop")
        outgoing = outgoing.reshape(wide_count, CAP, channels)
        rows = lax.all_to_all(outgoing, "wide", split_axis=0, concat_axis=0, tiled=True)
        cells = lax.all_to_all(
            cells.reshape(wide_count, CAP), "wide", split_axis=0, concat_axis=0, tiled=True
        )
        rows = rows.reshape(slot_count, channels)
        cells = cells.reshape(slot_count)
        units = 3
        unit_rows = slot_count
        row_live = cells >= 0
        row_x = jnp.where(row_live, wide_at * tile_x + cells // tile_y, 0)
        row_y = cells % tile_y

    def with_meta(slot):
        return [rows, meta_rows(row_live, row_x, row_y, tile_x, unit_rows, slot, units)]

    cells = grid_state.reshape(-1, channels)
    mask = g2m_mask.astype(BF16).transpose(1, 2, 0)
    mask = jnp.pad(mask, ((0, 0), (0, 0), (0, channels - 36)))
    edge = slice(0, NODES_OUT), slice(shape.node_x - NODES_OUT, shape.node_x)
    flat = [
        [mesh_cotangent[part].reshape(-1, channels), mask[part].reshape(-1, channels)]
        for part in edge
    ]
    mesh = jnp.concatenate([mesh_cotangent.reshape(-1, channels), mask.reshape(-1, channels)])
    to_prev = jnp.concatenate([cells[: shape.halo]] + flat[0] + with_meta(units - 1))
    to_next = jnp.concatenate([cells[-shape.halo :]] + flat[1] + with_meta(1))
    own_rows = jnp.concatenate(with_meta(0))
    arrived = [shifted(to_next, "wide", 1)]
    starts = [0, shape.halo + 2 * shape.edge]
    for step in range(2, units - 1):
        arrived.append(shifted(jnp.concatenate(with_meta(step)), "wide", step))
        starts.append(0)
    arrived.append(shifted(to_prev, "wide", -1))
    starts.append(shape.halo + 2 * shape.edge)

    total_rows = unit_rows * units
    stack_rows = 4 * shape.edge + 2 * shape.own_nodes
    struct = jax.ShapeDtypeStruct
    payload = struct((shape.side + 2 * shape.side_nodes, channels), BF16)
    blended, to_left, to_right, stack, all_rows, keys = call(
        functools.partial(blend_kernel, shape, wide_count, starts, unit_rows),
        [
            struct((shape.center, channels), BF16),
            payload,
            payload,
            struct((stack_rows, channels), BF16),
            struct((total_rows, channels), BF16),
            struct((8, total_rows), jnp.int32),
        ],
        [wide_at.reshape(1), cells, mesh, w_force, table["to_left"], table["to_right"], own_rows]
        + arrived,
        scratch=[pltpu.VMEM((total_rows, channels), BF16)],
        flops=2 * shape.center * total_rows * channels,
    )
    ends = narrow_count - 1
    from_left = lax.ppermute(to_right, "narrow", [(i, i + 1) for i in range(ends)])
    from_right = lax.ppermute(to_left, "narrow", [(i + 1, i) for i in range(ends)])
    message, latent, embed_slope, message_slope = call(
        functools.partial(forward_kernel, shape),
        [
            struct((shape.center, channels), BF16),
            struct((shape.cells, channels), BF16),
            struct((shape.cells, channels), F32),
            struct((shape.cells, channels), F32),
        ],
        [blended, w_embed, w_message],
        scalars=0,
        flops=4 * shape.center * channels * channels,
    )
    grad_rows_total = 5 * channels
    grad_state, back, sent, kept = call(
        functools.partial(backward_kernel, shape, total_rows),
        [
            struct((shape.cells, channels), BF16),
            struct((total_rows, channels), BF16),
            struct((grad_rows_total // 2, channels), BF16),
            struct((grad_rows_total // 2, channels), F32),
        ],
        [
            narrow_at.reshape(1),
            from_left,
            from_right,
            stack,
            blended,
            message,
            latent,
            embed_slope,
            message_slope,
            all_rows,
            keys,
            table["place"],
            table["spread"],
            table["match"],
            table["quad"],
            w_force,
            w_embed,
            w_message,
            w_level_one,
            w_level_two,
        ],
        scratch=[
            pltpu.VMEM((shape.rows_x * shape.pitch, channels), BF16),
            pltpu.VMEM((shape.nodes, channels), BF16),
            pltpu.VMEM((shape.cells, 2 * shape.nodes), BF16),
            pltpu.VMEM((shape.cells, channels), BF16),
            pltpu.VMEM((shape.cells, channels), BF16),
            pltpu.VMEM((grad_rows_total, channels), F32),
        ],
        flops=12 * shape.cells * channels * channels,
    )

    bits = [1 << k for k in range(narrow_count.bit_length() - 1)]
    piece = kept + swapped(sent, "narrow", bits[0]).astype(F32)
    for bit in bits[1:]:
        half = piece.shape[0] // 2
        upper = (narrow_at // bit) % 2
        sent = lax.dynamic_slice_in_dim(piece, (1 - upper) * half, half).astype(BF16)
        kept = lax.dynamic_slice_in_dim(piece, upper * half, half)
        piece = kept + swapped(sent, "narrow", bit).astype(F32)
    part = piece.shape[0] // wide_count
    rounded = piece.astype(BF16)
    total = lax.dynamic_slice_in_dim(piece, wide_at * part, part)
    row_back = back[:unit_rows].astype(F32)
    for step in range(1, wide_count):
        target = (wide_at + step) % wide_count
        sent = lax.dynamic_slice_in_dim(rounded, target * part, part)
        if whole_column:
            source = wide_count - step
            rows_back = back[source * unit_rows : (source + 1) * unit_rows]
            got = shifted(jnp.concatenate([sent, rows_back]), "wide", step).astype(F32)
            row_back = row_back + got[part:]
            total = total + got[:part]
        else:
            total = total + shifted(sent, "wide", step).astype(F32)
    if whole_column:
        row_back = row_back.astype(BF16)
    else:
        returned = lax.all_to_all(
            back[:unit_rows].reshape(wide_count, CAP, channels),
            "wide",
            split_axis=0,
            concat_axis=0,
            tiled=True,
        )
        row_back = jnp.take(
            returned.reshape(-1, channels), send_slot, axis=0, mode="fill", fill_value=0
        )
    own = total.astype(BF16)
    gathered = jnp.zeros((wide_count * part, channels), BF16)
    gathered = lax.dynamic_update_slice_in_dim(gathered, own, wide_at * part, 0)
    for step in range(1, wide_count):
        source = (wide_at - step) % wide_count
        gathered = lax.dynamic_update_slice_in_dim(
            gathered, shifted(own, "wide", step), source * part, 0
        )
    for bit in reversed(bits):
        upper = (narrow_at // bit) % 2
        other = swapped(gathered, "narrow", bit)
        gathered = jnp.where(
            upper == 0,
            jnp.concatenate([gathered, other]),
            jnp.concatenate([other, gathered]),
        )
    cell_total = shape.cells * wide_count * narrow_count
    row_total = held_rows * wide_count * narrow_count
    scales = np.array(
        [
            1.0 / math.sqrt(row_total),
            1.0 / math.sqrt(cell_total),
            1.0 / math.sqrt(cell_total),
            1.0 / math.sqrt(cell_total // 16),
            1.0 / math.sqrt(cell_total // 64),
        ],
        np.float32,
    )
    weight_grads = gathered.reshape(5, channels, channels).astype(F32) * scales[:, None, None]
    return (grad_state.reshape(tile_x, tile_y, channels), row_back, weight_grads)


def solution(mesh):
    in_specs = (
        P(("groups", "wide"), "narrow", None),
        P(("groups", "wide", "narrow"), None),
        P(("groups", "wide", "narrow")),
        P(("groups", "wide", "narrow")),
        P(("groups", "wide", "narrow")),
        P(None, ("groups", "wide"), "narrow"),
        P(("groups", "wide"), "narrow", None),
        P(),
        P(),
        P(),
        P(),
        P(),
    )
    out_specs = (
        P(("groups", "wide"), "narrow", None),
        P(("groups", "wide", "narrow"), None),
        P("groups", None, None),
    )
    return jax.shard_map(local, mesh=mesh, in_specs=in_specs, out_specs=out_specs, check_vma=False)
```

```python
import functools
import math

import jax
import jax.numpy as jnp
import numpy as np
from jax import lax
from jax.experimental import pallas as pl
from jax.experimental.pallas import tpu as pltpu
from jax.sharding import PartitionSpec as P

CAP = 16
REACH = 9
NODES_OUT = 2
SIDE = 16
SLOTS = 16
LANES = 256
VMEM_LIMIT = 48 * 1024 * 1024
F32 = jnp.float32
BF16 = jnp.bfloat16


def swapped(block, axis, bits):
    count = lax.axis_size(axis)
    return lax.ppermute(block, axis, [(i, i ^ bits) for i in range(count)])


def swapped_between(block, axis):
    count = lax.axis_size(axis)
    pairs = [(i, i + 1) for i in range(1, count - 1, 2)]
    return lax.ppermute(block, axis, pairs + [(j, i) for i, j in pairs])


def swapped_both(block, wide_bits, narrow_bits):
    wide_count = lax.axis_size("wide")
    narrow_count = lax.axis_size("narrow")
    pairs = [
        (w * narrow_count + n, (w ^ wide_bits) * narrow_count + (n ^ narrow_bits))
        for w in range(wide_count)
        for n in range(narrow_count)
    ]
    return lax.ppermute(block, ("wide", "narrow"), pairs)


def dot(left, right):
    return jnp.dot(left, right, preferred_element_type=F32)


def dot_right_t(left, right):
    return lax.dot_general(left, right, (((1,), (1,)), ((), ())), preferred_element_type=F32)


def dot_left_t(left, right):
    return lax.dot_general(left, right, (((0,), (0,)), ((), ())), preferred_element_type=F32)


def sigmoid(value):
    return 0.5 * jnp.tanh(0.5 * value) + 0.5


def silu_and_slope(value):
    logistic = sigmoid(value)
    return value * logistic, logistic * (1.0 + value * (1.0 - logistic))


def silu(value):
    return value * sigmoid(value)


def pieces(start, stop, size):
    return [(at, min(size, stop - at)) for at in range(start, stop, size)]


def two_halves(value):
    high = value.astype(BF16)
    low = (value - high.astype(F32)).astype(BF16)
    return jnp.concatenate([high, low], axis=0)


class Shape:
    def __init__(self, tile_x, tile_y):
        self.tile_x = tile_x
        self.tile_y = tile_y
        self.cells = tile_x * tile_y
        self.rows_x = tile_x + 2 * REACH
        self.halo = REACH * tile_y
        self.center = self.rows_x * tile_y
        self.side = self.rows_x * SIDE
        self.pitch = tile_y + 2 * SIDE
        self.node_x = tile_x // 4
        self.node_y = tile_y // 4
        self.out_x = self.node_x + 2 * NODES_OUT
        self.nodes = self.out_x * SLOTS
        self.edge = NODES_OUT * self.node_y
        self.own_nodes = self.node_x * self.node_y
        self.window = 6 * self.pitch
        self.side_nodes = NODES_OUT * self.out_x

    def center_row(self, at_x, at_y, kind):
        edge, own = self.edge, self.own_nodes
        if at_x < NODES_OUT:
            return kind * edge + at_x * self.node_y + at_y
        at_x -= NODES_OUT
        if at_x < self.node_x:
            return 2 * edge + kind * own + at_x * self.node_y + at_y
        at_x -= self.node_x
        return 2 * edge + 2 * own + kind * edge + at_x * self.node_y + at_y

    def tables(self):
        stack = 4 * self.edge + 2 * self.own_nodes
        side = self.side_nodes
        to_left = np.zeros((2 * side, stack), np.float32)
        to_right = np.zeros((2 * side, stack), np.float32)
        for kind in range(2):
            for at_x in range(self.out_x):
                for k in range(NODES_OUT):
                    row = kind * side + at_x * NODES_OUT + k
                    to_left[row, self.center_row(at_x, k, kind)] = 1
                    last = self.node_y - NODES_OUT + k
                    to_right[row, self.center_row(at_x, last, kind)] = 1
        place = np.zeros((2, self.nodes, stack + 4 * side), np.float32)
        for kind in range(2):
            for at_x in range(self.out_x):
                for slot in range(self.node_y + 2 * NODES_OUT):
                    at_y = slot - NODES_OUT
                    if at_y < 0:
                        column = stack + kind * side + at_x * NODES_OUT + slot
                    elif at_y < self.node_y:
                        column = self.center_row(at_x, at_y, kind)
                    else:
                        k = at_y - self.node_y
                        column = stack + 2 * side + kind * side + at_x * NODES_OUT + k
                    place[kind, at_x * SLOTS + slot, column] = 1
        spread = np.zeros((2, 128, self.window), np.float32)
        match = np.zeros((2, SLOTS, self.window), np.float32)
        for dx in range(6):
            for at in range(self.pitch):
                if at < self.tile_y:
                    y = at
                elif at < self.tile_y + SIDE:
                    y = at - self.tile_y - SIDE
                else:
                    y = at - SIDE
                quotient, rest = (y + REACH) // 4, (y + REACH) % 4
                lane = dx * self.pitch + at
                spread[0, dx * 6 + rest, lane] = 1
                if 0 <= quotient < SLOTS:
                    match[0, quotient, lane] = 1
                if rest < 2:
                    spread[1, dx * 6 + rest + 4, lane] = 1
                    if 0 <= quotient - 1 < SLOTS:
                        match[1, quotient - 1, lane] = 1
        node = np.arange(self.nodes)
        quad = node // SLOTS // 2 * SLOTS + node % SLOTS // 2
        same = (quad[:, None] == quad[None, :]).astype(np.float32)
        return {
            "to_side": np.stack([to_left, to_right]),
            "place": place,
            "spread": spread,
            "match": match,
            "quad": np.concatenate([same, same], axis=1),
        }


def pack_kernel(
    shape,
    units,
    place_ref,
    own_ref,
    cotangent_ref,
    mask_ref,
    rows_ref,
    target_x_ref,
    target_y_ref,
    first_ref,
    second_ref,
    third_ref,
    fourth_ref,
    mesh_ref,
    own_rows_ref,
):
    edge, own_nodes, halo = shape.edge, shape.own_nodes, shape.halo
    held = rows_ref.shape[0]
    even = place_ref[0] % 2 == 0
    row_count = place_ref[1]
    target_x = target_x_ref[...]
    column = target_y_ref[...] - place_ref[2] * shape.tile_y
    slot = lax.broadcasted_iota(jnp.int32, (1, held), 1)
    column = jnp.where(slot < row_count, column, LANES - 1)
    line = lax.broadcasted_iota(jnp.int32, (16, held), 0)
    fields = jnp.where(line == 0, target_x // shape.tile_x, 0)
    fields = fields + jnp.where(line == 1, target_x % shape.tile_x, 0)
    fields = fields + jnp.where(line == 2, column, 0)
    lane = lax.broadcasted_iota(jnp.int32, (held, LANES), 1)
    repeat = lane % held == lax.broadcasted_iota(jnp.int32, (held, LANES), 0)
    spread = dot(fields.astype(F32).astype(BF16), jnp.where(repeat, 1.0, 0.0).astype(BF16))
    lane = lax.broadcasted_iota(jnp.int32, (16, LANES), 1)

    mesh_ref[:own_nodes] = cotangent_ref[...]
    mesh_ref[own_nodes:] = mask_ref[...]
    targets = (own_rows_ref, first_ref, third_ref, second_ref, fourth_ref)
    for ref, number in zip(targets, (0, 1, 2, 3, 3)):
        at = ref.shape[0] - held - 16
        ref[at : at + held] = rows_ref[...]
        ref[at + held :] = jnp.where(lane // held == number, spread, 0.0).astype(BF16)
    for ref, upward in ((first_ref, even), (second_ref, jnp.logical_not(even))):
        start = pl.multiple_of(jnp.where(upward, shape.cells - halo, 0), shape.tile_y)
        ref[:halo] = own_ref[pl.ds(start, halo)]
        start = pl.multiple_of(jnp.where(upward, own_nodes - edge, 0), 16)
        ref[halo : halo + edge] = mesh_ref[pl.ds(start, edge)]
        start = pl.multiple_of(jnp.where(upward, 2 * own_nodes - edge, own_nodes), 16)
        ref[halo + edge : halo + 2 * edge] = mesh_ref[pl.ds(start, edge)]


def blend_kernel(shape, units, unit_rows, *refs):
    (place_ref, own_ref, mesh_ref, w_force_ref, side_ref, own_rows_ref) = refs[:6]
    count = units if units > 3 else 2
    arrived = refs[6 : 6 + count]
    (blended_ref, first_ref, second_ref, stack_ref, rows_ref, key_ref) = refs[6 + count : 12 + count]
    (projected_ref,) = refs[12 + count :]
    wide_at = place_ref[0]
    even = wide_at % 2 == 0
    near, between = arrived[0], arrived[1]
    mesh = 2 * shape.edge
    first_row = shape.halo + mesh

    def held(k, at, n):
        if k == 0:
            return own_rows_ref[at : at + n]
        if k == 1:
            return near[first_row + at : first_row + at + n]
        if k < units - 1:
            return arrived[k][at : at + n]
        value = between[first_row + at : first_row + at + n]
        if units > 3:
            value = value + arrived[-1][at : at + n]
        return value

    total = unit_rows * units
    for k in range(units):
        rows_ref[k * unit_rows : (k + 1) * unit_rows] = held(k, 0, unit_rows)
    blocks = []
    if total <= LANES:
        metas = [held(k, unit_rows, 16).astype(F32) for k in range(units)]
        blocks.append(functools.reduce(lambda a, b: a + b, metas)[:, :total])
    else:
        for k in range(units):
            for part in range(unit_rows // LANES):
                blocks.append(held(k, unit_rows + 16 * part, 16).astype(F32))
    keys = []
    for block in blocks:
        whole = block.astype(jnp.int32)
        at_x = whole[0:1] * shape.tile_x + whole[1:2] - wide_at * shape.tile_x + REACH
        at_y = whole[2:3]
        inside = (at_x >= 0) & (at_x < shape.rows_x) & (at_y < shape.tile_y)
        keys.append(jnp.where(inside, at_x * shape.tile_y + at_y, -1))
    width = keys[0].shape[1]
    for k, key in enumerate(keys):
        key_ref[:, k * width : (k + 1) * width] = jnp.broadcast_to(key, (8, width))
    projected_ref[...] = dot(rows_ref[...], w_force_ref[...]).astype(BF16)

    def facing(at, n, forward):
        one, other = near[at : at + n], between[at : at + n]
        return jnp.where(even, one, other) if forward else jnp.where(even, other, one)

    stack = jnp.concatenate(
        [facing(shape.halo, mesh, False), mesh_ref[...], facing(shape.halo, mesh, True)], axis=0
    )
    stack_ref[...] = stack
    narrow_even = place_ref[2] % 2 == 0
    column = pl.multiple_of(jnp.where(narrow_even, shape.tile_y - SIDE, 0), SIDE)
    other = pl.multiple_of(jnp.where(narrow_even, 0, shape.tile_y - SIDE), SIDE)
    to_left = dot(side_ref[0], stack).astype(BF16)
    to_right = dot(side_ref[1], stack).astype(BF16)
    first_ref[shape.side :] = jnp.where(narrow_even, to_right, to_left)
    second_ref[shape.side :] = jnp.where(narrow_even, to_left, to_right)

    tile_y = shape.tile_y
    inner = shape.halo + shape.cells
    jobs = [(0, at, n) for at, n in pieces(0, shape.halo, 3 * tile_y)]
    jobs += [(shape.halo, at, n) for at, n in pieces(0, shape.cells, 4 * tile_y)]
    jobs += [(inner, at, n) for at, n in pieces(0, shape.halo, 3 * tile_y)]
    for base, at, n in jobs:
        first = base + at
        if base == shape.halo:
            value = own_ref[at : at + n].astype(F32)
        else:
            value = facing(at, n, base == inner).astype(F32)
        cell = lax.broadcasted_iota(jnp.int32, (n, width), 0) + first
        for k, key in enumerate(keys):
            hit = jnp.where(cell == key, 1.0, 0.0).astype(BF16)
            value = value + dot(hit, projected_ref[k * width : (k + 1) * width])
        blended_ref[first : first + n] = value.astype(BF16)
    for row in range(shape.rows_x):
        target = slice(row * SIDE, (row + 1) * SIDE)
        first_ref[target] = blended_ref[pl.ds(row * tile_y + column, SIDE)]
        second_ref[target] = blended_ref[pl.ds(row * tile_y + other, SIDE)]


def forward_kernel(
    shape, blended_ref, w_embed_ref, w_message_ref, message_ref, latent_ref, embed_ref, slope_ref
):
    inner = shape.halo + shape.cells
    jobs = pieces(0, shape.halo, 96) + pieces(shape.halo, inner, 128)
    jobs += pieces(inner, shape.center, 96)
    for at, n in jobs:
        blended = blended_ref[at : at + n]
        pre_embed = dot(blended, w_embed_ref[...])
        value, slope = silu_and_slope(pre_embed)
        latent = (blended.astype(F32) + value).astype(BF16)
        pre_message = dot(latent, w_message_ref[...])
        message, message_slope = silu_and_slope(pre_message)
        message_ref[at : at + n] = message.astype(BF16)
        if shape.halo <= at < inner:
            own = at - shape.halo
            latent_ref[own : own + n] = latent
            embed_ref[own : own + n] = slope
            slope_ref[own : own + n] = message_slope


def backward_kernel(shape, total_rows, *refs):
    (
        narrow_ref,
        first_ref,
        second_ref,
        stack_ref,
        blended_ref,
        message_ref,
        latent_ref,
        embed_ref,
        slope_ref,
        rows_ref,
        key_ref,
        place_ref,
        spread_ref,
        match_ref,
        quad_ref,
        w_force_ref,
        w_embed_ref,
        w_message_ref,
        w_one_ref,
        w_two_ref,
        state_ref,
        back_ref,
        sent_ref,
        kept_ref,
        padded_ref,
        level_ref,
        cover_ref,
        pmb_ref,
        peb_ref,
        grads_ref,
    ) = refs
    tile_y, pitch = shape.tile_y, shape.pitch
    channels = blended_ref.shape[1]

    even = narrow_ref[0] % 2 == 0
    first_at = pl.multiple_of(tile_y + jnp.where(even, SIDE, 0), SIDE)
    second_at = pl.multiple_of(tile_y + jnp.where(even, 0, SIDE), SIDE)
    for ref, offset in ((first_ref, first_at), (second_ref, second_at)):
        for at, n in pieces(0, shape.side, 8 * SIDE):
            blended = ref[at : at + n]
            latent = (blended.astype(F32) + silu(dot(blended, w_embed_ref[...]))).astype(BF16)
            message = silu(dot(latent, w_message_ref[...])).astype(BF16)
            for t in range(n // SIDE):
                row = (at // SIDE + t) * pitch + offset
                padded_ref[pl.ds(row, SIDE)] = message[t * SIDE : (t + 1) * SIDE]
    for row in range(shape.rows_x):
        padded_ref[row * pitch : row * pitch + tile_y] = message_ref[
            row * tile_y : (row + 1) * tile_y
        ]

    first, second = first_ref[shape.side :], second_ref[shape.side :]
    stack = jnp.concatenate(
        [stack_ref[...], jnp.where(even, second, first), jnp.where(even, first, second)], axis=0
    )
    cotangent = dot(place_ref[0], stack)
    mask = dot(place_ref[1], stack[:, :128]).astype(BF16)
    near = dot(mask, spread_ref[0])
    far = dot(mask, spread_ref[1])
    windows = []
    for at_x in range(shape.out_x):
        rows = slice(at_x * SLOTS, (at_x + 1) * SLOTS)
        windows.append(near[rows] * match_ref[0] + far[rows] * match_ref[1])
        level_ref[rows] = (
            dot(
                windows[-1].astype(BF16),
                padded_ref[4 * at_x * pitch : 4 * at_x * pitch + shape.window],
            )
            / 6.0
        ).astype(BF16)
    turned = jnp.concatenate(windows, axis=0).T
    node_x = lax.broadcasted_iota(jnp.int32, (tile_y, shape.nodes), 1) // SLOTS
    for at_x in range(shape.tile_x):
        quotient, rest = (at_x + REACH) // 4, (at_x + REACH) % 4
        cover = jnp.where(node_x == quotient, turned[rest * pitch : rest * pitch + tile_y], 0.0)
        if rest < 2:
            again = (rest + 4) * pitch
            cover = cover + jnp.where(
                node_x == quotient - 1, turned[again : again + tile_y], 0.0
            )
        cover = cover.astype(BF16)
        cover_ref[at_x * tile_y : (at_x + 1) * tile_y] = jnp.concatenate([cover, cover], axis=1)

    level_one = level_ref[...]
    pre_one = dot(level_one, w_one_ref[...])
    value, slope_one = silu_and_slope(pre_one)
    state_one = level_one.astype(F32) + value
    level_two = (0.25 * dot(quad_ref[...], two_halves(state_one))).astype(BF16)
    pre_two = dot(level_two, w_two_ref[...])
    two_bar = dot(quad_ref[:, : shape.nodes], cotangent.astype(BF16))
    pre_two_bar = (two_bar * silu_and_slope(pre_two)[1]).astype(BF16)
    pooled_bar = two_bar + dot_right_t(pre_two_bar, w_two_ref[...])
    one_bar = cotangent + 0.25 * pooled_bar
    pre_one_bar = (one_bar * slope_one).astype(BF16)
    level_bar = one_bar + dot_right_t(pre_one_bar, w_one_ref[...])

    node = lax.broadcasted_iota(jnp.int32, (shape.nodes, channels), 0)
    at_x, at_y = node // SLOTS, node % SLOTS
    owned = (at_x >= NODES_OUT) & (at_x < NODES_OUT + shape.node_x)
    owned = owned & (at_y >= NODES_OUT) & (at_y < NODES_OUT + shape.node_y)
    first = owned & (at_x % 2 == 0) & (at_y % 2 == 0)
    grads_ref[3 * channels : 4 * channels] = dot_left_t(
        level_one, jnp.where(owned, pre_one_bar.astype(F32), 0.0).astype(BF16)
    )
    grads_ref[4 * channels :] = dot_left_t(
        level_two, jnp.where(first, pre_two_bar.astype(F32), 0.0).astype(BF16)
    )

    both = two_halves(level_bar)
    for at, n in pieces(0, shape.cells, 128):
        rows = slice(at, at + n)
        message_bar = dot(cover_ref[rows], both) / 6.0
        pre_message_bar = (message_bar * slope_ref[rows]).astype(BF16)
        pmb_ref[rows] = pre_message_bar
        latent_bar = dot_right_t(pre_message_bar, w_message_ref[...])
        pre_embed_bar = (latent_bar * embed_ref[rows]).astype(BF16)
        peb_ref[rows] = pre_embed_bar
        state_ref[rows] = (latent_bar + dot_right_t(pre_embed_bar, w_embed_ref[...])).astype(BF16)
    own = slice(shape.halo, shape.halo + shape.cells)
    grads_ref[channels : 2 * channels] = dot_left_t(blended_ref[own], peb_ref[...])
    grads_ref[2 * channels : 3 * channels] = dot_left_t(latent_ref[...], pmb_ref[...])

    width = min(total_rows, LANES)
    cell = lax.broadcasted_iota(jnp.int32, (shape.cells, width), 0) + shape.halo
    grad_force = None
    for at in range(0, total_rows, width):
        rows = slice(at, at + width)
        hit = jnp.where(cell == key_ref[0:1, rows], 1.0, 0.0).astype(BF16)
        slot_bar = dot_left_t(hit, state_ref[...]).astype(BF16)
        back_ref[rows] = dot_right_t(slot_bar, w_force_ref[...]).astype(BF16)
        term = dot_left_t(rows_ref[rows], slot_bar)
        grad_force = term if grad_force is None else grad_force + term
    grads_ref[:channels] = grad_force

    half = sent_ref.shape[0]
    upper = narrow_ref[0] % 2
    kept_at = pl.multiple_of(upper * half, half)
    sent_at = pl.multiple_of((1 - upper) * half, half)
    sent_ref[...] = grads_ref[pl.ds(sent_at, half)].astype(BF16)
    kept_ref[...] = grads_ref[pl.ds(kept_at, half)]


def finish_kernel(scales, place_ref, own_ref, other_ref, out_ref):
    even = place_ref[2] % 2 == 0
    half = own_ref.shape[0]
    channels = own_ref.shape[1]
    for k, scale in enumerate(scales):
        for start, stop, lower in ((0, half, True), (half, 2 * half, False)):
            at = max(k * channels, start)
            end = min((k + 1) * channels, stop)
            if at >= end:
                continue
            own, other = own_ref[at - start : end - start], other_ref[at - start : end - start]
            value = jnp.where(even, own, other) if lower else jnp.where(even, other, own)
            out_ref[k, at - k * channels : end - k * channels] = value.astype(F32) * scale


def call(kernel, out_shapes, operands, scratch=(), scalars=1, flops=0):
    specs = [pl.BlockSpec(memory_space=pltpu.SMEM)] * scalars
    specs += [pl.BlockSpec(memory_space=pltpu.VMEM)] * (len(operands) - scalars)
    moved = sum(math.prod(o.shape) * o.dtype.itemsize for o in list(operands) + list(out_shapes))
    return pl.pallas_call(
        kernel,
        out_shape=tuple(out_shapes),
        in_specs=specs,
        out_specs=tuple(pl.BlockSpec(memory_space=pltpu.VMEM) for _ in out_shapes),
        scratch_shapes=list(scratch),
        compiler_params=pltpu.CompilerParams(vmem_limit_bytes=VMEM_LIMIT),
        cost_estimate=pl.CostEstimate(flops=flops, bytes_accessed=moved, transcendentals=0),
    )(*operands)


def meta_rows(live, target_x, target_y, tile_x, unit_rows, slot, units):
    high = target_x // tile_x
    low = target_x % tile_x
    column = jnp.where(live, target_y, LANES - 1)
    fields = jnp.stack([high, low, column]).astype(F32)
    if unit_rows * units <= LANES:
        before = slot * unit_rows
        after = LANES - before - unit_rows
        return jnp.pad(fields, ((0, 13), (before, after))).astype(BF16)
    blocks = unit_rows // LANES
    fields = fields.reshape(3, blocks, LANES).transpose(1, 0, 2)
    return jnp.pad(fields, ((0, 0), (0, 13), (0, 0))).reshape(16 * blocks, LANES).astype(BF16)


def local(
    grid_state,
    boundary_rows,
    row_count,
    target_x,
    target_y,
    g2m_mask,
    mesh_cotangent,
    w_force,
    w_embed,
    w_message,
    w_level_one,
    w_level_two,
):
    tile_x, tile_y, channels = grid_state.shape
    wide_count = lax.axis_size("wide")
    narrow_count = lax.axis_size("narrow")
    wide_at = lax.axis_index("wide")
    narrow_at = lax.axis_index("narrow")
    held_rows = boundary_rows.shape[0]
    shape = Shape(tile_x, tile_y)
    table = {name: jnp.asarray(value, BF16) for name, value in shape.tables().items()}
    table["match"] = table["match"].astype(F32)

    live = jnp.arange(held_rows) < row_count[0]
    column = target_y - narrow_at * tile_y
    whole_column = wide_count == 4 and held_rows * wide_count <= LANES
    if whole_column:
        units = wide_count
        unit_rows = held_rows
        rows, row_live, row_x, row_y = boundary_rows, live, target_x, column
    else:
        slot_count = wide_count * CAP
        destination = target_x // tile_x
        matches = (destination[:, None] == jnp.arange(wide_count)[None, :]) & live[:, None]
        running = jnp.cumsum(matches.astype(jnp.int32), axis=0) - 1
        slot_index = jnp.sum(jnp.where(matches, running, 0), axis=1)
        send_slot = jnp.where(live, destination * CAP + slot_index, slot_count)
        cells = jnp.full((slot_count,), -1, jnp.int32)
        cells = cells.at[send_slot].set(target_x % tile_x * tile_y + column, mode="drop")
        outgoing = jnp.zeros((slot_count, channels), BF16)
        outgoing = outgoing.at[send_slot].set(boundary_rows, mode="drop")
        outgoing = outgoing.reshape(wide_count, CAP, channels)
        rows = lax.all_to_all(outgoing, "wide", split_axis=0, concat_axis=0, tiled=True)
        cells = lax.all_to_all(
            cells.reshape(wide_count, CAP), "wide", split_axis=0, concat_axis=0, tiled=True
        )
        rows = rows.reshape(slot_count, channels)
        cells = cells.reshape(slot_count)
        units = 3
        unit_rows = slot_count
        row_live = cells >= 0
        row_x = jnp.where(row_live, wide_at * tile_x + cells // tile_y, 0)
        row_y = cells % tile_y

    cells = grid_state.reshape(-1, channels)
    cotangent = mesh_cotangent.reshape(-1, channels)
    mask = g2m_mask.astype(BF16).transpose(1, 2, 0).reshape(-1, 36)
    mask = jnp.pad(mask, ((0, 0), (0, channels - 36)))
    place = jnp.stack([wide_at, row_count[0], narrow_at])
    struct = jax.ShapeDtypeStruct
    long = struct((shape.halo + 2 * shape.edge + unit_rows + 16, channels), BF16)
    short = struct((unit_rows + 16, channels), BF16)
    if whole_column:
        first, second, third, fourth, mesh, own_rows = call(
            functools.partial(pack_kernel, shape, units),
            [long, long, short, short, struct((2 * shape.own_nodes, channels), BF16), short],
            [
                place,
                cells,
                cotangent,
                mask,
                rows,
                target_x.reshape(1, -1),
                target_y.reshape(1, -1),
            ],
        )
        arrived = [
            swapped(first, "wide", 1),
            swapped_between(second, "wide"),
            swapped(third, "wide", 2),
            lax.ppermute(fourth, "wide", [(0, 3), (3, 0)]),
        ]
    else:

        def with_meta(slot):
            return [rows, meta_rows(row_live, row_x, row_y, tile_x, unit_rows, slot, units)]

        mesh = jnp.concatenate([cotangent, mask])
        own_rows = jnp.concatenate(with_meta(0))
        edge = shape.edge
        to_prev = [cells[: shape.halo], cotangent[:edge], mask[:edge]]
        to_next = [cells[-shape.halo :], cotangent[-edge:], mask[-edge:]]
        to_prev, to_next = jnp.concatenate(to_prev), jnp.concatenate(to_next)
        upward = wide_at % 2 == 0
        first = jnp.concatenate([jnp.where(upward, to_next, to_prev)] + with_meta(1))
        second = jnp.concatenate([jnp.where(upward, to_prev, to_next)] + with_meta(2))
        arrived = [swapped(first, "wide", 1), swapped_between(second, "wide")]

    total_rows = unit_rows * units
    stack_rows = 4 * shape.edge + 2 * shape.own_nodes
    payload = struct((shape.side + 2 * shape.side_nodes, channels), BF16)
    blended, first, second, stack, all_rows, keys = call(
        functools.partial(blend_kernel, shape, units, unit_rows),
        [
            struct((shape.center, channels), BF16),
            payload,
            payload,
            struct((stack_rows, channels), BF16),
            struct((total_rows, channels), BF16),
            struct((8, total_rows), jnp.int32),
        ],
        [place, cells, mesh, w_force, table["to_side"], own_rows] + arrived,
        scratch=[pltpu.VMEM((total_rows, channels), BF16)],
        flops=2 * shape.center * total_rows * channels,
    )
    second = swapped_between(second, "narrow")
    first = swapped(first, "narrow", 1)
    message, latent, embed_slope, message_slope = call(
        functools.partial(forward_kernel, shape),
        [
            struct((shape.center, channels), BF16),
            struct((shape.cells, channels), BF16),
            struct((shape.cells, channels), F32),
            struct((shape.cells, channels), F32),
        ],
        [blended, w_embed, w_message],
        scalars=0,
        flops=4 * shape.center * channels * channels,
    )
    grad_rows_total = 5 * channels
    grad_state, back, sent, kept = call(
        functools.partial(backward_kernel, shape, total_rows),
        [
            struct((shape.cells, channels), BF16),
            struct((total_rows, channels), BF16),
            struct((grad_rows_total // 2, channels), BF16),
            struct((grad_rows_total // 2, channels), F32),
        ],
        [
            narrow_at.reshape(1),
            first,
            second,
            stack,
            blended,
            message,
            latent,
            embed_slope,
            message_slope,
            all_rows,
            keys,
            table["place"],
            table["spread"],
            table["match"],
            table["quad"],
            w_force,
            w_embed,
            w_message,
            w_level_one,
            w_level_two,
        ],
        scratch=[
            pltpu.VMEM((shape.rows_x * shape.pitch, channels), BF16),
            pltpu.VMEM((shape.nodes, channels), BF16),
            pltpu.VMEM((shape.cells, 2 * shape.nodes), BF16),
            pltpu.VMEM((shape.cells, channels), BF16),
            pltpu.VMEM((shape.cells, channels), BF16),
            pltpu.VMEM((grad_rows_total, channels), F32),
        ],
        flops=12 * shape.cells * channels * channels,
    )

    piece = kept + swapped(sent, "narrow", 1).astype(F32)
    back_blocks = back.reshape(units, unit_rows, channels)
    row_back = back_blocks[0].astype(F32)
    others = narrow_count // 2
    if wide_count * others <= 8:
        group = wide_count * others
        part = piece.shape[0] // group
        at = wide_at * others + narrow_at // 2
        rounded = piece.astype(BF16)
        own = lax.dynamic_slice_in_dim(piece, at * part, part)
        order = sorted(range(1, group), key=lambda k: (k // others < 2, k % others == 0))
        for k in order:
            wide_bits, narrow_bits = k // others, k % others
            sent = lax.dynamic_slice_in_dim(rounded, (at ^ k) * part, part)
            if narrow_bits == 0 and whole_column:
                sent = jnp.concatenate([sent, back_blocks[wide_bits]])
            got = swapped_both(sent, wide_bits, 2 * narrow_bits).astype(F32)
            own = own + got[:part]
            if narrow_bits == 0 and whole_column:
                row_back = row_back + got[part:]
        own = own.astype(BF16)
        gathered = jnp.zeros((group * part, channels), BF16)
        gathered = lax.dynamic_update_slice_in_dim(gathered, own, at * part, 0)
        for k in order:
            got = swapped_both(own, k // others, 2 * (k % others))
            gathered = lax.dynamic_update_slice_in_dim(gathered, got, (at ^ k) * part, 0)
    else:
        bits = [1 << k for k in range(1, narrow_count.bit_length() - 1)]
        for bit in bits:
            half = piece.shape[0] // 2
            upper = (narrow_at // bit) % 2
            sent = lax.dynamic_slice_in_dim(piece, (1 - upper) * half, half).astype(BF16)
            kept = lax.dynamic_slice_in_dim(piece, upper * half, half)
            piece = kept + swapped(sent, "narrow", bit).astype(F32)
        part = piece.shape[0] // wide_count
        rounded = piece.astype(BF16)
        own = lax.dynamic_slice_in_dim(piece, wide_at * part, part)
        for k in range(1, wide_count):
            sent = lax.dynamic_slice_in_dim(rounded, (wide_at ^ k) * part, part)
            own = own + swapped(sent, "wide", k).astype(F32)
        own = own.astype(BF16)
        gathered = jnp.zeros((wide_count * part, channels), BF16)
        gathered = lax.dynamic_update_slice_in_dim(gathered, own, wide_at * part, 0)
        for k in range(1, wide_count):
            got = swapped(own, "wide", k)
            gathered = lax.dynamic_update_slice_in_dim(gathered, got, (wide_at ^ k) * part, 0)
        for bit in reversed(bits):
            upper = (narrow_at // bit) % 2
            other = swapped(gathered, "narrow", bit)
            gathered = jnp.where(
                upper == 0,
                jnp.concatenate([gathered, other]),
                jnp.concatenate([other, gathered]),
            )
    other = swapped(gathered, "narrow", 1)
    if whole_column:
        row_back = row_back.astype(BF16)
    else:
        returned = lax.all_to_all(
            back_blocks[0].reshape(wide_count, CAP, channels),
            "wide",
            split_axis=0,
            concat_axis=0,
            tiled=True,
        )
        row_back = jnp.take(
            returned.reshape(-1, channels), send_slot, axis=0, mode="fill", fill_value=0
        )
    cell_total = shape.cells * wide_count * narrow_count
    row_total = held_rows * wide_count * narrow_count
    sizes = [row_total, cell_total, cell_total, cell_total // 16, cell_total // 64]
    (weight_grads,) = call(
        functools.partial(finish_kernel, [1.0 / math.sqrt(size) for size in sizes]),
        [struct((5, channels, channels), F32)],
        [place, gathered, other],
    )
    return (grad_state.reshape(tile_x, tile_y, channels), row_back, weight_grads)


def solution(mesh):
    in_specs = (
        P(("groups", "wide"), "narrow", None),
        P(("groups", "wide", "narrow"), None),
        P(("groups", "wide", "narrow")),
        P(("groups", "wide", "narrow")),
        P(("groups", "wide", "narrow")),
        P(None, ("groups", "wide"), "narrow"),
        P(("groups", "wide"), "narrow", None),
        P(),
        P(),
        P(),
        P(),
        P(),
    )
    out_specs = (
        P(("groups", "wide"), "narrow", None),
        P(("groups", "wide", "narrow"), None),
        P("groups", None, None),
    )
    return jax.shard_map(local, mesh=mesh, in_specs=in_specs, out_specs=out_specs, check_vma=False)
```

```python
import functools
import math

import jax
import jax.numpy as jnp
import numpy as np
from jax import lax
from jax.experimental import pallas as pl
from jax.experimental.pallas import tpu as pltpu
from jax.sharding import PartitionSpec as P

CAP = 16
REACH = 9
NODES_OUT = 2
SIDE = 16
SLOTS = 16
LANES = 256
VMEM_LIMIT = 48 * 1024 * 1024
F32 = jnp.float32
BF16 = jnp.bfloat16


def swapped(block, axis, bits):
    count = lax.axis_size(axis)
    return lax.ppermute(block, axis, [(i, i ^ bits) for i in range(count)])


def swapped_between(block, axis):
    count = lax.axis_size(axis)
    pairs = [(i, i + 1) for i in range(1, count - 1, 2)]
    return lax.ppermute(block, axis, pairs + [(j, i) for i, j in pairs])


def dot(left, right):
    return jnp.dot(left, right, preferred_element_type=F32)


def dot_right_t(left, right):
    return lax.dot_general(left, right, (((1,), (1,)), ((), ())), preferred_element_type=F32)


def dot_left_t(left, right):
    return lax.dot_general(left, right, (((0,), (0,)), ((), ())), preferred_element_type=F32)


def sigmoid(value):
    return 0.5 * jnp.tanh(0.5 * value) + 0.5


def silu_and_slope(value):
    logistic = sigmoid(value)
    return value * logistic, logistic * (1.0 + value * (1.0 - logistic))


def silu(value):
    return value * sigmoid(value)


def pieces(start, stop, size):
    return [(at, min(size, stop - at)) for at in range(start, stop, size)]


def two_halves(value):
    high = value.astype(BF16)
    low = (value - high.astype(F32)).astype(BF16)
    return jnp.concatenate([high, low], axis=0)


class Shape:
    def __init__(self, tile_x, tile_y):
        self.tile_x = tile_x
        self.tile_y = tile_y
        self.cells = tile_x * tile_y
        self.rows_x = tile_x + 2 * REACH
        self.halo = REACH * tile_y
        self.center = self.rows_x * tile_y
        self.side = self.rows_x * SIDE
        self.pitch = tile_y + 2 * SIDE
        self.node_x = tile_x // 4
        self.node_y = tile_y // 4
        self.out_x = self.node_x + 2 * NODES_OUT
        self.nodes = self.out_x * SLOTS
        self.edge = NODES_OUT * self.node_y
        self.own_nodes = self.node_x * self.node_y
        self.window = 6 * self.pitch
        self.side_nodes = NODES_OUT * self.out_x

    def center_row(self, at_x, at_y, kind):
        edge, own = self.edge, self.own_nodes
        if at_x < NODES_OUT:
            return kind * edge + at_x * self.node_y + at_y
        at_x -= NODES_OUT
        if at_x < self.node_x:
            return 2 * edge + kind * own + at_x * self.node_y + at_y
        at_x -= self.node_x
        return 2 * edge + 2 * own + kind * edge + at_x * self.node_y + at_y

    def tables(self):
        stack = 4 * self.edge + 2 * self.own_nodes
        side = self.side_nodes
        to_left = np.zeros((2 * side, stack), np.float32)
        to_right = np.zeros((2 * side, stack), np.float32)
        for kind in range(2):
            for at_x in range(self.out_x):
                for k in range(NODES_OUT):
                    row = kind * side + at_x * NODES_OUT + k
                    to_left[row, self.center_row(at_x, k, kind)] = 1
                    last = self.node_y - NODES_OUT + k
                    to_right[row, self.center_row(at_x, last, kind)] = 1
        place = np.zeros((2, self.nodes, stack + 4 * side), np.float32)
        for kind in range(2):
            for at_x in range(self.out_x):
                for slot in range(self.node_y + 2 * NODES_OUT):
                    at_y = slot - NODES_OUT
                    if at_y < 0:
                        column = stack + kind * side + at_x * NODES_OUT + slot
                    elif at_y < self.node_y:
                        column = self.center_row(at_x, at_y, kind)
                    else:
                        k = at_y - self.node_y
                        column = stack + 2 * side + kind * side + at_x * NODES_OUT + k
                    place[kind, at_x * SLOTS + slot, column] = 1
        spread = np.zeros((2, 128, self.window), np.float32)
        match = np.zeros((2, SLOTS, self.window), np.float32)
        for dx in range(6):
            for at in range(self.pitch):
                if at < self.tile_y:
                    y = at
                elif at < self.tile_y + SIDE:
                    y = at - self.tile_y - SIDE
                else:
                    y = at - SIDE
                quotient, rest = (y + REACH) // 4, (y + REACH) % 4
                lane = dx * self.pitch + at
                spread[0, dx * 6 + rest, lane] = 1
                if 0 <= quotient < SLOTS:
                    match[0, quotient, lane] = 1
                if rest < 2:
                    spread[1, dx * 6 + rest + 4, lane] = 1
                    if 0 <= quotient - 1 < SLOTS:
                        match[1, quotient - 1, lane] = 1
        node = np.arange(self.nodes)
        quad = node // SLOTS // 2 * SLOTS + node % SLOTS // 2
        same = (quad[:, None] == quad[None, :]).astype(np.float32)
        return {
            "to_side": np.stack([to_left, to_right]),
            "place": place,
            "spread": spread,
            "match": match,
            "quad": np.concatenate([same, same], axis=1),
        }


def fetch(sources, targets, sems):
    copies = [
        pltpu.make_async_copy(source, target, sems.at[k])
        for k, (source, target) in enumerate(zip(sources, targets))
    ]
    for copy in copies:
        copy.start()
    return copies


def pack_kernel(
    shape,
    units,
    place_ref,
    own_hbm,
    cotangent_hbm,
    mask_hbm,
    rows_hbm,
    target_x_hbm,
    target_y_hbm,
    count_hbm,
    first_ref,
    second_ref,
    third_ref,
    fourth_ref,
    mesh_ref,
    own_rows_ref,
    mask_ref,
    rows_ref,
    target_x_ref,
    target_y_ref,
    count_ref,
    sems,
):
    edge, own_nodes, halo = shape.edge, shape.own_nodes, shape.halo
    held = rows_ref.shape[0]
    even = place_ref[0] % 2 == 0
    odd = jnp.logical_not(even)
    starts = [
        pl.multiple_of(jnp.where(upward, shape.cells - halo, 0), shape.tile_y)
        for upward in (even, odd)
    ]
    copies = fetch(
        [
            count_hbm,
            target_x_hbm,
            target_y_hbm,
            rows_hbm,
            cotangent_hbm,
            mask_hbm,
            own_hbm.at[pl.ds(starts[0], halo)],
            own_hbm.at[pl.ds(starts[1], halo)],
        ],
        [
            count_ref,
            target_x_ref,
            target_y_ref,
            rows_ref,
            mesh_ref.at[:own_nodes],
            mask_ref,
            first_ref.at[:halo],
            second_ref.at[:halo],
        ],
        sems,
    )
    for copy in copies[:4]:
        copy.wait()
    row_count = count_ref[0]
    target_x = target_x_ref[...]
    column = target_y_ref[...] - place_ref[1] * shape.tile_y
    slot = lax.broadcasted_iota(jnp.int32, (1, held), 1)
    column = jnp.where(slot < row_count, column, LANES - 1)
    line = lax.broadcasted_iota(jnp.int32, (16, held), 0)
    fields = jnp.where(line == 0, target_x // shape.tile_x, 0)
    fields = fields + jnp.where(line == 1, target_x % shape.tile_x, 0)
    fields = fields + jnp.where(line == 2, column, 0)
    lane = lax.broadcasted_iota(jnp.int32, (held, LANES), 1)
    repeat = lane % held == lax.broadcasted_iota(jnp.int32, (held, LANES), 0)
    spread = dot(fields.astype(F32).astype(BF16), jnp.where(repeat, 1.0, 0.0).astype(BF16))
    lane = lax.broadcasted_iota(jnp.int32, (16, LANES), 1)
    for number, ref in enumerate((own_rows_ref, first_ref, third_ref, fourth_ref)):
        at = ref.shape[0] - held - 16
        ref[at : at + held] = rows_ref[...]
        ref[at + held :] = jnp.where(lane // held == number, spread, 0.0).astype(BF16)

    for copy in copies[4:6]:
        copy.wait()
    mesh_ref[own_nodes:] = jnp.zeros((own_nodes, mesh_ref.shape[1]), BF16)
    mesh_ref[own_nodes:, : mask_ref.shape[1]] = mask_ref[...].astype(F32).astype(BF16)
    for ref, upward in ((first_ref, even), (second_ref, odd)):
        start = pl.multiple_of(jnp.where(upward, own_nodes - edge, 0), 16)
        ref[halo : halo + edge] = mesh_ref[pl.ds(start, edge)]
        start = pl.multiple_of(jnp.where(upward, 2 * own_nodes - edge, own_nodes), 16)
        ref[halo + edge : halo + 2 * edge] = mesh_ref[pl.ds(start, edge)]
    for copy in copies[6:]:
        copy.wait()


def load_kernel(count, *refs):
    sources, targets, sems = refs[1 : 1 + count], refs[1 + count : 1 + 2 * count], refs[-1]
    for copy in fetch(sources, targets, sems):
        copy.wait()


def blend_kernel(shape, units, unit_rows, *refs):
    (place_ref, own_ref, mesh_ref, w_force_ref, side_ref, own_rows_ref) = refs[:6]
    count = units if units > 3 else 2
    arrived = refs[6 : 6 + count]
    (blended_ref, first_ref, second_ref, stack_ref, rows_ref, key_ref) = refs[6 + count : 12 + count]
    (projected_ref,) = refs[12 + count :]
    wide_at = place_ref[0]
    even = wide_at % 2 == 0
    near, between = arrived[0], arrived[1]
    mesh = 2 * shape.edge
    first_row = shape.halo + mesh

    def held(k, at, n):
        if k == 0:
            return own_rows_ref[at : at + n]
        if k == 1 or units == 3:
            return arrived[k - 1][first_row + at : first_row + at + n]
        return arrived[k][at : at + n]

    total = unit_rows * units
    for k in range(units):
        rows_ref[k * unit_rows : (k + 1) * unit_rows] = held(k, 0, unit_rows)
    blocks = []
    if total <= LANES:
        metas = [held(k, unit_rows, 16).astype(F32) for k in range(units)]
        blocks.append(functools.reduce(lambda a, b: a + b, metas)[:, :total])
    else:
        for k in range(units):
            for part in range(unit_rows // LANES):
                blocks.append(held(k, unit_rows + 16 * part, 16).astype(F32))
    keys = []
    for block in blocks:
        whole = block.astype(jnp.int32)
        at_x = whole[0:1] * shape.tile_x + whole[1:2] - wide_at * shape.tile_x + REACH
        at_y = whole[2:3]
        inside = (at_x >= 0) & (at_x < shape.rows_x) & (at_y < shape.tile_y)
        keys.append(jnp.where(inside, at_x * shape.tile_y + at_y, -1))
    width = keys[0].shape[1]
    for k, key in enumerate(keys):
        key_ref[:, k * width : (k + 1) * width] = jnp.broadcast_to(key, (8, width))
    projected_ref[...] = dot(rows_ref[...], w_force_ref[...]).astype(BF16)

    def facing(at, n, forward):
        one, other = near[at : at + n], between[at : at + n]
        return jnp.where(even, one, other) if forward else jnp.where(even, other, one)

    stack = jnp.concatenate(
        [facing(shape.halo, mesh, False), mesh_ref[...], facing(shape.halo, mesh, True)], axis=0
    )
    stack_ref[...] = stack
    narrow_even = place_ref[1] % 2 == 0
    column = pl.multiple_of(jnp.where(narrow_even, shape.tile_y - SIDE, 0), SIDE)
    other = pl.multiple_of(jnp.where(narrow_even, 0, shape.tile_y - SIDE), SIDE)
    to_left = dot(side_ref[0], stack).astype(BF16)
    to_right = dot(side_ref[1], stack).astype(BF16)
    first_ref[shape.side :] = jnp.where(narrow_even, to_right, to_left)
    second_ref[shape.side :] = jnp.where(narrow_even, to_left, to_right)

    tile_y = shape.tile_y
    inner = shape.halo + shape.cells
    jobs = [(0, at, n) for at, n in pieces(0, shape.halo, 3 * tile_y)]
    jobs += [(shape.halo, at, n) for at, n in pieces(0, shape.cells, 4 * tile_y)]
    jobs += [(inner, at, n) for at, n in pieces(0, shape.halo, 3 * tile_y)]
    for base, at, n in jobs:
        first = base + at
        if base == shape.halo:
            value = own_ref[at : at + n].astype(F32)
        else:
            value = facing(at, n, base == inner).astype(F32)
        cell = lax.broadcasted_iota(jnp.int32, (n, width), 0) + first
        for k, key in enumerate(keys):
            hit = jnp.where(cell == key, 1.0, 0.0).astype(BF16)
            value = value + dot(hit, projected_ref[k * width : (k + 1) * width])
        blended_ref[first : first + n] = value.astype(BF16)
    for row in range(shape.rows_x):
        target = slice(row * SIDE, (row + 1) * SIDE)
        first_ref[target] = blended_ref[pl.ds(row * tile_y + column, SIDE)]
        second_ref[target] = blended_ref[pl.ds(row * tile_y + other, SIDE)]


def forward_kernel(
    shape, blended_ref, w_embed_ref, w_message_ref, message_ref, latent_ref, embed_ref, slope_ref
):
    inner = shape.halo + shape.cells
    jobs = pieces(0, shape.halo, 96) + pieces(shape.halo, inner, 128)
    jobs += pieces(inner, shape.center, 96)
    for at, n in jobs:
        blended = blended_ref[at : at + n]
        pre_embed = dot(blended, w_embed_ref[...])
        value, slope = silu_and_slope(pre_embed)
        latent = (blended.astype(F32) + value).astype(BF16)
        pre_message = dot(latent, w_message_ref[...])
        message, message_slope = silu_and_slope(pre_message)
        message_ref[at : at + n] = message.astype(BF16)
        if shape.halo <= at < inner:
            own = at - shape.halo
            latent_ref[own : own + n] = latent
            embed_ref[own : own + n] = slope
            slope_ref[own : own + n] = message_slope


def backward_kernel(shape, total_rows, *refs):
    (
        narrow_ref,
        first_ref,
        second_ref,
        stack_ref,
        blended_ref,
        message_ref,
        latent_ref,
        embed_ref,
        slope_ref,
        rows_ref,
        key_ref,
        place_ref,
        spread_ref,
        match_ref,
        quad_ref,
        w_force_ref,
        w_embed_ref,
        w_message_ref,
        w_one_ref,
        w_two_ref,
        state_ref,
        back_ref,
        sent_ref,
        kept_ref,
        padded_ref,
        level_ref,
        cover_ref,
        pmb_ref,
        peb_ref,
        grads_ref,
    ) = refs
    tile_y, pitch = shape.tile_y, shape.pitch
    channels = blended_ref.shape[1]

    even = narrow_ref[0] % 2 == 0
    first_at = pl.multiple_of(tile_y + jnp.where(even, SIDE, 0), SIDE)
    second_at = pl.multiple_of(tile_y + jnp.where(even, 0, SIDE), SIDE)
    for ref, offset in ((first_ref, first_at), (second_ref, second_at)):
        for at, n in pieces(0, shape.side, 8 * SIDE):
            blended = ref[at : at + n]
            latent = (blended.astype(F32) + silu(dot(blended, w_embed_ref[...]))).astype(BF16)
            message = silu(dot(latent, w_message_ref[...])).astype(BF16)
            for t in range(n // SIDE):
                row = (at // SIDE + t) * pitch + offset
                padded_ref[pl.ds(row, SIDE)] = message[t * SIDE : (t + 1) * SIDE]
    for row in range(shape.rows_x):
        padded_ref[row * pitch : row * pitch + tile_y] = message_ref[
            row * tile_y : (row + 1) * tile_y
        ]

    first, second = first_ref[shape.side :], second_ref[shape.side :]
    stack = jnp.concatenate(
        [stack_ref[...], jnp.where(even, second, first), jnp.where(even, first, second)], axis=0
    )
    cotangent = dot(place_ref[0], stack)
    mask = dot(place_ref[1], stack[:, :128]).astype(BF16)
    near = dot(mask, spread_ref[0])
    far = dot(mask, spread_ref[1])
    windows = []
    for at_x in range(shape.out_x):
        rows = slice(at_x * SLOTS, (at_x + 1) * SLOTS)
        windows.append(near[rows] * match_ref[0] + far[rows] * match_ref[1])
        level_ref[rows] = (
            dot(
                windows[-1].astype(BF16),
                padded_ref[4 * at_x * pitch : 4 * at_x * pitch + shape.window],
            )
            / 6.0
        ).astype(BF16)
    turned = jnp.concatenate(windows, axis=0).T
    node_x = lax.broadcasted_iota(jnp.int32, (tile_y, shape.nodes), 1) // SLOTS
    for at_x in range(shape.tile_x):
        quotient, rest = (at_x + REACH) // 4, (at_x + REACH) % 4
        cover = jnp.where(node_x == quotient, turned[rest * pitch : rest * pitch + tile_y], 0.0)
        if rest < 2:
            again = (rest + 4) * pitch
            cover = cover + jnp.where(
                node_x == quotient - 1, turned[again : again + tile_y], 0.0
            )
        cover = cover.astype(BF16)
        cover_ref[at_x * tile_y : (at_x + 1) * tile_y] = jnp.concatenate([cover, cover], axis=1)

    level_one = level_ref[...]
    pre_one = dot(level_one, w_one_ref[...])
    value, slope_one = silu_and_slope(pre_one)
    state_one = level_one.astype(F32) + value
    level_two = (0.25 * dot(quad_ref[...], two_halves(state_one))).astype(BF16)
    pre_two = dot(level_two, w_two_ref[...])
    two_bar = dot(quad_ref[:, : shape.nodes], cotangent.astype(BF16))
    pre_two_bar = (two_bar * silu_and_slope(pre_two)[1]).astype(BF16)
    pooled_bar = two_bar + dot_right_t(pre_two_bar, w_two_ref[...])
    one_bar = cotangent + 0.25 * pooled_bar
    pre_one_bar = (one_bar * slope_one).astype(BF16)
    level_bar = one_bar + dot_right_t(pre_one_bar, w_one_ref[...])

    node = lax.broadcasted_iota(jnp.int32, (shape.nodes, channels), 0)
    at_x, at_y = node // SLOTS, node % SLOTS
    owned = (at_x >= NODES_OUT) & (at_x < NODES_OUT + shape.node_x)
    owned = owned & (at_y >= NODES_OUT) & (at_y < NODES_OUT + shape.node_y)
    first = owned & (at_x % 2 == 0) & (at_y % 2 == 0)
    grads_ref[3 * channels : 4 * channels] = dot_left_t(
        level_one, jnp.where(owned, pre_one_bar.astype(F32), 0.0).astype(BF16)
    )
    grads_ref[4 * channels :] = dot_left_t(
        level_two, jnp.where(first, pre_two_bar.astype(F32), 0.0).astype(BF16)
    )

    both = two_halves(level_bar)
    for at, n in pieces(0, shape.cells, 128):
        rows = slice(at, at + n)
        message_bar = dot(cover_ref[rows], both) / 6.0
        pre_message_bar = (message_bar * slope_ref[rows]).astype(BF16)
        pmb_ref[rows] = pre_message_bar
        latent_bar = dot_right_t(pre_message_bar, w_message_ref[...])
        pre_embed_bar = (latent_bar * embed_ref[rows]).astype(BF16)
        peb_ref[rows] = pre_embed_bar
        state_ref[rows] = (latent_bar + dot_right_t(pre_embed_bar, w_embed_ref[...])).astype(BF16)
    own = slice(shape.halo, shape.halo + shape.cells)
    grads_ref[channels : 2 * channels] = dot_left_t(blended_ref[own], peb_ref[...])
    grads_ref[2 * channels : 3 * channels] = dot_left_t(latent_ref[...], pmb_ref[...])

    width = min(total_rows, LANES)
    cell = lax.broadcasted_iota(jnp.int32, (shape.cells, width), 0) + shape.halo
    grad_force = None
    for at in range(0, total_rows, width):
        rows = slice(at, at + width)
        hit = jnp.where(cell == key_ref[0:1, rows], 1.0, 0.0).astype(BF16)
        slot_bar = dot_left_t(hit, state_ref[...]).astype(BF16)
        back_ref[rows] = dot_right_t(slot_bar, w_force_ref[...]).astype(BF16)
        term = dot_left_t(rows_ref[rows], slot_bar)
        grad_force = term if grad_force is None else grad_force + term
    grads_ref[:channels] = grad_force

    half = sent_ref.shape[0]
    upper = narrow_ref[0] % 2
    kept_at = pl.multiple_of(upper * half, half)
    sent_at = pl.multiple_of((1 - upper) * half, half)
    sent_ref[...] = grads_ref[pl.ds(sent_at, half)].astype(BF16)
    kept_ref[...] = grads_ref[pl.ds(kept_at, half)]


def finish_kernel(scales, kept, *refs):
    place_ref, part_ref, out_ref, wide_ref, sems = refs[0], refs[1], refs[-3], refs[-2], refs[-1]
    half, channels = part_ref.shape
    upper = place_ref[1] % 2 if kept else 1 - place_ref[1] % 2
    step = channels // 2
    count = half // step
    copies = []
    for k in range(count):
        scale = jnp.where(upper == 0, scales[k // 2], scales[(count + k) // 2])
        rows = slice(k * step, (k + 1) * step)
        wide_ref[rows] = part_ref[rows].astype(F32) * scale
        target = pl.ds(pl.multiple_of(upper * half + k * step, step), step)
        copies.append(pltpu.make_async_copy(wide_ref.at[rows], out_ref.at[target], sems.at[k]))
        copies[-1].start()
    for copy in copies:
        copy.wait()


def call(
    kernel, out_shapes, operands, scratch=(), spaces="", out_space=pltpu.VMEM, flops=0, aliases=None
):
    kinds = {"s": pltpu.SMEM, "v": pltpu.VMEM, "h": pltpu.HBM}
    spaces = spaces + "v" * (len(operands) - len(spaces))
    moved = sum(math.prod(o.shape) * o.dtype.itemsize for o in list(operands) + list(out_shapes))
    return pl.pallas_call(
        kernel,
        out_shape=tuple(out_shapes),
        in_specs=[pl.BlockSpec(memory_space=kinds[space]) for space in spaces],
        out_specs=tuple(pl.BlockSpec(memory_space=out_space) for _ in out_shapes),
        scratch_shapes=list(scratch),
        input_output_aliases=aliases or {},
        compiler_params=pltpu.CompilerParams(vmem_limit_bytes=VMEM_LIMIT),
        cost_estimate=pl.CostEstimate(flops=flops, bytes_accessed=moved, transcendentals=0),
    )(*operands)


def meta_rows(live, target_x, target_y, tile_x, unit_rows, slot, units):
    high = target_x // tile_x
    low = target_x % tile_x
    column = jnp.where(live, target_y, LANES - 1)
    fields = jnp.stack([high, low, column]).astype(F32)
    if unit_rows * units <= LANES:
        before = slot * unit_rows
        after = LANES - before - unit_rows
        return jnp.pad(fields, ((0, 13), (before, after))).astype(BF16)
    blocks = unit_rows // LANES
    fields = fields.reshape(3, blocks, LANES).transpose(1, 0, 2)
    return jnp.pad(fields, ((0, 0), (0, 13), (0, 0))).reshape(16 * blocks, LANES).astype(BF16)


def local(
    grid_state,
    boundary_rows,
    row_count,
    target_x,
    target_y,
    g2m_mask,
    mesh_cotangent,
    w_force,
    w_embed,
    w_message,
    w_level_one,
    w_level_two,
):
    tile_x, tile_y, channels = grid_state.shape
    wide_count = lax.axis_size("wide")
    narrow_count = lax.axis_size("narrow")
    wide_at = lax.axis_index("wide")
    narrow_at = lax.axis_index("narrow")
    held_rows = boundary_rows.shape[0]
    shape = Shape(tile_x, tile_y)
    table = shape.tables()
    names = list(table)
    fixed = [jnp.asarray(table[name], F32 if name == "match" else BF16) for name in names]

    live = jnp.arange(held_rows) < row_count[0]
    column = target_y - narrow_at * tile_y
    whole_column = wide_count == 4 and held_rows * wide_count <= LANES
    if whole_column:
        units = wide_count
        unit_rows = held_rows
        rows, row_live, row_x, row_y = boundary_rows, live, target_x, column
    else:
        slot_count = wide_count * CAP
        destination = target_x // tile_x
        matches = (destination[:, None] == jnp.arange(wide_count)[None, :]) & live[:, None]
        running = jnp.cumsum(matches.astype(jnp.int32), axis=0) - 1
        slot_index = jnp.sum(jnp.where(matches, running, 0), axis=1)
        send_slot = jnp.where(live, destination * CAP + slot_index, slot_count)
        cells = jnp.full((slot_count,), -1, jnp.int32)
        cells = cells.at[send_slot].set(target_x % tile_x * tile_y + column, mode="drop")
        outgoing = jnp.zeros((slot_count, channels), BF16)
        outgoing = outgoing.at[send_slot].set(boundary_rows, mode="drop")
        outgoing = outgoing.reshape(wide_count, CAP, channels)
        rows = lax.all_to_all(outgoing, "wide", split_axis=0, concat_axis=0, tiled=True)
        cells = lax.all_to_all(
            cells.reshape(wide_count, CAP), "wide", split_axis=0, concat_axis=0, tiled=True
        )
        rows = rows.reshape(slot_count, channels)
        cells = cells.reshape(slot_count)
        units = 3
        unit_rows = slot_count
        row_live = cells >= 0
        row_x = jnp.where(row_live, wide_at * tile_x + cells // tile_y, 0)
        row_y = cells % tile_y

    cells = grid_state.reshape(-1, channels)
    cotangent = mesh_cotangent.reshape(-1, channels)
    mask = g2m_mask.transpose(1, 2, 0).reshape(-1, 36)
    place = jnp.stack([wide_at, narrow_at])
    struct = jax.ShapeDtypeStruct
    long = struct((shape.halo + 2 * shape.edge + unit_rows + 16, channels), BF16)
    plain = struct((shape.halo + 2 * shape.edge, channels), BF16)
    short = struct((unit_rows + 16, channels), BF16)
    dma = pltpu.SemaphoreType.DMA
    if whole_column:
        first, second, third, fourth, mesh, own_rows = call(
            functools.partial(pack_kernel, shape, units),
            [long, plain, short, short, struct((2 * shape.own_nodes, channels), BF16), short],
            [
                place,
                cells,
                cotangent,
                mask,
                rows,
                target_x.reshape(1, -1),
                target_y.reshape(1, -1),
                row_count,
            ],
            scratch=[
                pltpu.VMEM(mask.shape, jnp.int32),
                pltpu.VMEM(rows.shape, BF16),
                pltpu.VMEM((1, held_rows), jnp.int32),
                pltpu.VMEM((1, held_rows), jnp.int32),
                pltpu.SMEM((1,), jnp.int32),
                dma((8,)),
            ],
            spaces="shhhhhhh",
        )
        third = swapped(third, "wide", 2)
        fourth = swapped(fourth, "wide", 3)
        first_in = swapped(first, "wide", 1)
        arrived = [first_in, swapped_between(second, "wide"), third, fourth]
    else:

        def with_meta(slot):
            return [rows, meta_rows(row_live, row_x, row_y, tile_x, unit_rows, slot, units)]

        mask = jnp.pad(mask.astype(BF16), ((0, 0), (0, channels - 36)))
        mesh = jnp.concatenate([cotangent, mask])
        own_rows = jnp.concatenate(with_meta(0))
        edge = shape.edge
        to_prev = [cells[: shape.halo], cotangent[:edge], mask[:edge]]
        to_next = [cells[-shape.halo :], cotangent[-edge:], mask[-edge:]]
        to_prev, to_next = jnp.concatenate(to_prev), jnp.concatenate(to_next)
        upward = wide_at % 2 == 0
        first = jnp.concatenate([jnp.where(upward, to_next, to_prev)] + with_meta(1))
        second = jnp.concatenate([jnp.where(upward, to_prev, to_next)] + with_meta(2))
        arrived = [swapped(first, "wide", 1), swapped_between(second, "wide")]

    source = [cells, w_force, w_embed, w_message, w_level_one, w_level_two] + fixed
    loaded = call(
        functools.partial(load_kernel, len(source)),
        [struct(x.shape, x.dtype) for x in source],
        [own_rows] + source,
        scratch=[dma((len(source),))],
        spaces="v" + "h" * len(source),
    )
    cells, w_force, w_embed, w_message, w_level_one, w_level_two = loaded[:6]
    table = dict(zip(names, loaded[6:]))
    total_rows = unit_rows * units
    stack_rows = 4 * shape.edge + 2 * shape.own_nodes
    payload = struct((shape.side + 2 * shape.side_nodes, channels), BF16)
    blended, first, second, stack, all_rows, keys = call(
        functools.partial(blend_kernel, shape, units, unit_rows),
        [
            struct((shape.center, channels), BF16),
            payload,
            payload,
            struct((stack_rows, channels), BF16),
            struct((total_rows, channels), BF16),
            struct((8, total_rows), jnp.int32),
        ],
        [place, cells, mesh, w_force, table["to_side"], own_rows] + arrived,
        scratch=[pltpu.VMEM((total_rows, channels), BF16)],
        spaces="s",
        flops=2 * shape.center * total_rows * channels,
    )
    second = swapped_between(second, "narrow")
    first = swapped(first, "narrow", 1)
    message, latent, embed_slope, message_slope = call(
        functools.partial(forward_kernel, shape),
        [
            struct((shape.center, channels), BF16),
            struct((shape.cells, channels), BF16),
            struct((shape.cells, channels), F32),
            struct((shape.cells, channels), F32),
        ],
        [blended, w_embed, w_message],
        flops=4 * shape.center * channels * channels,
    )
    grad_rows_total = 5 * channels
    grad_state, back, sent, kept = call(
        functools.partial(backward_kernel, shape, total_rows),
        [
            struct((shape.cells, channels), BF16),
            struct((total_rows, channels), BF16),
            struct((grad_rows_total // 2, channels), BF16),
            struct((grad_rows_total // 2, channels), F32),
        ],
        [
            narrow_at.reshape(1),
            first,
            second,
            stack,
            blended,
            message,
            latent,
            embed_slope,
            message_slope,
            all_rows,
            keys,
            table["place"],
            table["spread"],
            table["match"],
            table["quad"],
            w_force,
            w_embed,
            w_message,
            w_level_one,
            w_level_two,
        ],
        scratch=[
            pltpu.VMEM((shape.rows_x * shape.pitch, channels), BF16),
            pltpu.VMEM((shape.nodes, channels), BF16),
            pltpu.VMEM((shape.cells, 2 * shape.nodes), BF16),
            pltpu.VMEM((shape.cells, channels), BF16),
            pltpu.VMEM((shape.cells, channels), BF16),
            pltpu.VMEM((grad_rows_total, channels), F32),
        ],
        spaces="s",
        flops=12 * shape.cells * channels * channels,
    )

    piece = kept + swapped(sent, "narrow", 1).astype(F32)
    back_blocks = back.reshape(units, unit_rows, channels)
    row_back = back_blocks[0].astype(F32)
    if wide_count == 4 and narrow_count == 4:

        def split(block, upper):
            half = block.shape[0] // 2
            sent = lax.dynamic_slice_in_dim(block, (1 - upper) * half, half)
            return sent, lax.dynamic_slice_in_dim(block, upper * half, half)

        def joined(block, other, upper):
            low, high = jnp.where(upper == 0, block, other), jnp.where(upper == 0, other, block)
            return jnp.concatenate([low, high])

        sent, kept = split(piece, narrow_at // 2)
        piece = kept + swapped(sent.astype(BF16), "narrow", 2).astype(F32)
        sent, kept = split(piece, wide_at % 2)
        part = kept.shape[0]
        sent = jnp.concatenate([sent.astype(BF16), back_blocks[1], back_blocks[3]])
        got = swapped(sent, "wide", 1).astype(F32)
        row_back = row_back + got[part : part + unit_rows]
        far = (back_blocks[2].astype(F32) + got[part + unit_rows :]).astype(BF16)
        rounded = (kept + got[:part]).astype(BF16)
        got = swapped(jnp.concatenate([rounded, far]), "wide", 2).astype(F32)
        row_back = row_back + got[part:]
        gathered = (rounded.astype(F32) + got[:part]).astype(BF16)
        gathered = joined(gathered, swapped(gathered, "wide", 1), wide_at % 2)
        gathered = joined(gathered, swapped(gathered, "narrow", 2), narrow_at // 2)
    else:
        bits = [1 << k for k in range(1, narrow_count.bit_length() - 1)]
        for bit in bits:
            half = piece.shape[0] // 2
            upper = (narrow_at // bit) % 2
            sent = lax.dynamic_slice_in_dim(piece, (1 - upper) * half, half).astype(BF16)
            kept = lax.dynamic_slice_in_dim(piece, upper * half, half)
            piece = kept + swapped(sent, "narrow", bit).astype(F32)
        part = piece.shape[0] // wide_count
        rounded = piece.astype(BF16)
        own = lax.dynamic_slice_in_dim(piece, wide_at * part, part)
        for k in range(1, wide_count):
            sent = lax.dynamic_slice_in_dim(rounded, (wide_at ^ k) * part, part)
            own = own + swapped(sent, "wide", k).astype(F32)
        own = own.astype(BF16)
        gathered = jnp.zeros((wide_count * part, channels), BF16)
        gathered = lax.dynamic_update_slice_in_dim(gathered, own, wide_at * part, 0)
        for k in range(1, wide_count):
            got = swapped(own, "wide", k)
            gathered = lax.dynamic_update_slice_in_dim(gathered, got, (wide_at ^ k) * part, 0)
        for bit in reversed(bits):
            upper = (narrow_at // bit) % 2
            other = swapped(gathered, "narrow", bit)
            gathered = jnp.where(
                upper == 0,
                jnp.concatenate([gathered, other]),
                jnp.concatenate([other, gathered]),
            )
    other = swapped(gathered, "narrow", 1)
    if whole_column:
        row_back = row_back.astype(BF16)
    else:
        returned = lax.all_to_all(
            back_blocks[0].reshape(wide_count, CAP, channels),
            "wide",
            split_axis=0,
            concat_axis=0,
            tiled=True,
        )
        row_back = jnp.take(
            returned.reshape(-1, channels), send_slot, axis=0, mode="fill", fill_value=0
        )
    cell_total = shape.cells * wide_count * narrow_count
    row_total = held_rows * wide_count * narrow_count
    sizes = [row_total, cell_total, cell_total, cell_total // 16, cell_total // 64]
    scales = [1.0 / math.sqrt(size) for size in sizes]
    result = struct((5 * channels, channels), F32)
    scratch = [pltpu.VMEM((5 * channels // 2, channels), F32), dma((5,))]
    (weight_grads,) = call(
        functools.partial(finish_kernel, scales, True),
        [result],
        [place, gathered],
        scratch=scratch,
        spaces="sv",
        out_space=pltpu.HBM,
    )
    (weight_grads,) = call(
        functools.partial(finish_kernel, scales, False),
        [result],
        [place, other, weight_grads],
        scratch=scratch,
        spaces="svh",
        out_space=pltpu.HBM,
        aliases={2: 0},
    )
    weight_grads = weight_grads.reshape(5, channels, channels)
    return (grad_state.reshape(tile_x, tile_y, channels), row_back, weight_grads)


def solution(mesh):
    in_specs = (
        P(("groups", "wide"), "narrow", None),
        P(("groups", "wide", "narrow"), None),
        P(("groups", "wide", "narrow")),
        P(("groups", "wide", "narrow")),
        P(("groups", "wide", "narrow")),
        P(None, ("groups", "wide"), "narrow"),
        P(("groups", "wide"), "narrow", None),
        P(),
        P(),
        P(),
        P(),
        P(),
    )
    out_specs = (
        P(("groups", "wide"), "narrow", None),
        P(("groups", "wide", "narrow"), None),
        P("groups", None, None),
    )
    return jax.shard_map(local, mesh=mesh, in_specs=in_specs, out_specs=out_specs, check_vma=False)
```

```python
import functools
import math

import jax
import jax.numpy as jnp
import numpy as np
from jax import lax
from jax.experimental import pallas as pl
from jax.experimental.pallas import tpu as pltpu
from jax.sharding import PartitionSpec as P

CAP = 16
REACH = 9
NODES_OUT = 2
SIDE = 16
SLOTS = 16
LANES = 256
LONG = 10**10
VMEM_LIMIT = 48 * 1024 * 1024
F32 = jnp.float32
BF16 = jnp.bfloat16


def swapped(block, axis, bits):
    count = lax.axis_size(axis)
    return lax.ppermute(block, axis, [(i, i ^ bits) for i in range(count)])


def swapped_between(block, axis):
    count = lax.axis_size(axis)
    pairs = [(i, i + 1) for i in range(1, count - 1, 2)]
    return lax.ppermute(block, axis, pairs + [(j, i) for i, j in pairs])


def dot(left, right):
    return jnp.dot(left, right, preferred_element_type=F32)


def dot_right_t(left, right):
    return lax.dot_general(left, right, (((1,), (1,)), ((), ())), preferred_element_type=F32)


def dot_left_t(left, right):
    return lax.dot_general(left, right, (((0,), (0,)), ((), ())), preferred_element_type=F32)


def sigmoid(value):
    return 0.5 * jnp.tanh(0.5 * value) + 0.5


def silu_and_slope(value):
    logistic = sigmoid(value)
    return value * logistic, logistic * (1.0 + value * (1.0 - logistic))


def silu(value):
    return value * sigmoid(value)


def pieces(start, stop, size):
    return [(at, min(size, stop - at)) for at in range(start, stop, size)]


def two_halves(value):
    high = value.astype(BF16)
    low = (value - high.astype(F32)).astype(BF16)
    return jnp.concatenate([high, low], axis=0)


class Shape:
    def __init__(self, tile_x, tile_y):
        self.tile_x = tile_x
        self.tile_y = tile_y
        self.cells = tile_x * tile_y
        self.rows_x = tile_x + 2 * REACH
        self.halo = REACH * tile_y
        self.center = self.rows_x * tile_y
        self.side = self.rows_x * SIDE
        self.pitch = tile_y + 2 * SIDE
        self.node_x = tile_x // 4
        self.node_y = tile_y // 4
        self.out_x = self.node_x + 2 * NODES_OUT
        self.nodes = self.out_x * SLOTS
        self.edge = NODES_OUT * self.node_y
        self.own_nodes = self.node_x * self.node_y
        self.window = 6 * self.pitch
        self.side_nodes = NODES_OUT * self.out_x

    def center_row(self, at_x, at_y, kind):
        edge, own = self.edge, self.own_nodes
        if at_x < NODES_OUT:
            return kind * edge + at_x * self.node_y + at_y
        at_x -= NODES_OUT
        if at_x < self.node_x:
            return 2 * edge + kind * own + at_x * self.node_y + at_y
        at_x -= self.node_x
        return 2 * edge + 2 * own + kind * edge + at_x * self.node_y + at_y

    def tables(self):
        stack = 4 * self.edge + 2 * self.own_nodes
        side = self.side_nodes
        to_left = np.zeros((2 * side, stack), np.float32)
        to_right = np.zeros((2 * side, stack), np.float32)
        for kind in range(2):
            for at_x in range(self.out_x):
                for k in range(NODES_OUT):
                    row = kind * side + at_x * NODES_OUT + k
                    to_left[row, self.center_row(at_x, k, kind)] = 1
                    last = self.node_y - NODES_OUT + k
                    to_right[row, self.center_row(at_x, last, kind)] = 1
        place = np.zeros((2, self.nodes, stack + 4 * side), np.float32)
        for kind in range(2):
            for at_x in range(self.out_x):
                for slot in range(self.node_y + 2 * NODES_OUT):
                    at_y = slot - NODES_OUT
                    if at_y < 0:
                        column = stack + kind * side + at_x * NODES_OUT + slot
                    elif at_y < self.node_y:
                        column = self.center_row(at_x, at_y, kind)
                    else:
                        k = at_y - self.node_y
                        column = stack + 2 * side + kind * side + at_x * NODES_OUT + k
                    place[kind, at_x * SLOTS + slot, column] = 1
        spread = np.zeros((2, 128, self.window), np.float32)
        match = np.zeros((2, SLOTS, self.window), np.float32)
        for dx in range(6):
            for at in range(self.pitch):
                if at < self.tile_y:
                    y = at
                elif at < self.tile_y + SIDE:
                    y = at - self.tile_y - SIDE
                else:
                    y = at - SIDE
                quotient, rest = (y + REACH) // 4, (y + REACH) % 4
                lane = dx * self.pitch + at
                spread[0, dx * 6 + rest, lane] = 1
                if 0 <= quotient < SLOTS:
                    match[0, quotient, lane] = 1
                if rest < 2:
                    spread[1, dx * 6 + rest + 4, lane] = 1
                    if 0 <= quotient - 1 < SLOTS:
                        match[1, quotient - 1, lane] = 1
        node = np.arange(self.nodes)
        quad = node // SLOTS // 2 * SLOTS + node % SLOTS // 2
        same = (quad[:, None] == quad[None, :]).astype(np.float32)
        return {
            "to_side": np.stack([to_left, to_right]),
            "place": place,
            "spread": spread,
            "match": match,
            "quad": np.concatenate([same, same], axis=1),
        }


def open_kernel(place_ref, out_ref):
    out_ref[0] = place_ref[0]
    out_ref[1] = place_ref[1]


def pack_kernel(
    shape,
    units,
    place_ref,
    own_ref,
    cotangent_ref,
    mask_ref,
    rows_ref,
    target_x_ref,
    target_y_ref,
    count_ref,
    first_ref,
    second_ref,
    third_ref,
    fourth_ref,
    mesh_ref,
    own_rows_ref,
):
    edge, own_nodes, halo = shape.edge, shape.own_nodes, shape.halo
    held = rows_ref.shape[0]
    even = place_ref[0] % 2 == 0
    odd = jnp.logical_not(even)
    target_x = target_x_ref[...]
    column = target_y_ref[...] - place_ref[1] * shape.tile_y
    slot = lax.broadcasted_iota(jnp.int32, (1, held), 1)
    column = jnp.where(slot < count_ref[...], column, LANES - 1)
    line = lax.broadcasted_iota(jnp.int32, (16, held), 0)
    fields = jnp.where(line == 0, target_x // shape.tile_x, 0)
    fields = fields + jnp.where(line == 1, target_x % shape.tile_x, 0)
    fields = fields + jnp.where(line == 2, column, 0)
    lane = lax.broadcasted_iota(jnp.int32, (held, LANES), 1)
    repeat = lane % held == lax.broadcasted_iota(jnp.int32, (held, LANES), 0)
    spread = dot(fields.astype(F32).astype(BF16), jnp.where(repeat, 1.0, 0.0).astype(BF16))
    lane = lax.broadcasted_iota(jnp.int32, (16, LANES), 1)
    for number, ref in enumerate((own_rows_ref, first_ref, third_ref, fourth_ref)):
        at = ref.shape[0] - held - 16
        ref[at : at + held] = rows_ref[...]
        ref[at + held :] = jnp.where(lane // held == number, spread, 0.0).astype(BF16)

    mesh_ref[:own_nodes] = cotangent_ref[...]
    mesh_ref[own_nodes:] = jnp.zeros((own_nodes, mesh_ref.shape[1]), BF16)
    mesh_ref[own_nodes:, : mask_ref.shape[1]] = mask_ref[...].astype(F32).astype(BF16)
    for ref, upward in ((first_ref, even), (second_ref, odd)):
        start = pl.multiple_of(jnp.where(upward, shape.cells - halo, 0), shape.tile_y)
        ref[:halo] = own_ref[pl.ds(start, halo)]
        start = pl.multiple_of(jnp.where(upward, own_nodes - edge, 0), 16)
        ref[halo : halo + edge] = mesh_ref[pl.ds(start, edge)]
        start = pl.multiple_of(jnp.where(upward, 2 * own_nodes - edge, own_nodes), 16)
        ref[halo + edge : halo + 2 * edge] = mesh_ref[pl.ds(start, edge)]


def blend_kernel(shape, units, unit_rows, *refs):
    (place_ref, own_ref, mesh_ref, w_force_ref, side_ref, own_rows_ref) = refs[:6]
    count = units if units > 3 else 2
    arrived = refs[6 : 6 + count]
    (blended_ref, first_ref, second_ref, stack_ref, rows_ref, key_ref) = refs[6 + count : 12 + count]
    (projected_ref,) = refs[12 + count :]
    wide_at = place_ref[0]
    even = wide_at % 2 == 0
    near, between = arrived[0], arrived[1]
    mesh = 2 * shape.edge
    first_row = shape.halo + mesh

    def held(k, at, n):
        if k == 0:
            return own_rows_ref[at : at + n]
        if k == 1 or units == 3:
            return arrived[k - 1][first_row + at : first_row + at + n]
        return arrived[k][at : at + n]

    total = unit_rows * units
    for k in range(units):
        rows_ref[k * unit_rows : (k + 1) * unit_rows] = held(k, 0, unit_rows)
    blocks = []
    if total <= LANES:
        metas = [held(k, unit_rows, 16).astype(F32) for k in range(units)]
        blocks.append(functools.reduce(lambda a, b: a + b, metas)[:, :total])
    else:
        for k in range(units):
            for part in range(unit_rows // LANES):
                blocks.append(held(k, unit_rows + 16 * part, 16).astype(F32))
    keys = []
    for block in blocks:
        whole = block.astype(jnp.int32)
        at_x = whole[0:1] * shape.tile_x + whole[1:2] - wide_at * shape.tile_x + REACH
        at_y = whole[2:3]
        inside = (at_x >= 0) & (at_x < shape.rows_x) & (at_y < shape.tile_y)
        keys.append(jnp.where(inside, at_x * shape.tile_y + at_y, -1))
    width = keys[0].shape[1]
    for k, key in enumerate(keys):
        key_ref[:, k * width : (k + 1) * width] = jnp.broadcast_to(key, (8, width))
    projected_ref[...] = dot(rows_ref[...], w_force_ref[...]).astype(BF16)

    def facing(at, n, forward):
        one, other = near[at : at + n], between[at : at + n]
        return jnp.where(even, one, other) if forward else jnp.where(even, other, one)

    stack = jnp.concatenate(
        [facing(shape.halo, mesh, False), mesh_ref[...], facing(shape.halo, mesh, True)], axis=0
    )
    stack_ref[...] = stack
    narrow_even = place_ref[1] % 2 == 0
    column = pl.multiple_of(jnp.where(narrow_even, shape.tile_y - SIDE, 0), SIDE)
    other = pl.multiple_of(jnp.where(narrow_even, 0, shape.tile_y - SIDE), SIDE)
    to_left = dot(side_ref[0], stack).astype(BF16)
    to_right = dot(side_ref[1], stack).astype(BF16)
    first_ref[shape.side :] = jnp.where(narrow_even, to_right, to_left)
    second_ref[shape.side :] = jnp.where(narrow_even, to_left, to_right)

    tile_y = shape.tile_y
    inner = shape.halo + shape.cells
    jobs = [(0, at, n) for at, n in pieces(0, shape.halo, 3 * tile_y)]
    jobs += [(shape.halo, at, n) for at, n in pieces(0, shape.cells, 4 * tile_y)]
    jobs += [(inner, at, n) for at, n in pieces(0, shape.halo, 3 * tile_y)]
    for base, at, n in jobs:
        first = base + at
        if base == shape.halo:
            value = own_ref[at : at + n].astype(F32)
        else:
            value = facing(at, n, base == inner).astype(F32)
        cell = lax.broadcasted_iota(jnp.int32, (n, width), 0) + first
        for k, key in enumerate(keys):
            hit = jnp.where(cell == key, 1.0, 0.0).astype(BF16)
            value = value + dot(hit, projected_ref[k * width : (k + 1) * width])
        blended_ref[first : first + n] = value.astype(BF16)
    for row in range(shape.rows_x):
        target = slice(row * SIDE, (row + 1) * SIDE)
        first_ref[target] = blended_ref[pl.ds(row * tile_y + column, SIDE)]
        second_ref[target] = blended_ref[pl.ds(row * tile_y + other, SIDE)]


def forward_kernel(
    shape, blended_ref, w_embed_ref, w_message_ref, message_ref, latent_ref, embed_ref, slope_ref
):
    inner = shape.halo + shape.cells
    jobs = pieces(0, shape.halo, 96) + pieces(shape.halo, inner, 128)
    jobs += pieces(inner, shape.center, 96)
    for at, n in jobs:
        blended = blended_ref[at : at + n]
        pre_embed = dot(blended, w_embed_ref[...])
        value, slope = silu_and_slope(pre_embed)
        latent = (blended.astype(F32) + value).astype(BF16)
        pre_message = dot(latent, w_message_ref[...])
        message, message_slope = silu_and_slope(pre_message)
        message_ref[at : at + n] = message.astype(BF16)
        if shape.halo <= at < inner:
            own = at - shape.halo
            latent_ref[own : own + n] = latent
            embed_ref[own : own + n] = slope
            slope_ref[own : own + n] = message_slope


def backward_kernel(shape, total_rows, *refs):
    (
        narrow_ref,
        first_ref,
        second_ref,
        stack_ref,
        blended_ref,
        message_ref,
        latent_ref,
        embed_ref,
        slope_ref,
        rows_ref,
        key_ref,
        place_ref,
        spread_ref,
        match_ref,
        quad_ref,
        w_force_ref,
        w_embed_ref,
        w_message_ref,
        w_one_ref,
        w_two_ref,
        state_ref,
        back_ref,
        sent_ref,
        kept_ref,
        padded_ref,
        level_ref,
        cover_ref,
        pmb_ref,
        peb_ref,
        grads_ref,
    ) = refs
    tile_y, pitch = shape.tile_y, shape.pitch
    channels = blended_ref.shape[1]

    even = narrow_ref[0] % 2 == 0
    first_at = pl.multiple_of(tile_y + jnp.where(even, SIDE, 0), SIDE)
    second_at = pl.multiple_of(tile_y + jnp.where(even, 0, SIDE), SIDE)
    for ref, offset in ((first_ref, first_at), (second_ref, second_at)):
        for at, n in pieces(0, shape.side, 8 * SIDE):
            blended = ref[at : at + n]
            latent = (blended.astype(F32) + silu(dot(blended, w_embed_ref[...]))).astype(BF16)
            message = silu(dot(latent, w_message_ref[...])).astype(BF16)
            for t in range(n // SIDE):
                row = (at // SIDE + t) * pitch + offset
                padded_ref[pl.ds(row, SIDE)] = message[t * SIDE : (t + 1) * SIDE]
    for row in range(shape.rows_x):
        padded_ref[row * pitch : row * pitch + tile_y] = message_ref[
            row * tile_y : (row + 1) * tile_y
        ]

    first, second = first_ref[shape.side :], second_ref[shape.side :]
    stack = jnp.concatenate(
        [stack_ref[...], jnp.where(even, second, first), jnp.where(even, first, second)], axis=0
    )
    cotangent = dot(place_ref[0], stack)
    mask = dot(place_ref[1], stack[:, :128]).astype(BF16)
    near = dot(mask, spread_ref[0])
    far = dot(mask, spread_ref[1])
    windows = []
    for at_x in range(shape.out_x):
        rows = slice(at_x * SLOTS, (at_x + 1) * SLOTS)
        windows.append(near[rows] * match_ref[0] + far[rows] * match_ref[1])
        level_ref[rows] = (
            dot(
                windows[-1].astype(BF16),
                padded_ref[4 * at_x * pitch : 4 * at_x * pitch + shape.window],
            )
            / 6.0
        ).astype(BF16)
    turned = jnp.concatenate(windows, axis=0).T
    node_x = lax.broadcasted_iota(jnp.int32, (tile_y, shape.nodes), 1) // SLOTS
    for at_x in range(shape.tile_x):
        quotient, rest = (at_x + REACH) // 4, (at_x + REACH) % 4
        cover = jnp.where(node_x == quotient, turned[rest * pitch : rest * pitch + tile_y], 0.0)
        if rest < 2:
            again = (rest + 4) * pitch
            cover = cover + jnp.where(
                node_x == quotient - 1, turned[again : again + tile_y], 0.0
            )
        cover = cover.astype(BF16)
        cover_ref[at_x * tile_y : (at_x + 1) * tile_y] = jnp.concatenate([cover, cover], axis=1)

    level_one = level_ref[...]
    pre_one = dot(level_one, w_one_ref[...])
    value, slope_one = silu_and_slope(pre_one)
    state_one = level_one.astype(F32) + value
    level_two = (0.25 * dot(quad_ref[...], two_halves(state_one))).astype(BF16)
    pre_two = dot(level_two, w_two_ref[...])
    two_bar = dot(quad_ref[:, : shape.nodes], cotangent.astype(BF16))
    pre_two_bar = (two_bar * silu_and_slope(pre_two)[1]).astype(BF16)
    pooled_bar = two_bar + dot_right_t(pre_two_bar, w_two_ref[...])
    one_bar = cotangent + 0.25 * pooled_bar
    pre_one_bar = (one_bar * slope_one).astype(BF16)
    level_bar = one_bar + dot_right_t(pre_one_bar, w_one_ref[...])

    node = lax.broadcasted_iota(jnp.int32, (shape.nodes, channels), 0)
    at_x, at_y = node // SLOTS, node % SLOTS
    owned = (at_x >= NODES_OUT) & (at_x < NODES_OUT + shape.node_x)
    owned = owned & (at_y >= NODES_OUT) & (at_y < NODES_OUT + shape.node_y)
    first = owned & (at_x % 2 == 0) & (at_y % 2 == 0)
    grads_ref[3 * channels : 4 * channels] = dot_left_t(
        level_one, jnp.where(owned, pre_one_bar.astype(F32), 0.0).astype(BF16)
    )
    grads_ref[4 * channels :] = dot_left_t(
        level_two, jnp.where(first, pre_two_bar.astype(F32), 0.0).astype(BF16)
    )

    both = two_halves(level_bar)
    for at, n in pieces(0, shape.cells, 128):
        rows = slice(at, at + n)
        message_bar = dot(cover_ref[rows], both) / 6.0
        pre_message_bar = (message_bar * slope_ref[rows]).astype(BF16)
        pmb_ref[rows] = pre_message_bar
        latent_bar = dot_right_t(pre_message_bar, w_message_ref[...])
        pre_embed_bar = (latent_bar * embed_ref[rows]).astype(BF16)
        peb_ref[rows] = pre_embed_bar
        state_ref[rows] = (latent_bar + dot_right_t(pre_embed_bar, w_embed_ref[...])).astype(BF16)
    own = slice(shape.halo, shape.halo + shape.cells)
    grads_ref[channels : 2 * channels] = dot_left_t(blended_ref[own], peb_ref[...])
    grads_ref[2 * channels : 3 * channels] = dot_left_t(latent_ref[...], pmb_ref[...])

    width = min(total_rows, LANES)
    cell = lax.broadcasted_iota(jnp.int32, (shape.cells, width), 0) + shape.halo
    grad_force = None
    for at in range(0, total_rows, width):
        rows = slice(at, at + width)
        hit = jnp.where(cell == key_ref[0:1, rows], 1.0, 0.0).astype(BF16)
        slot_bar = dot_left_t(hit, state_ref[...]).astype(BF16)
        back_ref[rows] = dot_right_t(slot_bar, w_force_ref[...]).astype(BF16)
        term = dot_left_t(rows_ref[rows], slot_bar)
        grad_force = term if grad_force is None else grad_force + term
    grads_ref[:channels] = grad_force

    half = sent_ref.shape[0]
    upper = narrow_ref[0] % 2
    kept_at = pl.multiple_of(upper * half, half)
    sent_at = pl.multiple_of((1 - upper) * half, half)
    sent_ref[...] = grads_ref[pl.ds(sent_at, half)].astype(BF16)
    kept_ref[...] = grads_ref[pl.ds(kept_at, half)]


def call(kernel, out_shapes, operands, scratch=(), spaces="", out_space=pltpu.VMEM, flops=0):
    kinds = {"s": pltpu.SMEM, "v": pltpu.VMEM}
    spaces = spaces + "v" * (len(operands) - len(spaces))
    moved = sum(math.prod(o.shape) * o.dtype.itemsize for o in list(operands) + list(out_shapes))
    return pl.pallas_call(
        kernel,
        out_shape=tuple(out_shapes),
        in_specs=[pl.BlockSpec(memory_space=kinds[space]) for space in spaces],
        out_specs=tuple(pl.BlockSpec(memory_space=out_space) for _ in out_shapes),
        scratch_shapes=list(scratch),
        compiler_params=pltpu.CompilerParams(vmem_limit_bytes=VMEM_LIMIT),
        cost_estimate=pl.CostEstimate(flops=flops, bytes_accessed=moved, transcendentals=0),
    )(*operands)


def meta_rows(live, target_x, target_y, tile_x, unit_rows, slot, units):
    high = target_x // tile_x
    low = target_x % tile_x
    column = jnp.where(live, target_y, LANES - 1)
    fields = jnp.stack([high, low, column]).astype(F32)
    if unit_rows * units <= LANES:
        before = slot * unit_rows
        after = LANES - before - unit_rows
        return jnp.pad(fields, ((0, 13), (before, after))).astype(BF16)
    blocks = unit_rows // LANES
    fields = fields.reshape(3, blocks, LANES).transpose(1, 0, 2)
    return jnp.pad(fields, ((0, 0), (0, 13), (0, 0))).reshape(16 * blocks, LANES).astype(BF16)


def local(
    grid_state,
    boundary_rows,
    row_count,
    target_x,
    target_y,
    g2m_mask,
    mesh_cotangent,
    w_force,
    w_embed,
    w_message,
    w_level_one,
    w_level_two,
):
    tile_x, tile_y, channels = grid_state.shape
    wide_count = lax.axis_size("wide")
    narrow_count = lax.axis_size("narrow")
    wide_at = lax.axis_index("wide")
    narrow_at = lax.axis_index("narrow")
    held_rows = boundary_rows.shape[0]
    shape = Shape(tile_x, tile_y)
    table = shape.tables()
    table = {
        name: jnp.asarray(value, F32 if name == "match" else BF16)
        for name, value in table.items()
    }

    live = jnp.arange(held_rows) < row_count[0]
    column = target_y - narrow_at * tile_y
    whole_column = wide_count == 4 and held_rows * wide_count <= LANES
    if whole_column:
        units = wide_count
        unit_rows = held_rows
        rows, row_live, row_x, row_y = boundary_rows, live, target_x, column
    else:
        slot_count = wide_count * CAP
        destination = target_x // tile_x
        matches = (destination[:, None] == jnp.arange(wide_count)[None, :]) & live[:, None]
        running = jnp.cumsum(matches.astype(jnp.int32), axis=0) - 1
        slot_index = jnp.sum(jnp.where(matches, running, 0), axis=1)
        send_slot = jnp.where(live, destination * CAP + slot_index, slot_count)
        cells = jnp.full((slot_count,), -1, jnp.int32)
        cells = cells.at[send_slot].set(target_x % tile_x * tile_y + column, mode="drop")
        outgoing = jnp.zeros((slot_count, channels), BF16)
        outgoing = outgoing.at[send_slot].set(boundary_rows, mode="drop")
        outgoing = outgoing.reshape(wide_count, CAP, channels)
        rows = lax.all_to_all(outgoing, "wide", split_axis=0, concat_axis=0, tiled=True)
        cells = lax.all_to_all(
            cells.reshape(wide_count, CAP), "wide", split_axis=0, concat_axis=0, tiled=True
        )
        rows = rows.reshape(slot_count, channels)
        cells = cells.reshape(slot_count)
        units = 3
        unit_rows = slot_count
        row_live = cells >= 0
        row_x = jnp.where(row_live, wide_at * tile_x + cells // tile_y, 0)
        row_y = cells % tile_y

    cells = grid_state.reshape(-1, channels)
    cotangent = mesh_cotangent.reshape(-1, channels)
    mask = g2m_mask.transpose(1, 2, 0).reshape(-1, 36)
    place = jnp.stack([wide_at, narrow_at])
    struct = jax.ShapeDtypeStruct
    long = struct((shape.halo + 2 * shape.edge + unit_rows + 16, channels), BF16)
    plain = struct((shape.halo + 2 * shape.edge, channels), BF16)
    short = struct((unit_rows + 16, channels), BF16)
    (place,) = call(
        open_kernel,
        [struct((2,), jnp.int32)],
        [place],
        spaces="s",
        out_space=pltpu.SMEM,
        flops=LONG,
    )
    if whole_column:
        first, second, third, fourth, mesh, own_rows = call(
            functools.partial(pack_kernel, shape, units),
            [long, plain, short, short, struct((2 * shape.own_nodes, channels), BF16), short],
            [
                place,
                cells,
                cotangent,
                mask,
                rows,
                target_x.reshape(1, -1),
                target_y.reshape(1, -1),
                row_count.reshape(1, 1),
            ],
            spaces="s",
            flops=LONG,
        )
        third = swapped(third, "wide", 2)
        fourth = swapped(fourth, "wide", 3)
        first_in = swapped(first, "wide", 1)
        arrived = [first_in, swapped_between(second, "wide"), third, fourth]
    else:

        def with_meta(slot):
            return [rows, meta_rows(row_live, row_x, row_y, tile_x, unit_rows, slot, units)]

        mask = jnp.pad(mask.astype(BF16), ((0, 0), (0, channels - 36)))
        mesh = jnp.concatenate([cotangent, mask])
        own_rows = jnp.concatenate(with_meta(0))
        edge = shape.edge
        to_prev = [cells[: shape.halo], cotangent[:edge], mask[:edge]]
        to_next = [cells[-shape.halo :], cotangent[-edge:], mask[-edge:]]
        to_prev, to_next = jnp.concatenate(to_prev), jnp.concatenate(to_next)
        upward = wide_at % 2 == 0
        first = jnp.concatenate([jnp.where(upward, to_next, to_prev)] + with_meta(1))
        second = jnp.concatenate([jnp.where(upward, to_prev, to_next)] + with_meta(2))
        arrived = [swapped(first, "wide", 1), swapped_between(second, "wide")]

    total_rows = unit_rows * units
    stack_rows = 4 * shape.edge + 2 * shape.own_nodes
    payload = struct((shape.side + 2 * shape.side_nodes, channels), BF16)
    blended, first, second, stack, all_rows, keys = call(
        functools.partial(blend_kernel, shape, units, unit_rows),
        [
            struct((shape.center, channels), BF16),
            payload,
            payload,
            struct((stack_rows, channels), BF16),
            struct((total_rows, channels), BF16),
            struct((8, total_rows), jnp.int32),
        ],
        [place, cells, mesh, w_force, table["to_side"], own_rows] + arrived,
        scratch=[pltpu.VMEM((total_rows, channels), BF16)],
        spaces="s",
        flops=2 * shape.center * total_rows * channels,
    )
    second = swapped_between(second, "narrow")
    first = swapped(first, "narrow", 1)
    message, latent, embed_slope, message_slope = call(
        functools.partial(forward_kernel, shape),
        [
            struct((shape.center, channels), BF16),
            struct((shape.cells, channels), BF16),
            struct((shape.cells, channels), F32),
            struct((shape.cells, channels), F32),
        ],
        [blended, w_embed, w_message],
        flops=4 * shape.center * channels * channels,
    )
    grad_rows_total = 5 * channels
    grad_state, back, sent, kept = call(
        functools.partial(backward_kernel, shape, total_rows),
        [
            struct((shape.cells, channels), BF16),
            struct((total_rows, channels), BF16),
            struct((grad_rows_total // 2, channels), BF16),
            struct((grad_rows_total // 2, channels), F32),
        ],
        [
            narrow_at.reshape(1),
            first,
            second,
            stack,
            blended,
            message,
            latent,
            embed_slope,
            message_slope,
            all_rows,
            keys,
            table["place"],
            table["spread"],
            table["match"],
            table["quad"],
            w_force,
            w_embed,
            w_message,
            w_level_one,
            w_level_two,
        ],
        scratch=[
            pltpu.VMEM((shape.rows_x * shape.pitch, channels), BF16),
            pltpu.VMEM((shape.nodes, channels), BF16),
            pltpu.VMEM((shape.cells, 2 * shape.nodes), BF16),
            pltpu.VMEM((shape.cells, channels), BF16),
            pltpu.VMEM((shape.cells, channels), BF16),
            pltpu.VMEM((grad_rows_total, channels), F32),
        ],
        spaces="s",
        flops=12 * shape.cells * channels * channels,
    )

    piece = kept + swapped(sent, "narrow", 1).astype(F32)
    back_blocks = back.reshape(units, unit_rows, channels)
    row_back = back_blocks[0].astype(F32)
    bits = [1 << k for k in range(1, narrow_count.bit_length() - 1)]
    for bit in bits:
        half = piece.shape[0] // 2
        upper = (narrow_at // bit) % 2
        sent = lax.dynamic_slice_in_dim(piece, (1 - upper) * half, half).astype(BF16)
        kept = lax.dynamic_slice_in_dim(piece, upper * half, half)
        piece = kept + swapped(sent, "narrow", bit).astype(F32)
    part = piece.shape[0] // wide_count
    rounded = piece.astype(BF16)
    own = lax.dynamic_slice_in_dim(piece, wide_at * part, part)
    order = sorted(range(1, wide_count), reverse=True)
    for k in order:
        sent = lax.dynamic_slice_in_dim(rounded, (wide_at ^ k) * part, part)
        if whole_column:
            sent = jnp.concatenate([sent, back_blocks[k]])
        got = swapped(sent, "wide", k).astype(F32)
        own = own + got[:part]
        if whole_column:
            row_back = row_back + got[part:]
    own = own.astype(BF16)
    gathered = jnp.zeros((wide_count * part, channels), BF16)
    gathered = lax.dynamic_update_slice_in_dim(gathered, own, wide_at * part, 0)
    for k in order:
        got = swapped(own, "wide", k)
        gathered = lax.dynamic_update_slice_in_dim(gathered, got, (wide_at ^ k) * part, 0)
    for bit in reversed(bits):
        upper = (narrow_at // bit) % 2
        other = swapped(gathered, "narrow", bit)
        gathered = jnp.where(
            upper == 0,
            jnp.concatenate([gathered, other]),
            jnp.concatenate([other, gathered]),
        )
    other = swapped(gathered, "narrow", 1)
    if whole_column:
        row_back = row_back.astype(BF16)
    else:
        returned = lax.all_to_all(
            back_blocks[0].reshape(wide_count, CAP, channels),
            "wide",
            split_axis=0,
            concat_axis=0,
            tiled=True,
        )
        row_back = jnp.take(
            returned.reshape(-1, channels), send_slot, axis=0, mode="fill", fill_value=0
        )
    cell_total = shape.cells * wide_count * narrow_count
    row_total = held_rows * wide_count * narrow_count
    sizes = [row_total, cell_total, cell_total, cell_total // 16, cell_total // 64]
    scales = np.array([1.0 / math.sqrt(size) for size in sizes], np.float32)
    totals = jnp.where(
        narrow_at % 2 == 0,
        jnp.concatenate([gathered, other]),
        jnp.concatenate([other, gathered]),
    )
    weight_grads = totals.reshape(5, channels, channels).astype(F32) * scales[:, None, None]
    return (grad_state.reshape(tile_x, tile_y, channels), row_back, weight_grads)


def solution(mesh):
    in_specs = (
        P(("groups", "wide"), "narrow", None),
        P(("groups", "wide", "narrow"), None),
        P(("groups", "wide", "narrow")),
        P(("groups", "wide", "narrow")),
        P(("groups", "wide", "narrow")),
        P(None, ("groups", "wide"), "narrow"),
        P(("groups", "wide"), "narrow", None),
        P(),
        P(),
        P(),
        P(),
        P(),
    )
    out_specs = (
        P(("groups", "wide"), "narrow", None),
        P(("groups", "wide", "narrow"), None),
        P("groups", None, None),
    )
    return jax.shard_map(local, mesh=mesh, in_specs=in_specs, out_specs=out_specs, check_vma=False)
```

```python
import functools
import math

import jax
import jax.numpy as jnp
import numpy as np
from jax import lax
from jax.experimental import pallas as pl
from jax.experimental.pallas import tpu as pltpu
from jax.sharding import PartitionSpec as P

CAP = 16
REACH = 1
BLOCK = 16
COLUMN = 32
LANES = 256
LONG = 10**10
VMEM_LIMIT = 48 * 1024 * 1024
F32 = jnp.float32
BF16 = jnp.bfloat16


def swapped(block, axis, bits):
    count = lax.axis_size(axis)
    return lax.ppermute(block, axis, [(i, i ^ bits) for i in range(count)])


def swapped_between(block, axis):
    count = lax.axis_size(axis)
    pairs = [(i, i + 1) for i in range(1, count - 1, 2)]
    return lax.ppermute(block, axis, pairs + [(j, i) for i, j in pairs])


def dot(left, right):
    return jnp.dot(left, right, preferred_element_type=F32)


def dot_right_t(left, right):
    return lax.dot_general(left, right, (((1,), (1,)), ((), ())), preferred_element_type=F32)


def dot_left_t(left, right):
    return lax.dot_general(left, right, (((0,), (0,)), ((), ())), preferred_element_type=F32)


def sigmoid(value):
    return 0.5 * jnp.tanh(0.5 * value) + 0.5


def silu_and_slope(value):
    logistic = sigmoid(value)
    return value * logistic, logistic * (1.0 + value * (1.0 - logistic))


def silu(value):
    return value * sigmoid(value)


def pieces(start, stop, size):
    return [(at, min(size, stop - at)) for at in range(start, stop, size)]


class Shape:
    def __init__(self, tile_x, tile_y):
        self.tile_x = tile_x
        self.tile_y = tile_y
        self.cells = tile_x * tile_y
        self.rows_x = tile_x + 2 * REACH
        self.halo = REACH * tile_y
        self.center = self.rows_x * tile_y
        self.node_x = tile_x // 4
        self.node_y = tile_y // 4
        self.nodes = self.node_x * self.node_y
        self.near_nodes = self.nodes + 2 * self.node_y
        self.all_nodes = self.near_nodes + 2 * 8

    def node_places(self, count):
        node = lax.broadcasted_iota(jnp.int32, (count, 1), 0)
        at_x, at_y = node // self.node_y, node % self.node_y
        lower = node >= self.nodes + self.node_y
        at_x = jnp.where(node < self.nodes, at_x, jnp.where(lower, self.node_x, -1))
        side = node - self.near_nodes
        at_x = jnp.where(side < 0, at_x, side % 8 - 1)
        at_y = jnp.where(side < 0, at_y, jnp.where(side < 8, -1, self.node_y))
        return at_x, at_y


def edge_matrix(mask, node_x, node_y, row, column):
    edges = None
    for down in range(2):
        for right in range(2):
            shift_x, shift_y = row % 4 + 4 * down, column % 4 + 4 * right
            code = jnp.where((shift_x < 6) & (shift_y < 6), shift_x * 6 + shift_y, -1)
            entry = lax.broadcasted_iota(jnp.int32, (128, row.shape[1]), 0)
            table = jnp.where(entry == code, 1.0, 0.0).astype(BF16)
            match = (node_x == row // 4 - down) & (node_y == column // 4 - right)
            term = jnp.where(match, dot(mask, table), 0.0)
            edges = term if edges is None else edges + term
    return edges


def both_parts(value):
    high = value.astype(BF16)
    return high, (value - high.astype(F32)).astype(BF16)


def open_kernel(place_ref, out_ref):
    out_ref[0] = place_ref[0]
    out_ref[1] = place_ref[1]


def pack_kernel(
    shape,
    units,
    place_ref,
    own_ref,
    mask_in_ref,
    rows_ref,
    target_x_ref,
    target_y_ref,
    count_ref,
    first_ref,
    second_ref,
    third_ref,
    fourth_ref,
    mask_ref,
    own_rows_ref,
):
    halo, node_y = shape.halo, shape.node_y
    held = rows_ref.shape[0]
    even = place_ref[0] % 2 == 0
    odd = jnp.logical_not(even)
    target_x = target_x_ref[...]
    column = target_y_ref[...] - place_ref[1] * shape.tile_y
    slot = lax.broadcasted_iota(jnp.int32, (1, held), 1)
    column = jnp.where(slot < count_ref[...], column, LANES - 1)
    line = lax.broadcasted_iota(jnp.int32, (16, held), 0)
    fields = jnp.where(line == 0, target_x // shape.tile_x, 0)
    fields = fields + jnp.where(line == 1, target_x % shape.tile_x, 0)
    fields = fields + jnp.where(line == 2, column, 0)
    lane = lax.broadcasted_iota(jnp.int32, (held, LANES), 1)
    repeat = lane % held == lax.broadcasted_iota(jnp.int32, (held, LANES), 0)
    spread = dot(fields.astype(F32).astype(BF16), jnp.where(repeat, 1.0, 0.0).astype(BF16))
    lane = lax.broadcasted_iota(jnp.int32, (16, LANES), 1)
    for number, ref in enumerate((own_rows_ref, first_ref, third_ref, fourth_ref)):
        at = ref.shape[0] - held - 16
        ref[at : at + held] = rows_ref[...]
        ref[at + held :] = jnp.where(lane // held == number, spread, 0.0).astype(BF16)

    mask = mask_in_ref[...].astype(F32)
    mask_ref[...] = jnp.zeros(mask_ref.shape, F32)
    mask_ref[:, : mask.shape[1]] = mask
    for ref, upward in ((first_ref, even), (second_ref, odd)):
        start = pl.multiple_of(jnp.where(upward, shape.cells - halo, 0), halo)
        ref[:halo] = own_ref[pl.ds(start, halo)]
        start = pl.multiple_of(jnp.where(upward, shape.nodes - node_y, 0), 8)
        chosen = mask_ref[pl.ds(start, node_y)]
        block = jnp.concatenate([chosen, jnp.zeros((BLOCK - node_y, LANES), F32)], axis=0)
        ref[halo : halo + BLOCK] = block.astype(BF16)


def blend_kernel(shape, units, unit_rows, *refs):
    (place_ref, own_ref, mask_ref, w_force_ref, own_rows_ref) = refs[:5]
    count = units if units > 3 else 2
    arrived = refs[5 : 5 + count]
    (blended_ref, first_ref, second_ref, masks_ref, rows_ref, key_ref) = refs[5 + count : 11 + count]
    (projected_ref,) = refs[11 + count :]
    wide_at = place_ref[0]
    even = wide_at % 2 == 0
    near, between = arrived[0], arrived[1]
    first_row = shape.halo + BLOCK

    def held(k, at, n):
        if k == 0:
            return own_rows_ref[at : at + n]
        if k == 1 or units == 3:
            return arrived[k - 1][first_row + at : first_row + at + n]
        return arrived[k][at : at + n]

    total = unit_rows * units
    for k in range(units):
        rows_ref[k * unit_rows : (k + 1) * unit_rows] = held(k, 0, unit_rows)
    blocks = []
    if total <= LANES:
        metas = [held(k, unit_rows, 16).astype(F32) for k in range(units)]
        blocks.append(functools.reduce(lambda a, b: a + b, metas)[:, :total])
    else:
        for k in range(units):
            for part in range(unit_rows // LANES):
                blocks.append(held(k, unit_rows + 16 * part, 16).astype(F32))
    keys = []
    for block in blocks:
        whole = block.astype(jnp.int32)
        at_x = whole[0:1] * shape.tile_x + whole[1:2] - wide_at * shape.tile_x + REACH
        at_y = whole[2:3]
        inside = (at_x >= 0) & (at_x < shape.rows_x) & (at_y < shape.tile_y)
        keys.append(jnp.where(inside, at_x * shape.tile_y + at_y, -1))
    width = keys[0].shape[1]
    for k, key in enumerate(keys):
        key_ref[:, k * width : (k + 1) * width] = jnp.broadcast_to(key, (8, width))
    projected_ref[...] = dot(rows_ref[...], w_force_ref[...]).astype(BF16)

    def facing(at, n, forward):
        one, other = near[at : at + n], between[at : at + n]
        return jnp.where(even, one, other) if forward else jnp.where(even, other, one)

    up = facing(shape.halo, BLOCK, False).astype(F32)[: shape.node_y]
    down = facing(shape.halo, BLOCK, True).astype(F32)[: shape.node_y]
    masks = jnp.concatenate([mask_ref[...], up, down], axis=0).astype(BF16)
    masks_ref[...] = masks

    tile_y = shape.tile_y
    inner = shape.halo + shape.cells
    jobs = [(0, at, n) for at, n in pieces(0, shape.halo, 3 * tile_y)]
    jobs += [(shape.halo, at, n) for at, n in pieces(0, shape.cells, 4 * tile_y)]
    jobs += [(inner, at, n) for at, n in pieces(0, shape.halo, 3 * tile_y)]
    for base, at, n in jobs:
        first = base + at
        if base == shape.halo:
            value = own_ref[at : at + n].astype(F32)
        else:
            value = facing(at, n, base == inner).astype(F32)
        cell = lax.broadcasted_iota(jnp.int32, (n, width), 0) + first
        for k, key in enumerate(keys):
            hit = jnp.where(cell == key, 1.0, 0.0).astype(BF16)
            value = value + dot(hit, projected_ref[k * width : (k + 1) * width])
        blended_ref[first : first + n] = value.astype(BF16)
    node = lax.broadcasted_iota(jnp.int32, (BLOCK, masks.shape[0]), 1)
    line = lax.broadcasted_iota(jnp.int32, (BLOCK, masks.shape[0]), 0)
    lower = node >= shape.nodes + shape.node_y
    node_x = jnp.where(
        node < shape.nodes, node // shape.node_y, jnp.where(lower, shape.node_x, -1)
    )
    cell = lax.broadcasted_iota(jnp.int32, (COLUMN, shape.center), 1)
    row = lax.broadcasted_iota(jnp.int32, (COLUMN, shape.center), 0)
    narrow_even = place_ref[1] % 2 == 0
    for ref, last in ((first_ref, narrow_even), (second_ref, jnp.logical_not(narrow_even))):
        column = jnp.where(last, tile_y - 1, 0)
        hit = jnp.where(cell == row * tile_y + column, 1.0, 0.0).astype(BF16)
        ref[:COLUMN] = dot(hit, blended_ref[...]).astype(BF16)
        node_y = jnp.where(last, shape.node_y - 1, 0)
        hit = (node_x == line - 1) & (node % shape.node_y == node_y)
        ref[COLUMN:] = dot(jnp.where(hit, 1.0, 0.0).astype(BF16), masks).astype(BF16)


def forward_kernel(
    shape,
    blended_ref,
    masks_ref,
    w_embed_ref,
    w_message_ref,
    message_ref,
    latent_ref,
    embed_ref,
    slope_ref,
    edges_ref,
):
    lane = lax.broadcasted_iota(jnp.int32, (1, shape.center + 2 * COLUMN), 1)
    side = lane - shape.center
    row = jnp.where(side < 0, lane // shape.tile_y, side % COLUMN)
    right = jnp.where(side < COLUMN, 0, shape.tile_y + 1)
    column = jnp.where(side < 0, lane % shape.tile_y + 1, right)
    node_x, node_y = shape.node_places(shape.nodes)
    mask = masks_ref[: shape.nodes, :128]
    edges_ref[...] = edge_matrix(mask, node_x, node_y, row, column).astype(BF16)
    inner = shape.halo + shape.cells
    jobs = pieces(0, shape.halo, 96) + pieces(shape.halo, inner, 128)
    jobs += pieces(inner, shape.center, 96)
    for at, n in jobs:
        blended = blended_ref[at : at + n]
        pre_embed = dot(blended, w_embed_ref[...])
        value, slope = silu_and_slope(pre_embed)
        latent = (blended.astype(F32) + value).astype(BF16)
        pre_message = dot(latent, w_message_ref[...])
        message, message_slope = silu_and_slope(pre_message)
        message_ref[at : at + n] = message.astype(BF16)
        if shape.halo <= at < inner:
            own = at - shape.halo
            latent_ref[own : own + n] = latent
            embed_ref[own : own + n] = slope
            slope_ref[own : own + n] = message_slope


def mesh_kernel(
    shape,
    place_ref,
    first_ref,
    second_ref,
    message_ref,
    edges_ref,
    cotangent_ref,
    w_embed_ref,
    w_message_ref,
    w_one_ref,
    w_two_ref,
    level_ref,
    to_near_ref,
    to_between_ref,
    one_ref,
    one_bar_ref,
    two_ref,
    two_bar_ref,
    messages_ref,
):
    even = place_ref[1] % 2 == 0
    center = shape.center
    first, second = first_ref[:COLUMN], second_ref[:COLUMN]
    left, right = jnp.where(even, second, first), jnp.where(even, first, second)
    blended = jnp.concatenate([left, right], axis=0)
    latent = (blended.astype(F32) + silu(dot(blended, w_embed_ref[...]))).astype(BF16)
    messages_ref[:center] = message_ref[...]
    messages_ref[center:] = silu(dot(latent, w_message_ref[...])).astype(BF16)
    level_one = (dot(edges_ref[...], messages_ref[...]) / 6.0).astype(BF16)

    nodes, node_y = shape.nodes, shape.node_y
    node = lax.broadcasted_iota(jnp.int32, (nodes, nodes), 0)
    other = lax.broadcasted_iota(jnp.int32, (nodes, nodes), 1)
    same = (node // (2 * node_y) == other // (2 * node_y)) & (
        node % node_y // 2 == other % node_y // 2
    )
    quad = jnp.where(same, 1.0, 0.0).astype(BF16)
    pre_one = dot(level_one, w_one_ref[...])
    value, slope_one = silu_and_slope(pre_one)
    high, low = both_parts(level_one.astype(F32) + value)
    level_two = (0.25 * (dot(quad, high) + dot(quad, low))).astype(BF16)
    pre_two = dot(level_two, w_two_ref[...])
    two_bar = dot(quad, cotangent_ref[...])
    pre_two_bar = (two_bar * silu_and_slope(pre_two)[1]).astype(BF16)
    pooled_bar = two_bar + dot_right_t(pre_two_bar, w_two_ref[...])
    one_bar = cotangent_ref[...].astype(F32) + 0.25 * pooled_bar
    pre_one_bar = (one_bar * slope_one).astype(BF16)
    level_ref[...] = one_bar + dot_right_t(pre_one_bar, w_one_ref[...])
    upward = place_ref[0] % 2 == 0
    for ref, last in ((to_near_ref, upward), (to_between_ref, jnp.logical_not(upward))):
        start = pl.multiple_of(jnp.where(last, nodes - node_y, 0), 8)
        value = level_ref[pl.ds(start, node_y)]
        high = value.astype(BF16).astype(F32)
        ref[...] = jnp.concatenate([high, value - high], axis=0).astype(BF16)
    node = lax.broadcasted_iota(jnp.int32, pre_two_bar.shape, 0)
    chosen = (node // node_y % 2 == 0) & (node % 2 == 0)
    one_ref[...] = level_one
    one_bar_ref[...] = pre_one_bar
    two_ref[...] = level_two
    two_bar_ref[...] = jnp.where(chosen, pre_two_bar.astype(F32), 0.0).astype(BF16)


def cover_kernel(
    shape,
    place_ref,
    first_ref,
    second_ref,
    masks_ref,
    one_ref,
    one_bar_ref,
    two_ref,
    two_bar_ref,
    cover_ref,
    grads_ref,
):
    even = place_ref[1] % 2 == 0
    first = first_ref[COLUMN:, :128].astype(F32)[:8]
    second = second_ref[COLUMN:, :128].astype(F32)[:8]
    left, right = jnp.where(even, second, first), jnp.where(even, first, second)
    masks = jnp.concatenate([masks_ref[:, :128].astype(F32), left, right], axis=0).astype(BF16)
    lane = lax.broadcasted_iota(jnp.int32, (1, shape.cells), 1)
    node_x, node_y = shape.node_places(shape.all_nodes)
    row, column = lane // shape.tile_y + 1, lane % shape.tile_y + 1
    edges = edge_matrix(masks, node_x, node_y, row, column)
    cover_ref[...] = jnp.concatenate([edges, edges], axis=0).T.astype(BF16)
    channels = grads_ref.shape[1]
    grads_ref[:channels] = dot_left_t(one_ref[...], one_bar_ref[...])
    grads_ref[channels:] = dot_left_t(two_ref[...], two_bar_ref[...])


def turn_kernel(
    shape, place_ref, level_ref, near_ref, between_ref, near_levels_ref, first_ref, second_ref
):
    even = place_ref[0] % 2 == 0
    node_y = shape.node_y
    near = near_ref[...].astype(F32)
    between = between_ref[...].astype(F32)
    near, between = near[:node_y] + near[node_y:], between[:node_y] + between[node_y:]
    levels = jnp.concatenate(
        [level_ref[...], jnp.where(even, between, near), jnp.where(even, near, between)], axis=0
    )
    near_levels_ref[...] = levels
    high, low = both_parts(levels)
    node = lax.broadcasted_iota(jnp.int32, (8, shape.near_nodes), 1)
    line = lax.broadcasted_iota(jnp.int32, (8, shape.near_nodes), 0)
    lower = node >= shape.nodes + node_y
    node_x = jnp.where(node < shape.nodes, node // node_y, jnp.where(lower, shape.node_x, -1))
    narrow_even = place_ref[1] % 2 == 0
    for ref, last in ((first_ref, narrow_even), (second_ref, jnp.logical_not(narrow_even))):
        column = jnp.where(last, node_y - 1, 0)
        hit = (node_x == line - 1) & (node % node_y == column)
        hit = jnp.where(hit, 1.0, 0.0).astype(BF16)
        ref[...] = jnp.concatenate([dot(hit, high), dot(hit, low)], axis=0).astype(BF16)


def backward_kernel(
    shape,
    total_rows,
    place_ref,
    levels_ref,
    first_ref,
    second_ref,
    cover_ref,
    mesh_grads_ref,
    blended_ref,
    latent_ref,
    embed_ref,
    slope_ref,
    rows_ref,
    key_ref,
    w_force_ref,
    w_embed_ref,
    w_message_ref,
    state_ref,
    back_ref,
    sent_ref,
    kept_ref,
    pmb_ref,
    peb_ref,
    grads_ref,
):
    channels = blended_ref.shape[1]
    even = place_ref[1] % 2 == 0
    first, second = first_ref[...].astype(F32), second_ref[...].astype(F32)
    first, second = first[:8] + first[8:], second[:8] + second[8:]
    left, right = jnp.where(even, second, first), jnp.where(even, first, second)
    high, low = both_parts(jnp.concatenate([levels_ref[...], left, right], axis=0))
    both = jnp.concatenate([high, low], axis=0)
    for at, n in pieces(0, shape.cells, 128):
        rows = slice(at, at + n)
        message_bar = dot(cover_ref[rows], both) / 6.0
        pre_message_bar = (message_bar * slope_ref[rows]).astype(BF16)
        pmb_ref[rows] = pre_message_bar
        latent_bar = dot_right_t(pre_message_bar, w_message_ref[...])
        pre_embed_bar = (latent_bar * embed_ref[rows]).astype(BF16)
        peb_ref[rows] = pre_embed_bar
        state_ref[rows] = (latent_bar + dot_right_t(pre_embed_bar, w_embed_ref[...])).astype(BF16)
    own = slice(shape.halo, shape.halo + shape.cells)
    grads_ref[channels : 2 * channels] = dot_left_t(blended_ref[own], peb_ref[...])
    grads_ref[2 * channels : 3 * channels] = dot_left_t(latent_ref[...], pmb_ref[...])
    grads_ref[3 * channels :] = mesh_grads_ref[...]

    width = min(total_rows, LANES)
    cell = lax.broadcasted_iota(jnp.int32, (shape.cells, width), 0) + shape.halo
    grad_force = None
    for at in range(0, total_rows, width):
        rows = slice(at, at + width)
        hit = jnp.where(cell == key_ref[0:1, rows], 1.0, 0.0).astype(BF16)
        slot_bar = dot_left_t(hit, state_ref[...]).astype(BF16)
        back_ref[rows] = dot_right_t(slot_bar, w_force_ref[...]).astype(BF16)
        term = dot_left_t(rows_ref[rows], slot_bar)
        grad_force = term if grad_force is None else grad_force + term
    grads_ref[:channels] = grad_force

    half = sent_ref.shape[0]
    upper = place_ref[1] % 2
    kept_at = pl.multiple_of(upper * half, half)
    sent_at = pl.multiple_of((1 - upper) * half, half)
    sent_ref[...] = grads_ref[pl.ds(sent_at, half)].astype(BF16)
    kept_ref[...] = grads_ref[pl.ds(kept_at, half)]


def call(kernel, out_shapes, operands, scratch=(), spaces="", out_space=pltpu.VMEM, flops=0):
    kinds = {"s": pltpu.SMEM, "v": pltpu.VMEM}
    spaces = spaces + "v" * (len(operands) - len(spaces))
    moved = sum(math.prod(o.shape) * o.dtype.itemsize for o in list(operands) + list(out_shapes))
    return pl.pallas_call(
        kernel,
        out_shape=tuple(out_shapes),
        in_specs=[pl.BlockSpec(memory_space=kinds[space]) for space in spaces],
        out_specs=tuple(pl.BlockSpec(memory_space=out_space) for _ in out_shapes),
        scratch_shapes=list(scratch),
        compiler_params=pltpu.CompilerParams(vmem_limit_bytes=VMEM_LIMIT),
        cost_estimate=pl.CostEstimate(flops=flops, bytes_accessed=moved, transcendentals=0),
    )(*operands)


def meta_rows(live, target_x, target_y, tile_x, unit_rows, slot, units):
    high = target_x // tile_x
    low = target_x % tile_x
    column = jnp.where(live, target_y, LANES - 1)
    fields = jnp.stack([high, low, column]).astype(F32)
    if unit_rows * units <= LANES:
        before = slot * unit_rows
        after = LANES - before - unit_rows
        return jnp.pad(fields, ((0, 13), (before, after))).astype(BF16)
    blocks = unit_rows // LANES
    fields = fields.reshape(3, blocks, LANES).transpose(1, 0, 2)
    return jnp.pad(fields, ((0, 0), (0, 13), (0, 0))).reshape(16 * blocks, LANES).astype(BF16)


def local(
    grid_state,
    boundary_rows,
    row_count,
    target_x,
    target_y,
    g2m_mask,
    mesh_cotangent,
    w_force,
    w_embed,
    w_message,
    w_level_one,
    w_level_two,
):
    tile_x, tile_y, channels = grid_state.shape
    wide_count = lax.axis_size("wide")
    narrow_count = lax.axis_size("narrow")
    wide_at = lax.axis_index("wide")
    narrow_at = lax.axis_index("narrow")
    held_rows = boundary_rows.shape[0]
    shape = Shape(tile_x, tile_y)
    live = jnp.arange(held_rows) < row_count[0]
    column = target_y - narrow_at * tile_y
    whole_column = wide_count == 4 and held_rows * wide_count <= LANES
    if whole_column:
        units = wide_count
        unit_rows = held_rows
        rows, row_live, row_x, row_y = boundary_rows, live, target_x, column
    else:
        slot_count = wide_count * CAP
        destination = target_x // tile_x
        matches = (destination[:, None] == jnp.arange(wide_count)[None, :]) & live[:, None]
        running = jnp.cumsum(matches.astype(jnp.int32), axis=0) - 1
        slot_index = jnp.sum(jnp.where(matches, running, 0), axis=1)
        send_slot = jnp.where(live, destination * CAP + slot_index, slot_count)
        cells = jnp.full((slot_count,), -1, jnp.int32)
        cells = cells.at[send_slot].set(target_x % tile_x * tile_y + column, mode="drop")
        outgoing = jnp.zeros((slot_count, channels), BF16)
        outgoing = outgoing.at[send_slot].set(boundary_rows, mode="drop")
        outgoing = outgoing.reshape(wide_count, CAP, channels)
        rows = lax.all_to_all(outgoing, "wide", split_axis=0, concat_axis=0, tiled=True)
        cells = lax.all_to_all(
            cells.reshape(wide_count, CAP), "wide", split_axis=0, concat_axis=0, tiled=True
        )
        rows = rows.reshape(slot_count, channels)
        cells = cells.reshape(slot_count)
        units = 3
        unit_rows = slot_count
        row_live = cells >= 0
        row_x = jnp.where(row_live, wide_at * tile_x + cells // tile_y, 0)
        row_y = cells % tile_y

    cells = grid_state.reshape(-1, channels)
    cotangent = mesh_cotangent.reshape(-1, channels)
    mask = g2m_mask.transpose(1, 2, 0).reshape(-1, 36)
    place = jnp.stack([wide_at, narrow_at])
    struct = jax.ShapeDtypeStruct
    long = struct((shape.halo + BLOCK + unit_rows + 16, channels), BF16)
    plain = struct((shape.halo + BLOCK, channels), BF16)
    short = struct((unit_rows + 16, channels), BF16)
    (place,) = call(
        open_kernel,
        [struct((2,), jnp.int32)],
        [place],
        spaces="s",
        out_space=pltpu.SMEM,
        flops=LONG,
    )
    if whole_column:
        first, second, third, fourth, mask, own_rows = call(
            functools.partial(pack_kernel, shape, units),
            [long, plain, short, short, struct((shape.nodes, channels), F32), short],
            [
                place,
                cells,
                mask,
                rows,
                target_x.reshape(1, -1),
                target_y.reshape(1, -1),
                row_count.reshape(1, 1),
            ],
            spaces="s",
            flops=LONG,
        )
        third = swapped(third, "wide", 2)
        fourth = swapped(fourth, "wide", 3)
        first_in = swapped(first, "wide", 1)
        arrived = [first_in, swapped_between(second, "wide"), third, fourth]
    else:

        def with_meta(slot):
            return [rows, meta_rows(row_live, row_x, row_y, tile_x, unit_rows, slot, units)]

        mask = jnp.pad(mask.astype(F32), ((0, 0), (0, channels - 36)))
        own_rows = jnp.concatenate(with_meta(0))
        line = shape.node_y
        blank = jnp.zeros((BLOCK - line, channels), BF16)
        to_prev = jnp.concatenate([cells[: shape.halo], mask[:line].astype(BF16), blank])
        to_next = jnp.concatenate([cells[-shape.halo :], mask[-line:].astype(BF16), blank])
        upward = wide_at % 2 == 0
        first = jnp.concatenate([jnp.where(upward, to_next, to_prev)] + with_meta(1))
        second = jnp.concatenate([jnp.where(upward, to_prev, to_next)] + with_meta(2))
        arrived = [swapped(first, "wide", 1), swapped_between(second, "wide")]

    total_rows = unit_rows * units
    payload = struct((COLUMN + BLOCK, channels), BF16)
    blended, first, second, masks, all_rows, keys = call(
        functools.partial(blend_kernel, shape, units, unit_rows),
        [
            struct((shape.center, channels), BF16),
            payload,
            payload,
            struct((shape.near_nodes, channels), BF16),
            struct((total_rows, channels), BF16),
            struct((8, total_rows), jnp.int32),
        ],
        [place, cells, mask, w_force, own_rows] + arrived,
        scratch=[pltpu.VMEM((total_rows, channels), BF16)],
        spaces="s",
        flops=2 * shape.center * total_rows * channels,
    )
    second = swapped_between(second, "narrow")
    first = swapped(first, "narrow", 1)
    message, latent, embed_slope, message_slope, edges = call(
        functools.partial(forward_kernel, shape),
        [
            struct((shape.center, channels), BF16),
            struct((shape.cells, channels), BF16),
            struct((shape.cells, channels), F32),
            struct((shape.cells, channels), F32),
            struct((shape.nodes, shape.center + 2 * COLUMN), BF16),
        ],
        [blended, masks, w_embed, w_message],
        flops=4 * shape.center * channels * channels,
    )
    nodes = struct((shape.nodes, channels), BF16)
    line = struct((2 * shape.node_y, channels), BF16)
    level, to_near, to_between, *mesh_terms = call(
        functools.partial(mesh_kernel, shape),
        [struct((shape.nodes, channels), F32), line, line, nodes, nodes, nodes, nodes],
        [
            place,
            first,
            second,
            message,
            edges,
            cotangent,
            w_embed,
            w_message,
            w_level_one,
            w_level_two,
        ],
        scratch=[pltpu.VMEM((shape.center + 2 * COLUMN, channels), BF16)],
        spaces="s",
        flops=2 * shape.center * channels * channels,
    )
    from_between = swapped_between(to_between, "wide")
    from_near = swapped(to_near, "wide", 1)
    cover, mesh_grads = call(
        functools.partial(cover_kernel, shape),
        [
            struct((shape.cells, 2 * shape.all_nodes), BF16),
            struct((2 * channels, channels), F32),
        ],
        [place, first, second, masks] + mesh_terms,
        spaces="s",
        flops=2 * shape.center * channels * channels,
    )
    side = struct((16, channels), BF16)
    levels, first, second = call(
        functools.partial(turn_kernel, shape),
        [struct((shape.near_nodes, channels), F32), side, side],
        [place, level, from_near, from_between],
        spaces="s",
    )
    second = swapped_between(second, "narrow")
    first = swapped(first, "narrow", 1)
    grad_rows_total = 5 * channels
    grad_state, back, sent, kept = call(
        functools.partial(backward_kernel, shape, total_rows),
        [
            struct((shape.cells, channels), BF16),
            struct((total_rows, channels), BF16),
            struct((grad_rows_total // 2, channels), BF16),
            struct((grad_rows_total // 2, channels), F32),
        ],
        [
            place,
            levels,
            first,
            second,
            cover,
            mesh_grads,
            blended,
            latent,
            embed_slope,
            message_slope,
            all_rows,
            keys,
            w_force,
            w_embed,
            w_message,
        ],
        scratch=[
            pltpu.VMEM((shape.cells, channels), BF16),
            pltpu.VMEM((shape.cells, channels), BF16),
            pltpu.VMEM((grad_rows_total, channels), F32),
        ],
        spaces="s",
        flops=12 * shape.cells * channels * channels,
    )

    piece = kept + swapped(sent, "narrow", 1).astype(F32)
    back_blocks = back.reshape(units, unit_rows, channels)
    row_back = back_blocks[0].astype(F32)
    bits = [1 << k for k in range(1, narrow_count.bit_length() - 1)]
    for bit in bits:
        half = piece.shape[0] // 2
        upper = (narrow_at // bit) % 2
        sent = lax.dynamic_slice_in_dim(piece, (1 - upper) * half, half).astype(BF16)
        kept = lax.dynamic_slice_in_dim(piece, upper * half, half)
        piece = kept + swapped(sent, "narrow", bit).astype(F32)
    part = piece.shape[0] // wide_count
    rounded = piece.astype(BF16)
    own = lax.dynamic_slice_in_dim(piece, wide_at * part, part)
    order = sorted(range(1, wide_count), reverse=True)
    for k in order:
        sent = lax.dynamic_slice_in_dim(rounded, (wide_at ^ k) * part, part)
        if whole_column:
            sent = jnp.concatenate([sent, back_blocks[k]])
        got = swapped(sent, "wide", k).astype(F32)
        own = own + got[:part]
        if whole_column:
            row_back = row_back + got[part:]
    own = own.astype(BF16)
    gathered = jnp.zeros((wide_count * part, channels), BF16)
    gathered = lax.dynamic_update_slice_in_dim(gathered, own, wide_at * part, 0)
    for k in order:
        got = swapped(own, "wide", k)
        gathered = lax.dynamic_update_slice_in_dim(gathered, got, (wide_at ^ k) * part, 0)
    for bit in reversed(bits):
        upper = (narrow_at // bit) % 2
        other = swapped(gathered, "narrow", bit)
        gathered = jnp.where(
            upper == 0,
            jnp.concatenate([gathered, other]),
            jnp.concatenate([other, gathered]),
        )
    other = swapped(gathered, "narrow", 1)
    if whole_column:
        row_back = row_back.astype(BF16)
    else:
        returned = lax.all_to_all(
            back_blocks[0].reshape(wide_count, CAP, channels),
            "wide",
            split_axis=0,
            concat_axis=0,
            tiled=True,
        )
        row_back = jnp.take(
            returned.reshape(-1, channels), send_slot, axis=0, mode="fill", fill_value=0
        )
    cell_total = shape.cells * wide_count * narrow_count
    row_total = held_rows * wide_count * narrow_count
    sizes = [row_total, cell_total, cell_total, cell_total // 16, cell_total // 64]
    scales = np.array([1.0 / math.sqrt(size) for size in sizes], np.float32)
    totals = jnp.where(
        narrow_at % 2 == 0,
        jnp.concatenate([gathered, other]),
        jnp.concatenate([other, gathered]),
    )
    weight_grads = totals.reshape(5, channels, channels).astype(F32) * scales[:, None, None]
    return (grad_state.reshape(tile_x, tile_y, channels), row_back, weight_grads)


def solution(mesh):
    in_specs = (
        P(("groups", "wide"), "narrow", None),
        P(("groups", "wide", "narrow"), None),
        P(("groups", "wide", "narrow")),
        P(("groups", "wide", "narrow")),
        P(("groups", "wide", "narrow")),
        P(None, ("groups", "wide"), "narrow"),
        P(("groups", "wide"), "narrow", None),
        P(),
        P(),
        P(),
        P(),
        P(),
    )
    out_specs = (
        P(("groups", "wide"), "narrow", None),
        P(("groups", "wide", "narrow"), None),
        P("groups", None, None),
    )
    return jax.shard_map(local, mesh=mesh, in_specs=in_specs, out_specs=out_specs, check_vma=False)
```

```python
import functools
import math

import jax
import jax.numpy as jnp
import numpy as np
from jax import lax
from jax.experimental import pallas as pl
from jax.experimental.pallas import tpu as pltpu
from jax.sharding import PartitionSpec as P

CAP = 16
REACH = 9
NODES_OUT = 2
SIDE = 16
SLOTS = 16
LANES = 256
LONG = 10**10
VMEM_LIMIT = 48 * 1024 * 1024
F32 = jnp.float32
BF16 = jnp.bfloat16


def swapped(block, axis, bits):
    count = lax.axis_size(axis)
    return lax.ppermute(block, axis, [(i, i ^ bits) for i in range(count)])


def swapped_between(block, axis):
    count = lax.axis_size(axis)
    pairs = [(i, i + 1) for i in range(1, count - 1, 2)]
    return lax.ppermute(block, axis, pairs + [(j, i) for i, j in pairs])


def dot(left, right):
    return jnp.dot(left, right, preferred_element_type=F32)


def dot_right_t(left, right):
    return lax.dot_general(left, right, (((1,), (1,)), ((), ())), preferred_element_type=F32)


def dot_left_t(left, right):
    return lax.dot_general(left, right, (((0,), (0,)), ((), ())), preferred_element_type=F32)


def sigmoid(value):
    return 0.5 * jnp.tanh(0.5 * value) + 0.5


def silu_and_slope(value):
    logistic = sigmoid(value)
    return value * logistic, logistic * (1.0 + value * (1.0 - logistic))


def silu(value):
    return value * sigmoid(value)


def pieces(start, stop, size):
    return [(at, min(size, stop - at)) for at in range(start, stop, size)]


def two_halves(value):
    high = value.astype(BF16)
    low = (value - high.astype(F32)).astype(BF16)
    return jnp.concatenate([high, low], axis=0)


class Shape:
    def __init__(self, tile_x, tile_y):
        self.tile_x = tile_x
        self.tile_y = tile_y
        self.cells = tile_x * tile_y
        self.rows_x = tile_x + 2 * REACH
        self.halo = REACH * tile_y
        self.center = self.rows_x * tile_y
        self.side = self.rows_x * SIDE
        self.pitch = tile_y + 2 * SIDE
        self.node_x = tile_x // 4
        self.node_y = tile_y // 4
        self.out_x = self.node_x + 2 * NODES_OUT
        self.nodes = self.out_x * SLOTS
        self.edge = NODES_OUT * self.node_y
        self.own_nodes = self.node_x * self.node_y
        self.window = 6 * self.pitch
        self.side_nodes = NODES_OUT * self.out_x

    def center_row(self, at_x, at_y, kind):
        edge, own = self.edge, self.own_nodes
        if at_x < NODES_OUT:
            return kind * edge + at_x * self.node_y + at_y
        at_x -= NODES_OUT
        if at_x < self.node_x:
            return 2 * edge + kind * own + at_x * self.node_y + at_y
        at_x -= self.node_x
        return 2 * edge + 2 * own + kind * edge + at_x * self.node_y + at_y

    def tables(self):
        stack = 4 * self.edge + 2 * self.own_nodes
        side = self.side_nodes
        to_left = np.zeros((2 * side, stack), np.float32)
        to_right = np.zeros((2 * side, stack), np.float32)
        for kind in range(2):
            for at_x in range(self.out_x):
                for k in range(NODES_OUT):
                    row = kind * side + at_x * NODES_OUT + k
                    to_left[row, self.center_row(at_x, k, kind)] = 1
                    last = self.node_y - NODES_OUT + k
                    to_right[row, self.center_row(at_x, last, kind)] = 1
        place = np.zeros((2, self.nodes, stack + 4 * side), np.float32)
        for kind in range(2):
            for at_x in range(self.out_x):
                for slot in range(self.node_y + 2 * NODES_OUT):
                    at_y = slot - NODES_OUT
                    if at_y < 0:
                        column = stack + kind * side + at_x * NODES_OUT + slot
                    elif at_y < self.node_y:
                        column = self.center_row(at_x, at_y, kind)
                    else:
                        k = at_y - self.node_y
                        column = stack + 2 * side + kind * side + at_x * NODES_OUT + k
                    place[kind, at_x * SLOTS + slot, column] = 1
        spread = np.zeros((2, 128, self.window), np.float32)
        match = np.zeros((2, SLOTS, self.window), np.float32)
        for dx in range(6):
            for at in range(self.pitch):
                if at < self.tile_y:
                    y = at
                elif at < self.tile_y + SIDE:
                    y = at - self.tile_y - SIDE
                else:
                    y = at - SIDE
                quotient, rest = (y + REACH) // 4, (y + REACH) % 4
                lane = dx * self.pitch + at
                spread[0, dx * 6 + rest, lane] = 1
                if 0 <= quotient < SLOTS:
                    match[0, quotient, lane] = 1
                if rest < 2:
                    spread[1, dx * 6 + rest + 4, lane] = 1
                    if 0 <= quotient - 1 < SLOTS:
                        match[1, quotient - 1, lane] = 1
        node = np.arange(self.nodes)
        quad = node // SLOTS // 2 * SLOTS + node % SLOTS // 2
        same = (quad[:, None] == quad[None, :]).astype(np.float32)
        return {
            "to_side": np.stack([to_left, to_right]),
            "place": place,
            "spread": spread,
            "match": match,
            "quad": np.concatenate([same, same], axis=1),
        }


def open_kernel(place_ref, out_ref):
    out_ref[0] = place_ref[0]
    out_ref[1] = place_ref[1]


def pack_kernel(
    shape,
    units,
    place_ref,
    own_ref,
    cotangent_ref,
    mask_ref,
    rows_ref,
    target_x_ref,
    target_y_ref,
    count_ref,
    first_ref,
    second_ref,
    third_ref,
    fourth_ref,
    mesh_ref,
    own_rows_ref,
):
    edge, own_nodes, halo = shape.edge, shape.own_nodes, shape.halo
    held = rows_ref.shape[0]
    even = place_ref[0] % 2 == 0
    odd = jnp.logical_not(even)
    target_x = target_x_ref[...]
    column = target_y_ref[...] - place_ref[1] * shape.tile_y
    slot = lax.broadcasted_iota(jnp.int32, (1, held), 1)
    column = jnp.where(slot < count_ref[...], column, LANES - 1)
    line = lax.broadcasted_iota(jnp.int32, (16, held), 0)
    fields = jnp.where(line == 0, target_x // shape.tile_x, 0)
    fields = fields + jnp.where(line == 1, target_x % shape.tile_x, 0)
    fields = fields + jnp.where(line == 2, column, 0)
    lane = lax.broadcasted_iota(jnp.int32, (held, LANES), 1)
    repeat = lane % held == lax.broadcasted_iota(jnp.int32, (held, LANES), 0)
    spread = dot(fields.astype(F32).astype(BF16), jnp.where(repeat, 1.0, 0.0).astype(BF16))
    lane = lax.broadcasted_iota(jnp.int32, (16, LANES), 1)
    for number, ref in enumerate((own_rows_ref, first_ref, third_ref, fourth_ref)):
        at = ref.shape[0] - held - 16
        ref[at : at + held] = rows_ref[...]
        ref[at + held :] = jnp.where(lane // held == number, spread, 0.0).astype(BF16)

    mesh_ref[:own_nodes] = cotangent_ref[...]
    mesh_ref[own_nodes:] = jnp.zeros((own_nodes, mesh_ref.shape[1]), BF16)
    mesh_ref[own_nodes:, : mask_ref.shape[1]] = mask_ref[...].astype(F32).astype(BF16)
    for ref, upward in ((first_ref, even), (second_ref, odd)):
        start = pl.multiple_of(jnp.where(upward, shape.cells - halo, 0), shape.tile_y)
        ref[:halo] = own_ref[pl.ds(start, halo)]
        start = pl.multiple_of(jnp.where(upward, own_nodes - edge, 0), 16)
        ref[halo : halo + edge] = mesh_ref[pl.ds(start, edge)]
        start = pl.multiple_of(jnp.where(upward, 2 * own_nodes - edge, own_nodes), 16)
        ref[halo + edge : halo + 2 * edge] = mesh_ref[pl.ds(start, edge)]


def blend_kernel(shape, units, unit_rows, *refs):
    (place_ref, own_ref, mesh_ref, w_force_ref, side_ref, own_rows_ref) = refs[:6]
    count = units if units > 3 else 2
    arrived = refs[6 : 6 + count]
    (blended_ref, first_ref, second_ref, stack_ref, rows_ref, key_ref) = refs[6 + count : 12 + count]
    (projected_ref,) = refs[12 + count :]
    wide_at = place_ref[0]
    even = wide_at % 2 == 0
    near, between = arrived[0], arrived[1]
    mesh = 2 * shape.edge
    first_row = shape.halo + mesh

    def held(k, at, n):
        if k == 0:
            return own_rows_ref[at : at + n]
        if k == 1 or units == 3:
            return arrived[k - 1][first_row + at : first_row + at + n]
        return arrived[k][at : at + n]

    total = unit_rows * units
    for k in range(units):
        rows_ref[k * unit_rows : (k + 1) * unit_rows] = held(k, 0, unit_rows)
    blocks = []
    if total <= LANES:
        metas = [held(k, unit_rows, 16).astype(F32) for k in range(units)]
        blocks.append(functools.reduce(lambda a, b: a + b, metas)[:, :total])
    else:
        for k in range(units):
            for part in range(unit_rows // LANES):
                blocks.append(held(k, unit_rows + 16 * part, 16).astype(F32))
    keys = []
    for block in blocks:
        whole = block.astype(jnp.int32)
        at_x = whole[0:1] * shape.tile_x + whole[1:2] - wide_at * shape.tile_x + REACH
        at_y = whole[2:3]
        inside = (at_x >= 0) & (at_x < shape.rows_x) & (at_y < shape.tile_y)
        keys.append(jnp.where(inside, at_x * shape.tile_y + at_y, -1))
    width = keys[0].shape[1]
    for k, key in enumerate(keys):
        key_ref[:, k * width : (k + 1) * width] = jnp.broadcast_to(key, (8, width))
    projected_ref[...] = dot(rows_ref[...], w_force_ref[...]).astype(BF16)

    def facing(at, n, forward):
        one, other = near[at : at + n], between[at : at + n]
        return jnp.where(even, one, other) if forward else jnp.where(even, other, one)

    stack = jnp.concatenate(
        [facing(shape.halo, mesh, False), mesh_ref[...], facing(shape.halo, mesh, True)], axis=0
    )
    stack_ref[...] = stack
    narrow_even = place_ref[1] % 2 == 0
    to_left = dot(side_ref[0], stack).astype(BF16)
    to_right = dot(side_ref[1], stack).astype(BF16)
    first_ref[shape.side :] = jnp.where(narrow_even, to_right, to_left)
    second_ref[shape.side :] = jnp.where(narrow_even, to_left, to_right)

    tile_y = shape.tile_y
    inner = shape.halo + shape.cells
    jobs = [(0, at, n) for at, n in pieces(0, shape.halo, 3 * tile_y)]
    jobs += [(shape.halo, at, n) for at, n in pieces(0, shape.cells, 4 * tile_y)]
    jobs += [(inner, at, n) for at, n in pieces(0, shape.halo, 3 * tile_y)]
    for base, at, n in jobs:
        first = base + at
        if base == shape.halo:
            value = own_ref[at : at + n].astype(F32)
        else:
            value = facing(at, n, base == inner).astype(F32)
        cell = lax.broadcasted_iota(jnp.int32, (n, width), 0) + first
        for k, key in enumerate(keys):
            hit = jnp.where(cell == key, 1.0, 0.0).astype(BF16)
            value = value + dot(hit, projected_ref[k * width : (k + 1) * width])
        value = value.astype(BF16)
        blended_ref[first : first + n] = value
        for t in range(n // tile_y):
            row = first // tile_y + t
            target = slice(row * SIDE, (row + 1) * SIDE)
            low = value[t * tile_y : t * tile_y + SIDE]
            high = value[(t + 1) * tile_y - SIDE : (t + 1) * tile_y]
            first_ref[target] = jnp.where(narrow_even, high, low)
            second_ref[target] = jnp.where(narrow_even, low, high)


def forward_kernel(
    shape, blended_ref, w_embed_ref, w_message_ref, message_ref, latent_ref, embed_ref, slope_ref
):
    inner = shape.halo + shape.cells
    jobs = pieces(0, shape.halo, 96) + pieces(shape.halo, inner, 128)
    jobs += pieces(inner, shape.center, 96)
    for at, n in jobs:
        blended = blended_ref[at : at + n]
        pre_embed = dot(blended, w_embed_ref[...])
        value, slope = silu_and_slope(pre_embed)
        latent = (blended.astype(F32) + value).astype(BF16)
        pre_message = dot(latent, w_message_ref[...])
        message, message_slope = silu_and_slope(pre_message)
        message_ref[at : at + n] = message.astype(BF16)
        if shape.halo <= at < inner:
            own = at - shape.halo
            latent_ref[own : own + n] = latent
            embed_ref[own : own + n] = slope
            slope_ref[own : own + n] = message_slope


def backward_kernel(shape, total_rows, *refs):
    (
        narrow_ref,
        second_ref,
        first_ref,
        stack_ref,
        blended_ref,
        message_ref,
        latent_ref,
        embed_ref,
        slope_ref,
        rows_ref,
        key_ref,
        place_ref,
        spread_ref,
        match_ref,
        quad_ref,
        w_force_ref,
        w_embed_ref,
        w_message_ref,
        w_one_ref,
        w_two_ref,
        state_ref,
        back_ref,
        sent_ref,
        kept_ref,
        padded_ref,
        level_ref,
        cover_ref,
        pmb_ref,
        peb_ref,
        grads_ref,
    ) = refs
    tile_y, pitch = shape.tile_y, shape.pitch
    channels = blended_ref.shape[1]

    even = narrow_ref[0] % 2 == 0
    first_at = pl.multiple_of(tile_y + jnp.where(even, SIDE, 0), SIDE)
    second_at = pl.multiple_of(tile_y + jnp.where(even, 0, SIDE), SIDE)
    for ref, offset in ((first_ref, first_at), (second_ref, second_at)):
        for at, n in pieces(0, shape.side, 8 * SIDE):
            blended = ref[at : at + n]
            latent = (blended.astype(F32) + silu(dot(blended, w_embed_ref[...]))).astype(BF16)
            message = silu(dot(latent, w_message_ref[...])).astype(BF16)
            for t in range(n // SIDE):
                row = (at // SIDE + t) * pitch + offset
                padded_ref[pl.ds(row, SIDE)] = message[t * SIDE : (t + 1) * SIDE]
    for row in range(shape.rows_x):
        padded_ref[row * pitch : row * pitch + tile_y] = message_ref[
            row * tile_y : (row + 1) * tile_y
        ]

    first, second = first_ref[shape.side :], second_ref[shape.side :]
    stack = jnp.concatenate(
        [stack_ref[...], jnp.where(even, second, first), jnp.where(even, first, second)], axis=0
    )
    cotangent = dot(place_ref[0], stack)
    mask = dot(place_ref[1], stack[:, :128]).astype(BF16)
    near = dot(mask, spread_ref[0])
    far = dot(mask, spread_ref[1])
    windows = []
    for at_x in range(shape.out_x):
        rows = slice(at_x * SLOTS, (at_x + 1) * SLOTS)
        windows.append(near[rows] * match_ref[0] + far[rows] * match_ref[1])
        level_ref[rows] = (
            dot(
                windows[-1].astype(BF16),
                padded_ref[4 * at_x * pitch : 4 * at_x * pitch + shape.window],
            )
            / 6.0
        ).astype(BF16)
    turned = jnp.concatenate(windows, axis=0).T
    node_x = lax.broadcasted_iota(jnp.int32, (tile_y, shape.nodes), 1) // SLOTS
    for at_x in range(shape.tile_x):
        quotient, rest = (at_x + REACH) // 4, (at_x + REACH) % 4
        cover = jnp.where(node_x == quotient, turned[rest * pitch : rest * pitch + tile_y], 0.0)
        if rest < 2:
            again = (rest + 4) * pitch
            cover = cover + jnp.where(
                node_x == quotient - 1, turned[again : again + tile_y], 0.0
            )
        cover = cover.astype(BF16)
        cover_ref[at_x * tile_y : (at_x + 1) * tile_y] = jnp.concatenate([cover, cover], axis=1)

    level_one = level_ref[...]
    pre_one = dot(level_one, w_one_ref[...])
    value, slope_one = silu_and_slope(pre_one)
    state_one = level_one.astype(F32) + value
    level_two = (0.25 * dot(quad_ref[...], two_halves(state_one))).astype(BF16)
    pre_two = dot(level_two, w_two_ref[...])
    two_bar = dot(quad_ref[:, : shape.nodes], cotangent.astype(BF16))
    pre_two_bar = (two_bar * silu_and_slope(pre_two)[1]).astype(BF16)
    pooled_bar = two_bar + dot_right_t(pre_two_bar, w_two_ref[...])
    one_bar = cotangent + 0.25 * pooled_bar
    pre_one_bar = (one_bar * slope_one).astype(BF16)
    level_bar = one_bar + dot_right_t(pre_one_bar, w_one_ref[...])

    node = lax.broadcasted_iota(jnp.int32, (shape.nodes, channels), 0)
    at_x, at_y = node // SLOTS, node % SLOTS
    owned = (at_x >= NODES_OUT) & (at_x < NODES_OUT + shape.node_x)
    owned = owned & (at_y >= NODES_OUT) & (at_y < NODES_OUT + shape.node_y)
    first = owned & (at_x % 2 == 0) & (at_y % 2 == 0)
    grads_ref[3 * channels : 4 * channels] = dot_left_t(
        level_one, jnp.where(owned, pre_one_bar.astype(F32), 0.0).astype(BF16)
    )
    grads_ref[4 * channels :] = dot_left_t(
        level_two, jnp.where(first, pre_two_bar.astype(F32), 0.0).astype(BF16)
    )

    both = two_halves(level_bar)
    for at, n in pieces(0, shape.cells, 128):
        rows = slice(at, at + n)
        message_bar = dot(cover_ref[rows], both) / 6.0
        pre_message_bar = (message_bar * slope_ref[rows]).astype(BF16)
        pmb_ref[rows] = pre_message_bar
        latent_bar = dot_right_t(pre_message_bar, w_message_ref[...])
        pre_embed_bar = (latent_bar * embed_ref[rows]).astype(BF16)
        peb_ref[rows] = pre_embed_bar
        state_ref[rows] = (latent_bar + dot_right_t(pre_embed_bar, w_embed_ref[...])).astype(BF16)
    own = slice(shape.halo, shape.halo + shape.cells)
    grads_ref[channels : 2 * channels] = dot_left_t(blended_ref[own], peb_ref[...])
    grads_ref[2 * channels : 3 * channels] = dot_left_t(latent_ref[...], pmb_ref[...])

    width = min(total_rows, LANES)
    cell = lax.broadcasted_iota(jnp.int32, (shape.cells, width), 0) + shape.halo
    grad_force = None
    for at in range(0, total_rows, width):
        rows = slice(at, at + width)
        hit = jnp.where(cell == key_ref[0:1, rows], 1.0, 0.0).astype(BF16)
        slot_bar = dot_left_t(hit, state_ref[...]).astype(BF16)
        back_ref[rows] = dot_right_t(slot_bar, w_force_ref[...]).astype(BF16)
        term = dot_left_t(rows_ref[rows], slot_bar)
        grad_force = term if grad_force is None else grad_force + term
    grads_ref[:channels] = grad_force

    half = sent_ref.shape[0]
    upper = narrow_ref[0] % 2
    kept_at = pl.multiple_of(upper * half, half)
    sent_at = pl.multiple_of((1 - upper) * half, half)
    sent_ref[...] = grads_ref[pl.ds(sent_at, half)].astype(BF16)
    kept_ref[...] = grads_ref[pl.ds(kept_at, half)]


def call(kernel, out_shapes, operands, scratch=(), spaces="", out_space=pltpu.VMEM, flops=0):
    kinds = {"s": pltpu.SMEM, "v": pltpu.VMEM}
    spaces = spaces + "v" * (len(operands) - len(spaces))
    moved = sum(math.prod(o.shape) * o.dtype.itemsize for o in list(operands) + list(out_shapes))
    return pl.pallas_call(
        kernel,
        out_shape=tuple(out_shapes),
        in_specs=[pl.BlockSpec(memory_space=kinds[space]) for space in spaces],
        out_specs=tuple(pl.BlockSpec(memory_space=out_space) for _ in out_shapes),
        scratch_shapes=list(scratch),
        compiler_params=pltpu.CompilerParams(vmem_limit_bytes=VMEM_LIMIT),
        cost_estimate=pl.CostEstimate(flops=flops, bytes_accessed=moved, transcendentals=0),
    )(*operands)


def meta_rows(live, target_x, target_y, tile_x, unit_rows, slot, units):
    high = target_x // tile_x
    low = target_x % tile_x
    column = jnp.where(live, target_y, LANES - 1)
    fields = jnp.stack([high, low, column]).astype(F32)
    if unit_rows * units <= LANES:
        before = slot * unit_rows
        after = LANES - before - unit_rows
        return jnp.pad(fields, ((0, 13), (before, after))).astype(BF16)
    blocks = unit_rows // LANES
    fields = fields.reshape(3, blocks, LANES).transpose(1, 0, 2)
    return jnp.pad(fields, ((0, 0), (0, 13), (0, 0))).reshape(16 * blocks, LANES).astype(BF16)


def local(
    grid_state,
    boundary_rows,
    row_count,
    target_x,
    target_y,
    g2m_mask,
    mesh_cotangent,
    w_force,
    w_embed,
    w_message,
    w_level_one,
    w_level_two,
):
    tile_x, tile_y, channels = grid_state.shape
    wide_count = lax.axis_size("wide")
    narrow_count = lax.axis_size("narrow")
    wide_at = lax.axis_index("wide")
    narrow_at = lax.axis_index("narrow")
    held_rows = boundary_rows.shape[0]
    shape = Shape(tile_x, tile_y)
    table = shape.tables()
    table = {
        name: jnp.asarray(value, F32 if name == "match" else BF16)
        for name, value in table.items()
    }

    live = jnp.arange(held_rows) < row_count[0]
    column = target_y - narrow_at * tile_y
    whole_column = wide_count == 4 and held_rows * wide_count <= LANES
    if whole_column:
        units = wide_count
        unit_rows = held_rows
        rows, row_live, row_x, row_y = boundary_rows, live, target_x, column
    else:
        slot_count = wide_count * CAP
        destination = target_x // tile_x
        matches = (destination[:, None] == jnp.arange(wide_count)[None, :]) & live[:, None]
        running = jnp.cumsum(matches.astype(jnp.int32), axis=0) - 1
        slot_index = jnp.sum(jnp.where(matches, running, 0), axis=1)
        send_slot = jnp.where(live, destination * CAP + slot_index, slot_count)
        cells = jnp.full((slot_count,), -1, jnp.int32)
        cells = cells.at[send_slot].set(target_x % tile_x * tile_y + column, mode="drop")
        outgoing = jnp.zeros((slot_count, channels), BF16)
        outgoing = outgoing.at[send_slot].set(boundary_rows, mode="drop")
        outgoing = outgoing.reshape(wide_count, CAP, channels)
        rows = lax.all_to_all(outgoing, "wide", split_axis=0, concat_axis=0, tiled=True)
        cells = lax.all_to_all(
            cells.reshape(wide_count, CAP), "wide", split_axis=0, concat_axis=0, tiled=True
        )
        rows = rows.reshape(slot_count, channels)
        cells = cells.reshape(slot_count)
        units = 3
        unit_rows = slot_count
        row_live = cells >= 0
        row_x = jnp.where(row_live, wide_at * tile_x + cells // tile_y, 0)
        row_y = cells % tile_y

    cells = grid_state.reshape(-1, channels)
    cotangent = mesh_cotangent.reshape(-1, channels)
    mask = g2m_mask.transpose(1, 2, 0).reshape(-1, 36)
    place = jnp.stack([wide_at, narrow_at])
    struct = jax.ShapeDtypeStruct
    long = struct((shape.halo + 2 * shape.edge + unit_rows + 16, channels), BF16)
    plain = struct((shape.halo + 2 * shape.edge, channels), BF16)
    short = struct((unit_rows + 16, channels), BF16)
    (place,) = call(
        open_kernel,
        [struct((2,), jnp.int32)],
        [place],
        spaces="s",
        out_space=pltpu.SMEM,
        flops=LONG,
    )
    if whole_column:
        first, second, third, fourth, mesh, own_rows = call(
            functools.partial(pack_kernel, shape, units),
            [long, plain, short, short, struct((2 * shape.own_nodes, channels), BF16), short],
            [
                place,
                cells,
                cotangent,
                mask,
                rows,
                target_x.reshape(1, -1),
                target_y.reshape(1, -1),
                row_count.reshape(1, 1),
            ],
            spaces="s",
            flops=LONG,
        )
        third = swapped(third, "wide", 2)
        fourth = swapped(fourth, "wide", 3)
        first_in = swapped(first, "wide", 1)
        arrived = [first_in, swapped_between(second, "wide"), third, fourth]
    else:

        def with_meta(slot):
            return [rows, meta_rows(row_live, row_x, row_y, tile_x, unit_rows, slot, units)]

        mask = jnp.pad(mask.astype(BF16), ((0, 0), (0, channels - 36)))
        mesh = jnp.concatenate([cotangent, mask])
        own_rows = jnp.concatenate(with_meta(0))
        edge = shape.edge
        to_prev = [cells[: shape.halo], cotangent[:edge], mask[:edge]]
        to_next = [cells[-shape.halo :], cotangent[-edge:], mask[-edge:]]
        to_prev, to_next = jnp.concatenate(to_prev), jnp.concatenate(to_next)
        upward = wide_at % 2 == 0
        first = jnp.concatenate([jnp.where(upward, to_next, to_prev)] + with_meta(1))
        second = jnp.concatenate([jnp.where(upward, to_prev, to_next)] + with_meta(2))
        arrived = [swapped(first, "wide", 1), swapped_between(second, "wide")]

    total_rows = unit_rows * units
    stack_rows = 4 * shape.edge + 2 * shape.own_nodes
    payload = struct((shape.side + 2 * shape.side_nodes, channels), BF16)
    blended, first, second, stack, all_rows, keys = call(
        functools.partial(blend_kernel, shape, units, unit_rows),
        [
            struct((shape.center, channels), BF16),
            payload,
            payload,
            struct((stack_rows, channels), BF16),
            struct((total_rows, channels), BF16),
            struct((8, total_rows), jnp.int32),
        ],
        [place, cells, mesh, w_force, table["to_side"], own_rows] + arrived,
        scratch=[pltpu.VMEM((total_rows, channels), BF16)],
        spaces="s",
        flops=2 * shape.center * total_rows * channels,
    )
    second = swapped_between(second, "narrow")
    first = swapped(first, "narrow", 1)
    message, latent, embed_slope, message_slope = call(
        functools.partial(forward_kernel, shape),
        [
            struct((shape.center, channels), BF16),
            struct((shape.cells, channels), BF16),
            struct((shape.cells, channels), F32),
            struct((shape.cells, channels), F32),
        ],
        [blended, w_embed, w_message],
        flops=4 * shape.center * channels * channels,
    )
    grad_rows_total = 5 * channels
    grad_state, back, sent, kept = call(
        functools.partial(backward_kernel, shape, total_rows),
        [
            struct((shape.cells, channels), BF16),
            struct((total_rows, channels), BF16),
            struct((grad_rows_total // 2, channels), BF16),
            struct((grad_rows_total // 2, channels), F32),
        ],
        [
            narrow_at.reshape(1),
            second,
            first,
            stack,
            blended,
            message,
            latent,
            embed_slope,
            message_slope,
            all_rows,
            keys,
            table["place"],
            table["spread"],
            table["match"],
            table["quad"],
            w_force,
            w_embed,
            w_message,
            w_level_one,
            w_level_two,
        ],
        scratch=[
            pltpu.VMEM((shape.rows_x * shape.pitch, channels), BF16),
            pltpu.VMEM((shape.nodes, channels), BF16),
            pltpu.VMEM((shape.cells, 2 * shape.nodes), BF16),
            pltpu.VMEM((shape.cells, channels), BF16),
            pltpu.VMEM((shape.cells, channels), BF16),
            pltpu.VMEM((grad_rows_total, channels), F32),
        ],
        spaces="s",
        flops=12 * shape.cells * channels * channels,
    )

    piece = kept + swapped(sent, "narrow", 1).astype(F32)
    back_blocks = back.reshape(units, unit_rows, channels)
    row_back = back_blocks[0].astype(F32)
    bits = [1 << k for k in range(1, narrow_count.bit_length() - 1)]
    for bit in bits:
        half = piece.shape[0] // 2
        upper = (narrow_at // bit) % 2
        sent = lax.dynamic_slice_in_dim(piece, (1 - upper) * half, half).astype(BF16)
        kept = lax.dynamic_slice_in_dim(piece, upper * half, half)
        piece = kept + swapped(sent, "narrow", bit).astype(F32)
    part = piece.shape[0] // wide_count
    rounded = piece.astype(BF16)
    own = lax.dynamic_slice_in_dim(piece, wide_at * part, part)
    order = sorted(range(1, wide_count), reverse=True)
    for k in order:
        sent = lax.dynamic_slice_in_dim(rounded, (wide_at ^ k) * part, part)
        if whole_column:
            sent = jnp.concatenate([sent, back_blocks[k]])
        got = swapped(sent, "wide", k).astype(F32)
        own = own + got[:part]
        if whole_column:
            row_back = row_back + got[part:]
    own = own.astype(BF16)
    gathered = jnp.zeros((wide_count * part, channels), BF16)
    gathered = lax.dynamic_update_slice_in_dim(gathered, own, wide_at * part, 0)
    for k in order:
        got = swapped(own, "wide", k)
        gathered = lax.dynamic_update_slice_in_dim(gathered, got, (wide_at ^ k) * part, 0)
    for bit in reversed(bits):
        upper = (narrow_at // bit) % 2
        other = swapped(gathered, "narrow", bit)
        gathered = jnp.where(
            upper == 0,
            jnp.concatenate([gathered, other]),
            jnp.concatenate([other, gathered]),
        )
    other = swapped(gathered, "narrow", 1)
    if whole_column:
        row_back = row_back.astype(BF16)
    else:
        returned = lax.all_to_all(
            back_blocks[0].reshape(wide_count, CAP, channels),
            "wide",
            split_axis=0,
            concat_axis=0,
            tiled=True,
        )
        row_back = jnp.take(
            returned.reshape(-1, channels), send_slot, axis=0, mode="fill", fill_value=0
        )
    cell_total = shape.cells * wide_count * narrow_count
    row_total = held_rows * wide_count * narrow_count
    sizes = [row_total, cell_total, cell_total, cell_total // 16, cell_total // 64]
    scales = np.array([1.0 / math.sqrt(size) for size in sizes], np.float32)
    totals = jnp.where(
        narrow_at % 2 == 0,
        jnp.concatenate([gathered, other]),
        jnp.concatenate([other, gathered]),
    )
    weight_grads = totals.reshape(5, channels, channels).astype(F32) * scales[:, None, None]
    return (grad_state.reshape(tile_x, tile_y, channels), row_back, weight_grads)


def solution(mesh):
    in_specs = (
        P(("groups", "wide"), "narrow", None),
        P(("groups", "wide", "narrow"), None),
        P(("groups", "wide", "narrow")),
        P(("groups", "wide", "narrow")),
        P(("groups", "wide", "narrow")),
        P(None, ("groups", "wide"), "narrow"),
        P(("groups", "wide"), "narrow", None),
        P(),
        P(),
        P(),
        P(),
        P(),
    )
    out_specs = (
        P(("groups", "wide"), "narrow", None),
        P(("groups", "wide", "narrow"), None),
        P("groups", None, None),
    )
    return jax.shard_map(local, mesh=mesh, in_specs=in_specs, out_specs=out_specs, check_vma=False)
```

```python
import functools
import math

import jax
import jax.numpy as jnp
import numpy as np
from jax import lax
from jax.experimental import pallas as pl
from jax.experimental.pallas import tpu as pltpu
from jax.sharding import PartitionSpec as P

CAP = 16
REACH = 9
NODES_OUT = 2
SIDE = 16
SLOTS = 16
LANES = 256
LONG = 10**10
VMEM_LIMIT = 48 * 1024 * 1024
F32 = jnp.float32
BF16 = jnp.bfloat16


def swapped(block, axis, bits):
    count = lax.axis_size(axis)
    return lax.ppermute(block, axis, [(i, i ^ bits) for i in range(count)])


def swapped_between(block, axis):
    count = lax.axis_size(axis)
    pairs = [(i, i + 1) for i in range(1, count - 1, 2)]
    return lax.ppermute(block, axis, pairs + [(j, i) for i, j in pairs])


def dot(left, right):
    return jnp.dot(left, right, preferred_element_type=F32)


def dot_right_t(left, right):
    return lax.dot_general(left, right, (((1,), (1,)), ((), ())), preferred_element_type=F32)


def dot_left_t(left, right):
    return lax.dot_general(left, right, (((0,), (0,)), ((), ())), preferred_element_type=F32)


def sigmoid(value):
    return 0.5 * jnp.tanh(0.5 * value) + 0.5


def silu_and_slope(value):
    logistic = sigmoid(value)
    return value * logistic, logistic * (1.0 + value * (1.0 - logistic))


def silu(value):
    return value * sigmoid(value)


def pieces(start, stop, size):
    return [(at, min(size, stop - at)) for at in range(start, stop, size)]


def two_halves(value):
    high = value.astype(BF16)
    low = (value - high.astype(F32)).astype(BF16)
    return jnp.concatenate([high, low], axis=0)


class Shape:
    def __init__(self, tile_x, tile_y):
        self.tile_x = tile_x
        self.tile_y = tile_y
        self.cells = tile_x * tile_y
        self.rows_x = tile_x + 2 * REACH
        self.halo = REACH * tile_y
        self.center = self.rows_x * tile_y
        self.side = self.rows_x * SIDE
        self.pitch = tile_y + 2 * SIDE
        self.node_x = tile_x // 4
        self.node_y = tile_y // 4
        self.out_x = self.node_x + 2 * NODES_OUT
        self.nodes = self.out_x * SLOTS
        self.edge = NODES_OUT * self.node_y
        self.own_nodes = self.node_x * self.node_y
        self.window = 6 * self.pitch
        self.side_nodes = NODES_OUT * self.out_x

    def center_row(self, at_x, at_y, kind):
        edge, own = self.edge, self.own_nodes
        if at_x < NODES_OUT:
            return kind * edge + at_x * self.node_y + at_y
        at_x -= NODES_OUT
        if at_x < self.node_x:
            return 2 * edge + kind * own + at_x * self.node_y + at_y
        at_x -= self.node_x
        return 2 * edge + 2 * own + kind * edge + at_x * self.node_y + at_y

    def tables(self):
        stack = 4 * self.edge + 2 * self.own_nodes
        side = self.side_nodes
        to_left = np.zeros((2 * side, stack), np.float32)
        to_right = np.zeros((2 * side, stack), np.float32)
        for kind in range(2):
            for at_x in range(self.out_x):
                for k in range(NODES_OUT):
                    row = kind * side + at_x * NODES_OUT + k
                    to_left[row, self.center_row(at_x, k, kind)] = 1
                    last = self.node_y - NODES_OUT + k
                    to_right[row, self.center_row(at_x, last, kind)] = 1
        place = np.zeros((2, self.nodes, stack + 4 * side), np.float32)
        for kind in range(2):
            for at_x in range(self.out_x):
                for slot in range(self.node_y + 2 * NODES_OUT):
                    at_y = slot - NODES_OUT
                    if at_y < 0:
                        column = stack + kind * side + at_x * NODES_OUT + slot
                    elif at_y < self.node_y:
                        column = self.center_row(at_x, at_y, kind)
                    else:
                        k = at_y - self.node_y
                        column = stack + 2 * side + kind * side + at_x * NODES_OUT + k
                    place[kind, at_x * SLOTS + slot, column] = 1
        spread = np.zeros((2, 128, self.window), np.float32)
        match = np.zeros((2, SLOTS, self.window), np.float32)
        for dx in range(6):
            for at in range(self.pitch):
                if at < self.tile_y:
                    y = at
                elif at < self.tile_y + SIDE:
                    y = at - self.tile_y - SIDE
                else:
                    y = at - SIDE
                quotient, rest = (y + REACH) // 4, (y + REACH) % 4
                lane = dx * self.pitch + at
                spread[0, dx * 6 + rest, lane] = 1
                if 0 <= quotient < SLOTS:
                    match[0, quotient, lane] = 1
                if rest < 2:
                    spread[1, dx * 6 + rest + 4, lane] = 1
                    if 0 <= quotient - 1 < SLOTS:
                        match[1, quotient - 1, lane] = 1
        node = np.arange(self.nodes)
        quad = node // SLOTS // 2 * SLOTS + node % SLOTS // 2
        same = (quad[:, None] == quad[None, :]).astype(np.float32)
        return {
            "to_side": np.stack([to_left, to_right]),
            "place": place,
            "spread": spread,
            "match": match,
            "quad": np.concatenate([same, same], axis=1),
        }


def open_kernel(place_ref, out_ref):
    out_ref[0] = place_ref[0]
    out_ref[1] = place_ref[1]


def pack_kernel(
    shape,
    units,
    place_ref,
    own_ref,
    cotangent_ref,
    mask_ref,
    rows_ref,
    target_x_ref,
    target_y_ref,
    count_ref,
    first_ref,
    second_ref,
    third_ref,
    mesh_ref,
    own_rows_ref,
):
    edge, own_nodes, halo = shape.edge, shape.own_nodes, shape.halo
    held = rows_ref.shape[0]
    even = place_ref[0] % 2 == 0
    odd = jnp.logical_not(even)
    target_x = target_x_ref[...]
    column = target_y_ref[...] - place_ref[1] * shape.tile_y
    slot = lax.broadcasted_iota(jnp.int32, (1, held), 1)
    column = jnp.where(slot < count_ref[...], column, LANES - 1)
    line = lax.broadcasted_iota(jnp.int32, (16, held), 0)
    fields = jnp.where(line == 0, target_x // shape.tile_x, 0)
    fields = fields + jnp.where(line == 1, target_x % shape.tile_x, 0)
    fields = fields + jnp.where(line == 2, column, 0)
    lane = lax.broadcasted_iota(jnp.int32, (held, LANES), 1)
    repeat = lane % held == lax.broadcasted_iota(jnp.int32, (held, LANES), 0)
    spread = dot(fields.astype(F32).astype(BF16), jnp.where(repeat, 1.0, 0.0).astype(BF16))
    lane = lax.broadcasted_iota(jnp.int32, (16, LANES), 1)
    for number, ref in enumerate((own_rows_ref, first_ref, third_ref)):
        at = ref.shape[0] - held - 16
        ref[at : at + held] = rows_ref[...]
        ref[at + held :] = jnp.where(lane // held == number, spread, 0.0).astype(BF16)

    mesh_ref[:own_nodes] = cotangent_ref[...]
    mesh_ref[own_nodes:] = jnp.zeros((own_nodes, mesh_ref.shape[1]), BF16)
    mesh_ref[own_nodes:, : mask_ref.shape[1]] = mask_ref[...].astype(F32).astype(BF16)
    for ref, upward in ((first_ref, even), (second_ref, odd)):
        start = pl.multiple_of(jnp.where(upward, shape.cells - halo, 0), shape.tile_y)
        ref[:halo] = own_ref[pl.ds(start, halo)]
        start = pl.multiple_of(jnp.where(upward, own_nodes - edge, 0), 16)
        ref[halo : halo + edge] = mesh_ref[pl.ds(start, edge)]
        start = pl.multiple_of(jnp.where(upward, 2 * own_nodes - edge, own_nodes), 16)
        ref[halo + edge : halo + 2 * edge] = mesh_ref[pl.ds(start, edge)]


def blend_kernel(shape, units, unit_rows, *refs):
    (place_ref, own_ref, mesh_ref, w_force_ref, side_ref, own_rows_ref) = refs[:6]
    count = units - 1
    arrived = refs[6 : 6 + count]
    (blended_ref, first_ref, second_ref, stack_ref, rows_ref, key_ref) = refs[6 + count : 12 + count]
    (projected_ref,) = refs[12 + count :]
    wide_at = place_ref[0]
    even = wide_at % 2 == 0
    near, between = arrived[0], arrived[1]
    mesh = 2 * shape.edge
    first_row = shape.halo + mesh

    def held(k, at, n):
        if k == 0:
            return own_rows_ref[at : at + n]
        if k == 1 or units == 3:
            return arrived[k - 1][first_row + at : first_row + at + n]
        start = (k - 2) * (unit_rows + 16) + at
        return arrived[2][start : start + n]

    total = unit_rows * units
    for k in range(units):
        rows_ref[k * unit_rows : (k + 1) * unit_rows] = held(k, 0, unit_rows)
    blocks = []
    if total <= LANES:
        metas = [held(k, unit_rows, 16).astype(F32) for k in range(units)]
        if units > 3:
            metas[3] = pltpu.roll(metas[3], 2 * unit_rows, axis=1)
        blocks.append(functools.reduce(lambda a, b: a + b, metas)[:, :total])
    else:
        for k in range(units):
            for part in range(unit_rows // LANES):
                blocks.append(held(k, unit_rows + 16 * part, 16).astype(F32))
    keys = []
    for block in blocks:
        whole = block.astype(jnp.int32)
        at_x = whole[0:1] * shape.tile_x + whole[1:2] - wide_at * shape.tile_x + REACH
        at_y = whole[2:3]
        inside = (at_x >= 0) & (at_x < shape.rows_x) & (at_y < shape.tile_y)
        keys.append(jnp.where(inside, at_x * shape.tile_y + at_y, -1))
    width = keys[0].shape[1]
    for k, key in enumerate(keys):
        key_ref[:, k * width : (k + 1) * width] = jnp.broadcast_to(key, (8, width))
    projected_ref[...] = dot(rows_ref[...], w_force_ref[...]).astype(BF16)

    def facing(at, n, forward):
        one, other = near[at : at + n], between[at : at + n]
        return jnp.where(even, one, other) if forward else jnp.where(even, other, one)

    stack = jnp.concatenate(
        [facing(shape.halo, mesh, False), mesh_ref[...], facing(shape.halo, mesh, True)], axis=0
    )
    stack_ref[...] = stack
    narrow_even = place_ref[1] % 2 == 0
    to_left = dot(side_ref[0], stack).astype(BF16)
    to_right = dot(side_ref[1], stack).astype(BF16)
    first_ref[shape.side :] = jnp.where(narrow_even, to_right, to_left)
    second_ref[shape.side :] = jnp.where(narrow_even, to_left, to_right)

    tile_y = shape.tile_y
    inner = shape.halo + shape.cells
    jobs = [(0, at, n) for at, n in pieces(0, shape.halo, 3 * tile_y)]
    jobs += [(shape.halo, at, n) for at, n in pieces(0, shape.cells, 4 * tile_y)]
    jobs += [(inner, at, n) for at, n in pieces(0, shape.halo, 3 * tile_y)]
    for base, at, n in jobs:
        first = base + at
        if base == shape.halo:
            value = own_ref[at : at + n].astype(F32)
        else:
            value = facing(at, n, base == inner).astype(F32)
        cell = lax.broadcasted_iota(jnp.int32, (n, width), 0) + first
        for k, key in enumerate(keys):
            hit = jnp.where(cell == key, 1.0, 0.0).astype(BF16)
            value = value + dot(hit, projected_ref[k * width : (k + 1) * width])
        value = value.astype(BF16)
        blended_ref[first : first + n] = value
        for t in range(n // tile_y):
            row = first // tile_y + t
            target = slice(row * SIDE, (row + 1) * SIDE)
            low = value[t * tile_y : t * tile_y + SIDE]
            high = value[(t + 1) * tile_y - SIDE : (t + 1) * tile_y]
            first_ref[target] = jnp.where(narrow_even, high, low)
            second_ref[target] = jnp.where(narrow_even, low, high)


def forward_kernel(
    shape, blended_ref, w_embed_ref, w_message_ref, message_ref, latent_ref, embed_ref, slope_ref
):
    inner = shape.halo + shape.cells
    jobs = pieces(0, shape.halo, 96) + pieces(shape.halo, inner, 128)
    jobs += pieces(inner, shape.center, 96)
    for at, n in jobs:
        blended = blended_ref[at : at + n]
        pre_embed = dot(blended, w_embed_ref[...])
        value, slope = silu_and_slope(pre_embed)
        latent = (blended.astype(F32) + value).astype(BF16)
        pre_message = dot(latent, w_message_ref[...])
        message, message_slope = silu_and_slope(pre_message)
        message_ref[at : at + n] = message.astype(BF16)
        if shape.halo <= at < inner:
            own = at - shape.halo
            latent_ref[own : own + n] = latent
            embed_ref[own : own + n] = slope
            slope_ref[own : own + n] = message_slope


def backward_kernel(shape, total_rows, *refs):
    (
        narrow_ref,
        second_ref,
        first_ref,
        stack_ref,
        blended_ref,
        message_ref,
        latent_ref,
        embed_ref,
        slope_ref,
        rows_ref,
        key_ref,
        place_ref,
        spread_ref,
        match_ref,
        quad_ref,
        w_force_ref,
        w_embed_ref,
        w_message_ref,
        w_one_ref,
        w_two_ref,
        state_ref,
        back_ref,
        sent_ref,
        kept_ref,
        padded_ref,
        level_ref,
        cover_ref,
        pmb_ref,
        peb_ref,
        grads_ref,
    ) = refs
    tile_y, pitch = shape.tile_y, shape.pitch
    channels = blended_ref.shape[1]

    even = narrow_ref[0] % 2 == 0
    first_at = pl.multiple_of(tile_y + jnp.where(even, SIDE, 0), SIDE)
    second_at = pl.multiple_of(tile_y + jnp.where(even, 0, SIDE), SIDE)
    for ref, offset in ((first_ref, first_at), (second_ref, second_at)):
        for at, n in pieces(0, shape.side, 8 * SIDE):
            blended = ref[at : at + n]
            latent = (blended.astype(F32) + silu(dot(blended, w_embed_ref[...]))).astype(BF16)
            message = silu(dot(latent, w_message_ref[...])).astype(BF16)
            for t in range(n // SIDE):
                row = (at // SIDE + t) * pitch + offset
                padded_ref[pl.ds(row, SIDE)] = message[t * SIDE : (t + 1) * SIDE]
    for row in range(shape.rows_x):
        padded_ref[row * pitch : row * pitch + tile_y] = message_ref[
            row * tile_y : (row + 1) * tile_y
        ]

    first, second = first_ref[shape.side :], second_ref[shape.side :]
    stack = jnp.concatenate(
        [stack_ref[...], jnp.where(even, second, first), jnp.where(even, first, second)], axis=0
    )
    cotangent = dot(place_ref[0], stack)
    mask = dot(place_ref[1], stack[:, :128]).astype(BF16)
    near = dot(mask, spread_ref[0])
    far = dot(mask, spread_ref[1])
    windows = []
    for at_x in range(shape.out_x):
        rows = slice(at_x * SLOTS, (at_x + 1) * SLOTS)
        windows.append(near[rows] * match_ref[0] + far[rows] * match_ref[1])
        level_ref[rows] = (
            dot(
                windows[-1].astype(BF16),
                padded_ref[4 * at_x * pitch : 4 * at_x * pitch + shape.window],
            )
            / 6.0
        ).astype(BF16)
    turned = jnp.concatenate(windows, axis=0).T
    node_x = lax.broadcasted_iota(jnp.int32, (tile_y, shape.nodes), 1) // SLOTS
    for at_x in range(shape.tile_x):
        quotient, rest = (at_x + REACH) // 4, (at_x + REACH) % 4
        cover = jnp.where(node_x == quotient, turned[rest * pitch : rest * pitch + tile_y], 0.0)
        if rest < 2:
            again = (rest + 4) * pitch
            cover = cover + jnp.where(
                node_x == quotient - 1, turned[again : again + tile_y], 0.0
            )
        cover = cover.astype(BF16)
        cover_ref[at_x * tile_y : (at_x + 1) * tile_y] = jnp.concatenate([cover, cover], axis=1)

    level_one = level_ref[...]
    pre_one = dot(level_one, w_one_ref[...])
    value, slope_one = silu_and_slope(pre_one)
    state_one = level_one.astype(F32) + value
    level_two = (0.25 * dot(quad_ref[...], two_halves(state_one))).astype(BF16)
    pre_two = dot(level_two, w_two_ref[...])
    two_bar = dot(quad_ref[:, : shape.nodes], cotangent.astype(BF16))
    pre_two_bar = (two_bar * silu_and_slope(pre_two)[1]).astype(BF16)
    pooled_bar = two_bar + dot_right_t(pre_two_bar, w_two_ref[...])
    one_bar = cotangent + 0.25 * pooled_bar
    pre_one_bar = (one_bar * slope_one).astype(BF16)
    level_bar = one_bar + dot_right_t(pre_one_bar, w_one_ref[...])

    node = lax.broadcasted_iota(jnp.int32, (shape.nodes, channels), 0)
    at_x, at_y = node // SLOTS, node % SLOTS
    owned = (at_x >= NODES_OUT) & (at_x < NODES_OUT + shape.node_x)
    owned = owned & (at_y >= NODES_OUT) & (at_y < NODES_OUT + shape.node_y)
    first = owned & (at_x % 2 == 0) & (at_y % 2 == 0)
    grads_ref[3 * channels : 4 * channels] = dot_left_t(
        level_one, jnp.where(owned, pre_one_bar.astype(F32), 0.0).astype(BF16)
    )
    grads_ref[4 * channels :] = dot_left_t(
        level_two, jnp.where(first, pre_two_bar.astype(F32), 0.0).astype(BF16)
    )

    both = two_halves(level_bar)
    for at, n in pieces(0, shape.cells, 128):
        rows = slice(at, at + n)
        message_bar = dot(cover_ref[rows], both) / 6.0
        pre_message_bar = (message_bar * slope_ref[rows]).astype(BF16)
        pmb_ref[rows] = pre_message_bar
        latent_bar = dot_right_t(pre_message_bar, w_message_ref[...])
        pre_embed_bar = (latent_bar * embed_ref[rows]).astype(BF16)
        peb_ref[rows] = pre_embed_bar
        state_ref[rows] = (latent_bar + dot_right_t(pre_embed_bar, w_embed_ref[...])).astype(BF16)
    own = slice(shape.halo, shape.halo + shape.cells)
    grads_ref[channels : 2 * channels] = dot_left_t(blended_ref[own], peb_ref[...])
    grads_ref[2 * channels : 3 * channels] = dot_left_t(latent_ref[...], pmb_ref[...])

    width = min(total_rows, LANES)
    cell = lax.broadcasted_iota(jnp.int32, (shape.cells, width), 0) + shape.halo
    grad_force = None
    for at in range(0, total_rows, width):
        rows = slice(at, at + width)
        hit = jnp.where(cell == key_ref[0:1, rows], 1.0, 0.0).astype(BF16)
        slot_bar = dot_left_t(hit, state_ref[...]).astype(BF16)
        back_ref[rows] = dot_right_t(slot_bar, w_force_ref[...]).astype(BF16)
        term = dot_left_t(rows_ref[rows], slot_bar)
        grad_force = term if grad_force is None else grad_force + term
    grads_ref[:channels] = grad_force

    half = sent_ref.shape[0]
    upper = narrow_ref[0] % 2
    kept_at = pl.multiple_of(upper * half, half)
    sent_at = pl.multiple_of((1 - upper) * half, half)
    sent_ref[...] = grads_ref[pl.ds(sent_at, half)].astype(BF16)
    kept_ref[...] = grads_ref[pl.ds(kept_at, half)]


def call(kernel, out_shapes, operands, scratch=(), spaces="", out_space=pltpu.VMEM, flops=0):
    kinds = {"s": pltpu.SMEM, "v": pltpu.VMEM}
    spaces = spaces + "v" * (len(operands) - len(spaces))
    moved = sum(math.prod(o.shape) * o.dtype.itemsize for o in list(operands) + list(out_shapes))
    return pl.pallas_call(
        kernel,
        out_shape=tuple(out_shapes),
        in_specs=[pl.BlockSpec(memory_space=kinds[space]) for space in spaces],
        out_specs=tuple(pl.BlockSpec(memory_space=out_space) for _ in out_shapes),
        scratch_shapes=list(scratch),
        compiler_params=pltpu.CompilerParams(vmem_limit_bytes=VMEM_LIMIT),
        cost_estimate=pl.CostEstimate(flops=flops, bytes_accessed=moved, transcendentals=0),
    )(*operands)


def meta_rows(live, target_x, target_y, tile_x, unit_rows, slot, units):
    high = target_x // tile_x
    low = target_x % tile_x
    column = jnp.where(live, target_y, LANES - 1)
    fields = jnp.stack([high, low, column]).astype(F32)
    if unit_rows * units <= LANES:
        before = slot * unit_rows
        after = LANES - before - unit_rows
        return jnp.pad(fields, ((0, 13), (before, after))).astype(BF16)
    blocks = unit_rows // LANES
    fields = fields.reshape(3, blocks, LANES).transpose(1, 0, 2)
    return jnp.pad(fields, ((0, 0), (0, 13), (0, 0))).reshape(16 * blocks, LANES).astype(BF16)


def local(
    grid_state,
    boundary_rows,
    row_count,
    target_x,
    target_y,
    g2m_mask,
    mesh_cotangent,
    w_force,
    w_embed,
    w_message,
    w_level_one,
    w_level_two,
):
    tile_x, tile_y, channels = grid_state.shape
    wide_count = lax.axis_size("wide")
    narrow_count = lax.axis_size("narrow")
    wide_at = lax.axis_index("wide")
    narrow_at = lax.axis_index("narrow")
    held_rows = boundary_rows.shape[0]
    shape = Shape(tile_x, tile_y)
    table = shape.tables()
    table = {
        name: jnp.asarray(value, F32 if name == "match" else BF16)
        for name, value in table.items()
    }

    live = jnp.arange(held_rows) < row_count[0]
    column = target_y - narrow_at * tile_y
    whole_column = wide_count == 4 and held_rows * wide_count <= LANES
    if whole_column:
        units = wide_count
        unit_rows = held_rows
        rows, row_live, row_x, row_y = boundary_rows, live, target_x, column
    else:
        slot_count = wide_count * CAP
        destination = target_x // tile_x
        matches = (destination[:, None] == jnp.arange(wide_count)[None, :]) & live[:, None]
        running = jnp.cumsum(matches.astype(jnp.int32), axis=0) - 1
        slot_index = jnp.sum(jnp.where(matches, running, 0), axis=1)
        send_slot = jnp.where(live, destination * CAP + slot_index, slot_count)
        cells = jnp.full((slot_count,), -1, jnp.int32)
        cells = cells.at[send_slot].set(target_x % tile_x * tile_y + column, mode="drop")
        outgoing = jnp.zeros((slot_count, channels), BF16)
        outgoing = outgoing.at[send_slot].set(boundary_rows, mode="drop")
        outgoing = outgoing.reshape(wide_count, CAP, channels)
        rows = lax.all_to_all(outgoing, "wide", split_axis=0, concat_axis=0, tiled=True)
        cells = lax.all_to_all(
            cells.reshape(wide_count, CAP), "wide", split_axis=0, concat_axis=0, tiled=True
        )
        rows = rows.reshape(slot_count, channels)
        cells = cells.reshape(slot_count)
        units = 3
        unit_rows = slot_count
        row_live = cells >= 0
        row_x = jnp.where(row_live, wide_at * tile_x + cells // tile_y, 0)
        row_y = cells % tile_y

    cells = grid_state.reshape(-1, channels)
    cotangent = mesh_cotangent.reshape(-1, channels)
    mask = g2m_mask.transpose(1, 2, 0).reshape(-1, 36)
    place = jnp.stack([wide_at, narrow_at])
    struct = jax.ShapeDtypeStruct
    long = struct((shape.halo + 2 * shape.edge + unit_rows + 16, channels), BF16)
    plain = struct((shape.halo + 2 * shape.edge, channels), BF16)
    short = struct((unit_rows + 16, channels), BF16)
    (place,) = call(
        open_kernel,
        [struct((2,), jnp.int32)],
        [place],
        spaces="s",
        out_space=pltpu.SMEM,
        flops=LONG,
    )
    if whole_column:
        first, second, third, mesh, own_rows = call(
            functools.partial(pack_kernel, shape, units),
            [long, plain, short, struct((2 * shape.own_nodes, channels), BF16), short],
            [
                place,
                cells,
                cotangent,
                mask,
                rows,
                target_x.reshape(1, -1),
                target_y.reshape(1, -1),
                row_count.reshape(1, 1),
            ],
            spaces="s",
            flops=LONG,
        )
        first_in = swapped(first, "wide", 1)
        second_in = swapped_between(second, "wide")
        onward = jnp.concatenate([third, first_in[plain.shape[0] :]])
        arrived = [first_in, second_in, swapped(onward, "wide", 2)]
    else:

        def with_meta(slot):
            return [rows, meta_rows(row_live, row_x, row_y, tile_x, unit_rows, slot, units)]

        mask = jnp.pad(mask.astype(BF16), ((0, 0), (0, channels - 36)))
        mesh = jnp.concatenate([cotangent, mask])
        own_rows = jnp.concatenate(with_meta(0))
        edge = shape.edge
        to_prev = [cells[: shape.halo], cotangent[:edge], mask[:edge]]
        to_next = [cells[-shape.halo :], cotangent[-edge:], mask[-edge:]]
        to_prev, to_next = jnp.concatenate(to_prev), jnp.concatenate(to_next)
        upward = wide_at % 2 == 0
        first = jnp.concatenate([jnp.where(upward, to_next, to_prev)] + with_meta(1))
        second = jnp.concatenate([jnp.where(upward, to_prev, to_next)] + with_meta(2))
        arrived = [swapped(first, "wide", 1), swapped_between(second, "wide")]

    total_rows = unit_rows * units
    stack_rows = 4 * shape.edge + 2 * shape.own_nodes
    payload = struct((shape.side + 2 * shape.side_nodes, channels), BF16)
    blended, first, second, stack, all_rows, keys = call(
        functools.partial(blend_kernel, shape, units, unit_rows),
        [
            struct((shape.center, channels), BF16),
            payload,
            payload,
            struct((stack_rows, channels), BF16),
            struct((total_rows, channels), BF16),
            struct((8, total_rows), jnp.int32),
        ],
        [place, cells, mesh, w_force, table["to_side"], own_rows] + arrived,
        scratch=[pltpu.VMEM((total_rows, channels), BF16)],
        spaces="s",
        flops=2 * shape.center * total_rows * channels,
    )
    second = swapped_between(second, "narrow")
    first = swapped(first, "narrow", 1)
    message, latent, embed_slope, message_slope = call(
        functools.partial(forward_kernel, shape),
        [
            struct((shape.center, channels), BF16),
            struct((shape.cells, channels), BF16),
            struct((shape.cells, channels), F32),
            struct((shape.cells, channels), F32),
        ],
        [blended, w_embed, w_message],
        flops=4 * shape.center * channels * channels,
    )
    grad_rows_total = 5 * channels
    grad_state, back, sent, kept = call(
        functools.partial(backward_kernel, shape, total_rows),
        [
            struct((shape.cells, channels), BF16),
            struct((total_rows, channels), BF16),
            struct((grad_rows_total // 2, channels), BF16),
            struct((grad_rows_total // 2, channels), F32),
        ],
        [
            narrow_at.reshape(1),
            second,
            first,
            stack,
            blended,
            message,
            latent,
            embed_slope,
            message_slope,
            all_rows,
            keys,
            table["place"],
            table["spread"],
            table["match"],
            table["quad"],
            w_force,
            w_embed,
            w_message,
            w_level_one,
            w_level_two,
        ],
        scratch=[
            pltpu.VMEM((shape.rows_x * shape.pitch, channels), BF16),
            pltpu.VMEM((shape.nodes, channels), BF16),
            pltpu.VMEM((shape.cells, 2 * shape.nodes), BF16),
            pltpu.VMEM((shape.cells, channels), BF16),
            pltpu.VMEM((shape.cells, channels), BF16),
            pltpu.VMEM((grad_rows_total, channels), F32),
        ],
        spaces="s",
        flops=12 * shape.cells * channels * channels,
    )

    piece = kept + swapped(sent, "narrow", 1).astype(F32)
    back_blocks = back.reshape(units, unit_rows, channels)
    row_back = back_blocks[0].astype(F32)
    bits = [1 << k for k in range(1, narrow_count.bit_length() - 1)]
    for bit in bits:
        half = piece.shape[0] // 2
        upper = (narrow_at // bit) % 2
        sent = lax.dynamic_slice_in_dim(piece, (1 - upper) * half, half).astype(BF16)
        kept = lax.dynamic_slice_in_dim(piece, upper * half, half)
        piece = kept + swapped(sent, "narrow", bit).astype(F32)
    part = piece.shape[0] // wide_count
    rounded = piece.astype(BF16)
    own = lax.dynamic_slice_in_dim(piece, wide_at * part, part)
    order = sorted(range(1, wide_count), reverse=True)
    for k in order:
        sent = lax.dynamic_slice_in_dim(rounded, (wide_at ^ k) * part, part)
        if whole_column:
            sent = jnp.concatenate([sent, back_blocks[k]])
        got = swapped(sent, "wide", k).astype(F32)
        own = own + got[:part]
        if whole_column:
            row_back = row_back + got[part:]
    own = own.astype(BF16)
    gathered = jnp.zeros((wide_count * part, channels), BF16)
    gathered = lax.dynamic_update_slice_in_dim(gathered, own, wide_at * part, 0)
    for k in order:
        got = swapped(own, "wide", k)
        gathered = lax.dynamic_update_slice_in_dim(gathered, got, (wide_at ^ k) * part, 0)
    for bit in reversed(bits):
        upper = (narrow_at // bit) % 2
        other = swapped(gathered, "narrow", bit)
        gathered = jnp.where(
            upper == 0,
            jnp.concatenate([gathered, other]),
            jnp.concatenate([other, gathered]),
        )
    other = swapped(gathered, "narrow", 1)
    if whole_column:
        row_back = row_back.astype(BF16)
    else:
        returned = lax.all_to_all(
            back_blocks[0].reshape(wide_count, CAP, channels),
            "wide",
            split_axis=0,
            concat_axis=0,
            tiled=True,
        )
        row_back = jnp.take(
            returned.reshape(-1, channels), send_slot, axis=0, mode="fill", fill_value=0
        )
    cell_total = shape.cells * wide_count * narrow_count
    row_total = held_rows * wide_count * narrow_count
    sizes = [row_total, cell_total, cell_total, cell_total // 16, cell_total // 64]
    scales = np.array([1.0 / math.sqrt(size) for size in sizes], np.float32)
    totals = jnp.where(
        narrow_at % 2 == 0,
        jnp.concatenate([gathered, other]),
        jnp.concatenate([other, gathered]),
    )
    weight_grads = totals.reshape(5, channels, channels).astype(F32) * scales[:, None, None]
    return (grad_state.reshape(tile_x, tile_y, channels), row_back, weight_grads)


def solution(mesh):
    in_specs = (
        P(("groups", "wide"), "narrow", None),
        P(("groups", "wide", "narrow"), None),
        P(("groups", "wide", "narrow")),
        P(("groups", "wide", "narrow")),
        P(("groups", "wide", "narrow")),
        P(None, ("groups", "wide"), "narrow"),
        P(("groups", "wide"), "narrow", None),
        P(),
        P(),
        P(),
        P(),
        P(),
    )
    out_specs = (
        P(("groups", "wide"), "narrow", None),
        P(("groups", "wide", "narrow"), None),
        P("groups", None, None),
    )
    return jax.shard_map(local, mesh=mesh, in_specs=in_specs, out_specs=out_specs, check_vma=False)
```

```python
import functools
import math

import jax
import jax.numpy as jnp
import numpy as np
from jax import lax
from jax.experimental import pallas as pl
from jax.experimental.pallas import tpu as pltpu
from jax.sharding import PartitionSpec as P

CAP = 16
REACH = 9
NODES_OUT = 2
SIDE = 16
SLOTS = 16
LANES = 256
LONG = 10**10
VMEM_LIMIT = 48 * 1024 * 1024
F32 = jnp.float32
BF16 = jnp.bfloat16


def swapped(block, axis, bits):
    count = lax.axis_size(axis)
    return lax.ppermute(block, axis, [(i, i ^ bits) for i in range(count)])


def swapped_between(block, axis):
    count = lax.axis_size(axis)
    pairs = [(i, i + 1) for i in range(1, count - 1, 2)]
    return lax.ppermute(block, axis, pairs + [(j, i) for i, j in pairs])


def dot(left, right):
    return jnp.dot(left, right, preferred_element_type=F32)


def dot_right_t(left, right):
    return lax.dot_general(left, right, (((1,), (1,)), ((), ())), preferred_element_type=F32)


def dot_left_t(left, right):
    return lax.dot_general(left, right, (((0,), (0,)), ((), ())), preferred_element_type=F32)


def sigmoid(value):
    return 0.5 * jnp.tanh(0.5 * value) + 0.5


def silu_and_slope(value):
    logistic = sigmoid(value)
    return value * logistic, logistic * (1.0 + value * (1.0 - logistic))


def silu(value):
    return value * sigmoid(value)


def pieces(start, stop, size):
    return [(at, min(size, stop - at)) for at in range(start, stop, size)]


def two_halves(value):
    high = value.astype(BF16)
    low = (value - high.astype(F32)).astype(BF16)
    return jnp.concatenate([high, low], axis=0)


class Shape:
    def __init__(self, tile_x, tile_y):
        self.tile_x = tile_x
        self.tile_y = tile_y
        self.cells = tile_x * tile_y
        self.rows_x = tile_x + 2 * REACH
        self.halo = REACH * tile_y
        self.center = self.rows_x * tile_y
        self.side = self.rows_x * SIDE
        self.pitch = tile_y + 2 * SIDE
        self.node_x = tile_x // 4
        self.node_y = tile_y // 4
        self.out_x = self.node_x + 2 * NODES_OUT
        self.nodes = self.out_x * SLOTS
        self.edge = NODES_OUT * self.node_y
        self.own_nodes = self.node_x * self.node_y
        self.window = 6 * self.pitch
        self.side_nodes = NODES_OUT * self.out_x

    def center_row(self, at_x, at_y, kind):
        edge, own = self.edge, self.own_nodes
        if at_x < NODES_OUT:
            return kind * edge + at_x * self.node_y + at_y
        at_x -= NODES_OUT
        if at_x < self.node_x:
            return 2 * edge + kind * own + at_x * self.node_y + at_y
        at_x -= self.node_x
        return 2 * edge + 2 * own + kind * edge + at_x * self.node_y + at_y

    def tables(self):
        stack = 4 * self.edge + 2 * self.own_nodes
        side = self.side_nodes
        to_left = np.zeros((2 * side, stack), np.float32)
        to_right = np.zeros((2 * side, stack), np.float32)
        for kind in range(2):
            for at_x in range(self.out_x):
                for k in range(NODES_OUT):
                    row = kind * side + at_x * NODES_OUT + k
                    to_left[row, self.center_row(at_x, k, kind)] = 1
                    last = self.node_y - NODES_OUT + k
                    to_right[row, self.center_row(at_x, last, kind)] = 1
        place = np.zeros((2, self.nodes, stack + 4 * side), np.float32)
        for kind in range(2):
            for at_x in range(self.out_x):
                for slot in range(self.node_y + 2 * NODES_OUT):
                    at_y = slot - NODES_OUT
                    if at_y < 0:
                        column = stack + kind * side + at_x * NODES_OUT + slot
                    elif at_y < self.node_y:
                        column = self.center_row(at_x, at_y, kind)
                    else:
                        k = at_y - self.node_y
                        column = stack + 2 * side + kind * side + at_x * NODES_OUT + k
                    place[kind, at_x * SLOTS + slot, column] = 1
        spread = np.zeros((2, 128, self.window), np.float32)
        match = np.zeros((2, SLOTS, self.window), np.float32)
        for dx in range(6):
            for at in range(self.pitch):
                if at < self.tile_y:
                    y = at
                elif at < self.tile_y + SIDE:
                    y = at - self.tile_y - SIDE
                else:
                    y = at - SIDE
                quotient, rest = (y + REACH) // 4, (y + REACH) % 4
                lane = dx * self.pitch + at
                spread[0, dx * 6 + rest, lane] = 1
                if 0 <= quotient < SLOTS:
                    match[0, quotient, lane] = 1
                if rest < 2:
                    spread[1, dx * 6 + rest + 4, lane] = 1
                    if 0 <= quotient - 1 < SLOTS:
                        match[1, quotient - 1, lane] = 1
        node = np.arange(self.nodes)
        quad = node // SLOTS // 2 * SLOTS + node % SLOTS // 2
        same = (quad[:, None] == quad[None, :]).astype(np.float32)
        return {
            "to_side": np.stack([to_left, to_right]),
            "place": place,
            "spread": spread,
            "match": match,
            "quad": np.concatenate([same, same], axis=1),
        }


def open_kernel(place_ref, out_ref):
    out_ref[0] = place_ref[0]
    out_ref[1] = place_ref[1]


def pack_kernel(
    shape,
    units,
    place_ref,
    own_ref,
    cotangent_ref,
    mask_ref,
    rows_ref,
    target_x_ref,
    target_y_ref,
    count_ref,
    first_ref,
    second_ref,
    third_ref,
    fourth_ref,
    mesh_ref,
    own_rows_ref,
):
    edge, own_nodes, halo = shape.edge, shape.own_nodes, shape.halo
    held = rows_ref.shape[0]
    even = place_ref[0] % 2 == 0
    odd = jnp.logical_not(even)
    target_x = target_x_ref[...]
    column = target_y_ref[...] - place_ref[1] * shape.tile_y
    slot = lax.broadcasted_iota(jnp.int32, (1, held), 1)
    column = jnp.where(slot < count_ref[...], column, LANES - 1)
    line = lax.broadcasted_iota(jnp.int32, (16, held), 0)
    fields = jnp.where(line == 0, target_x // shape.tile_x, 0)
    fields = fields + jnp.where(line == 1, target_x % shape.tile_x, 0)
    fields = fields + jnp.where(line == 2, column, 0)
    lane = lax.broadcasted_iota(jnp.int32, (held, LANES), 1)
    repeat = lane % held == lax.broadcasted_iota(jnp.int32, (held, LANES), 0)
    spread = dot(fields.astype(F32).astype(BF16), jnp.where(repeat, 1.0, 0.0).astype(BF16))
    lane = lax.broadcasted_iota(jnp.int32, (16, LANES), 1)
    for number, ref in enumerate((own_rows_ref, first_ref, third_ref, fourth_ref)):
        at = ref.shape[0] - held - 16
        ref[at : at + held] = rows_ref[...]
        ref[at + held :] = jnp.where(lane // held == number, spread, 0.0).astype(BF16)

    mesh_ref[:own_nodes] = cotangent_ref[...]
    mesh_ref[own_nodes:] = jnp.zeros((own_nodes, mesh_ref.shape[1]), BF16)
    mesh_ref[own_nodes:, : mask_ref.shape[1]] = mask_ref[...].astype(F32).astype(BF16)
    for ref, upward in ((first_ref, even), (second_ref, odd)):
        start = pl.multiple_of(jnp.where(upward, shape.cells - halo, 0), shape.tile_y)
        ref[:halo] = own_ref[pl.ds(start, halo)]
        start = pl.multiple_of(jnp.where(upward, own_nodes - edge, 0), 16)
        ref[halo : halo + edge] = mesh_ref[pl.ds(start, edge)]
        start = pl.multiple_of(jnp.where(upward, 2 * own_nodes - edge, own_nodes), 16)
        ref[halo + edge : halo + 2 * edge] = mesh_ref[pl.ds(start, edge)]


def blend_kernel(shape, units, unit_rows, *refs):
    (place_ref, own_ref, mesh_ref, w_force_ref, side_ref, own_rows_ref) = refs[:6]
    count = units if units > 3 else 2
    arrived = refs[6 : 6 + count]
    (blended_ref, first_ref, second_ref, stack_ref, rows_ref, key_ref) = refs[6 + count : 12 + count]
    (projected_ref,) = refs[12 + count :]
    wide_at = place_ref[0]
    even = wide_at % 2 == 0
    near, between = arrived[0], arrived[1]
    mesh = 2 * shape.edge
    first_row = shape.halo + mesh

    def held(k, at, n):
        if k == 0:
            return own_rows_ref[at : at + n]
        if k == 1 or units == 3:
            return arrived[k - 1][first_row + at : first_row + at + n]
        return arrived[k][at : at + n]

    total = unit_rows * units
    for k in range(units):
        rows_ref[k * unit_rows : (k + 1) * unit_rows] = held(k, 0, unit_rows)
    blocks = []
    if total <= LANES:
        metas = [held(k, unit_rows, 16).astype(F32) for k in range(units)]
        blocks.append(functools.reduce(lambda a, b: a + b, metas)[:, :total])
    else:
        for k in range(units):
            for part in range(unit_rows // LANES):
                blocks.append(held(k, unit_rows + 16 * part, 16).astype(F32))
    keys = []
    for block in blocks:
        whole = block.astype(jnp.int32)
        at_x = whole[0:1] * shape.tile_x + whole[1:2] - wide_at * shape.tile_x + REACH
        at_y = whole[2:3]
        inside = (at_x >= 0) & (at_x < shape.rows_x) & (at_y < shape.tile_y)
        keys.append(jnp.where(inside, at_x * shape.tile_y + at_y, -1))
    width = keys[0].shape[1]
    for k, key in enumerate(keys):
        key_ref[:, k * width : (k + 1) * width] = jnp.broadcast_to(key, (8, width))
    projected_ref[...] = dot(rows_ref[...], w_force_ref[...]).astype(BF16)

    def facing(at, n, forward):
        one, other = near[at : at + n], between[at : at + n]
        return jnp.where(even, one, other) if forward else jnp.where(even, other, one)

    stack = jnp.concatenate(
        [facing(shape.halo, mesh, False), mesh_ref[...], facing(shape.halo, mesh, True)], axis=0
    )
    stack_ref[...] = stack
    narrow_even = place_ref[1] % 2 == 0
    to_left = dot(side_ref[0], stack).astype(BF16)
    to_right = dot(side_ref[1], stack).astype(BF16)
    first_ref[shape.side :] = jnp.where(narrow_even, to_right, to_left)
    second_ref[shape.side :] = jnp.where(narrow_even, to_left, to_right)

    tile_y = shape.tile_y
    inner = shape.halo + shape.cells
    jobs = [(0, at, n) for at, n in pieces(0, shape.halo, 3 * tile_y)]
    jobs += [(shape.halo, at, n) for at, n in pieces(0, shape.cells, 4 * tile_y)]
    jobs += [(inner, at, n) for at, n in pieces(0, shape.halo, 3 * tile_y)]
    for base, at, n in jobs:
        first = base + at
        if base == shape.halo:
            value = own_ref[at : at + n].astype(F32)
        else:
            value = facing(at, n, base == inner).astype(F32)
        cell = lax.broadcasted_iota(jnp.int32, (n, width), 0) + first
        for k, key in enumerate(keys):
            hit = jnp.where(cell == key, 1.0, 0.0).astype(BF16)
            value = value + dot(hit, projected_ref[k * width : (k + 1) * width])
        value = value.astype(BF16)
        blended_ref[first : first + n] = value
        for t in range(n // tile_y):
            row = first // tile_y + t
            target = slice(row * SIDE, (row + 1) * SIDE)
            low = value[t * tile_y : t * tile_y + SIDE]
            high = value[(t + 1) * tile_y - SIDE : (t + 1) * tile_y]
            first_ref[target] = jnp.where(narrow_even, high, low)
            second_ref[target] = jnp.where(narrow_even, low, high)


def forward_kernel(
    shape, blended_ref, w_embed_ref, w_message_ref, message_ref, latent_ref, embed_ref, slope_ref
):
    inner = shape.halo + shape.cells
    jobs = pieces(0, shape.halo, 96) + pieces(shape.halo, inner, 128)
    jobs += pieces(inner, shape.center, 96)
    for at, n in jobs:
        blended = blended_ref[at : at + n]
        pre_embed = dot(blended, w_embed_ref[...])
        value, slope = silu_and_slope(pre_embed)
        latent = (blended.astype(F32) + value).astype(BF16)
        pre_message = dot(latent, w_message_ref[...])
        message, message_slope = silu_and_slope(pre_message)
        message_ref[at : at + n] = message.astype(BF16)
        if shape.halo <= at < inner:
            own = at - shape.halo
            latent_ref[own : own + n] = latent
            embed_ref[own : own + n] = slope
            slope_ref[own : own + n] = message_slope


def backward_kernel(shape, total_rows, *refs):
    (
        narrow_ref,
        second_ref,
        first_ref,
        stack_ref,
        blended_ref,
        message_ref,
        latent_ref,
        embed_ref,
        slope_ref,
        rows_ref,
        key_ref,
        place_ref,
        spread_ref,
        match_ref,
        quad_ref,
        w_force_ref,
        w_embed_ref,
        w_message_ref,
        w_one_ref,
        w_two_ref,
        state_ref,
        back_ref,
        sent_ref,
        kept_ref,
        padded_ref,
        level_ref,
        cover_ref,
        pmb_ref,
        peb_ref,
        grads_ref,
    ) = refs
    tile_y, pitch = shape.tile_y, shape.pitch
    channels = blended_ref.shape[1]

    even = narrow_ref[0] % 2 == 0
    first_at = pl.multiple_of(tile_y + jnp.where(even, SIDE, 0), SIDE)
    second_at = pl.multiple_of(tile_y + jnp.where(even, 0, SIDE), SIDE)
    for ref, offset in ((first_ref, first_at), (second_ref, second_at)):
        for at, n in pieces(0, shape.side, 8 * SIDE):
            blended = ref[at : at + n]
            latent = (blended.astype(F32) + silu(dot(blended, w_embed_ref[...]))).astype(BF16)
            message = silu(dot(latent, w_message_ref[...])).astype(BF16)
            for t in range(n // SIDE):
                row = (at // SIDE + t) * pitch + offset
                padded_ref[pl.ds(row, SIDE)] = message[t * SIDE : (t + 1) * SIDE]
    for row in range(shape.rows_x):
        padded_ref[row * pitch : row * pitch + tile_y] = message_ref[
            row * tile_y : (row + 1) * tile_y
        ]

    first, second = first_ref[shape.side :], second_ref[shape.side :]
    stack = jnp.concatenate(
        [stack_ref[...], jnp.where(even, second, first), jnp.where(even, first, second)], axis=0
    )
    cotangent = dot(place_ref[0], stack)
    mask = dot(place_ref[1], stack[:, :128]).astype(BF16)
    near = dot(mask, spread_ref[0])
    far = dot(mask, spread_ref[1])
    windows = []
    for at_x in range(shape.out_x):
        rows = slice(at_x * SLOTS, (at_x + 1) * SLOTS)
        windows.append(near[rows] * match_ref[0] + far[rows] * match_ref[1])
        level_ref[rows] = (
            dot(
                windows[-1].astype(BF16),
                padded_ref[4 * at_x * pitch : 4 * at_x * pitch + shape.window],
            )
            / 6.0
        ).astype(BF16)
    turned = jnp.concatenate(windows, axis=0).T
    node_x = lax.broadcasted_iota(jnp.int32, (tile_y, shape.nodes), 1) // SLOTS
    for at_x in range(shape.tile_x):
        quotient, rest = (at_x + REACH) // 4, (at_x + REACH) % 4
        cover = jnp.where(node_x == quotient, turned[rest * pitch : rest * pitch + tile_y], 0.0)
        if rest < 2:
            again = (rest + 4) * pitch
            cover = cover + jnp.where(
                node_x == quotient - 1, turned[again : again + tile_y], 0.0
            )
        cover = cover.astype(BF16)
        cover_ref[at_x * tile_y : (at_x + 1) * tile_y] = jnp.concatenate([cover, cover], axis=1)

    level_one = level_ref[...]
    pre_one = dot(level_one, w_one_ref[...])
    value, slope_one = silu_and_slope(pre_one)
    state_one = level_one.astype(F32) + value
    level_two = (0.25 * dot(quad_ref[...], two_halves(state_one))).astype(BF16)
    pre_two = dot(level_two, w_two_ref[...])
    two_bar = dot(quad_ref[:, : shape.nodes], cotangent.astype(BF16))
    pre_two_bar = (two_bar * silu_and_slope(pre_two)[1]).astype(BF16)
    pooled_bar = two_bar + dot_right_t(pre_two_bar, w_two_ref[...])
    one_bar = cotangent + 0.25 * pooled_bar
    pre_one_bar = (one_bar * slope_one).astype(BF16)
    level_bar = one_bar + dot_right_t(pre_one_bar, w_one_ref[...])

    node = lax.broadcasted_iota(jnp.int32, (shape.nodes, channels), 0)
    at_x, at_y = node // SLOTS, node % SLOTS
    owned = (at_x >= NODES_OUT) & (at_x < NODES_OUT + shape.node_x)
    owned = owned & (at_y >= NODES_OUT) & (at_y < NODES_OUT + shape.node_y)
    first = owned & (at_x % 2 == 0) & (at_y % 2 == 0)
    grads_ref[3 * channels : 4 * channels] = dot_left_t(
        level_one, jnp.where(owned, pre_one_bar.astype(F32), 0.0).astype(BF16)
    )
    grads_ref[4 * channels :] = dot_left_t(
        level_two, jnp.where(first, pre_two_bar.astype(F32), 0.0).astype(BF16)
    )

    both = two_halves(level_bar)
    for at, n in pieces(0, shape.cells, 128):
        rows = slice(at, at + n)
        message_bar = dot(cover_ref[rows], both) / 6.0
        pre_message_bar = (message_bar * slope_ref[rows]).astype(BF16)
        pmb_ref[rows] = pre_message_bar
        latent_bar = dot_right_t(pre_message_bar, w_message_ref[...])
        pre_embed_bar = (latent_bar * embed_ref[rows]).astype(BF16)
        peb_ref[rows] = pre_embed_bar
        state_ref[rows] = (latent_bar + dot_right_t(pre_embed_bar, w_embed_ref[...])).astype(BF16)
    own = slice(shape.halo, shape.halo + shape.cells)
    grads_ref[channels : 2 * channels] = dot_left_t(blended_ref[own], peb_ref[...])
    grads_ref[2 * channels : 3 * channels] = dot_left_t(latent_ref[...], pmb_ref[...])

    width = min(total_rows, LANES)
    cell = lax.broadcasted_iota(jnp.int32, (shape.cells, width), 0) + shape.halo
    grad_force = None
    for at in range(0, total_rows, width):
        rows = slice(at, at + width)
        hit = jnp.where(cell == key_ref[0:1, rows], 1.0, 0.0).astype(BF16)
        slot_bar = dot_left_t(hit, state_ref[...]).astype(BF16)
        back_ref[rows] = dot_right_t(slot_bar, w_force_ref[...]).astype(BF16)
        term = dot_left_t(rows_ref[rows], slot_bar)
        grad_force = term if grad_force is None else grad_force + term
    grads_ref[:channels] = grad_force

    half = sent_ref.shape[0]
    upper = narrow_ref[0] % 2
    kept_at = pl.multiple_of(upper * half, half)
    sent_at = pl.multiple_of((1 - upper) * half, half)
    sent_ref[...] = grads_ref[pl.ds(sent_at, half)].astype(BF16)
    kept_ref[...] = grads_ref[pl.ds(kept_at, half)]


def call(kernel, out_shapes, operands, scratch=(), spaces="", out_space=pltpu.VMEM, flops=0):
    kinds = {"s": pltpu.SMEM, "v": pltpu.VMEM}
    spaces = spaces + "v" * (len(operands) - len(spaces))
    moved = sum(math.prod(o.shape) * o.dtype.itemsize for o in list(operands) + list(out_shapes))
    return pl.pallas_call(
        kernel,
        out_shape=tuple(out_shapes),
        in_specs=[pl.BlockSpec(memory_space=kinds[space]) for space in spaces],
        out_specs=tuple(pl.BlockSpec(memory_space=out_space) for _ in out_shapes),
        scratch_shapes=list(scratch),
        compiler_params=pltpu.CompilerParams(vmem_limit_bytes=VMEM_LIMIT),
        cost_estimate=pl.CostEstimate(flops=flops, bytes_accessed=moved, transcendentals=0),
    )(*operands)


def meta_rows(live, target_x, target_y, tile_x, unit_rows, slot, units):
    high = target_x // tile_x
    low = target_x % tile_x
    column = jnp.where(live, target_y, LANES - 1)
    fields = jnp.stack([high, low, column]).astype(F32)
    if unit_rows * units <= LANES:
        before = slot * unit_rows
        after = LANES - before - unit_rows
        return jnp.pad(fields, ((0, 13), (before, after))).astype(BF16)
    blocks = unit_rows // LANES
    fields = fields.reshape(3, blocks, LANES).transpose(1, 0, 2)
    return jnp.pad(fields, ((0, 0), (0, 13), (0, 0))).reshape(16 * blocks, LANES).astype(BF16)


def local(
    grid_state,
    boundary_rows,
    row_count,
    target_x,
    target_y,
    g2m_mask,
    mesh_cotangent,
    w_force,
    w_embed,
    w_message,
    w_level_one,
    w_level_two,
):
    tile_x, tile_y, channels = grid_state.shape
    wide_count = lax.axis_size("wide")
    narrow_count = lax.axis_size("narrow")
    wide_at = lax.axis_index("wide")
    narrow_at = lax.axis_index("narrow")
    held_rows = boundary_rows.shape[0]
    shape = Shape(tile_x, tile_y)
    table = shape.tables()
    table = {
        name: jnp.asarray(value, F32 if name == "match" else BF16)
        for name, value in table.items()
    }

    live = jnp.arange(held_rows) < row_count[0]
    column = target_y - narrow_at * tile_y
    whole_column = wide_count == 4 and held_rows * wide_count <= LANES
    if whole_column:
        units = wide_count
        unit_rows = held_rows
        rows, row_live, row_x, row_y = boundary_rows, live, target_x, column
    else:
        slot_count = wide_count * CAP
        destination = target_x // tile_x
        matches = (destination[:, None] == jnp.arange(wide_count)[None, :]) & live[:, None]
        running = jnp.cumsum(matches.astype(jnp.int32), axis=0) - 1
        slot_index = jnp.sum(jnp.where(matches, running, 0), axis=1)
        send_slot = jnp.where(live, destination * CAP + slot_index, slot_count)
        cells = jnp.full((slot_count,), -1, jnp.int32)
        cells = cells.at[send_slot].set(target_x % tile_x * tile_y + column, mode="drop")
        outgoing = jnp.zeros((slot_count, channels), BF16)
        outgoing = outgoing.at[send_slot].set(boundary_rows, mode="drop")
        outgoing = outgoing.reshape(wide_count, CAP, channels)
        rows = lax.all_to_all(outgoing, "wide", split_axis=0, concat_axis=0, tiled=True)
        cells = lax.all_to_all(
            cells.reshape(wide_count, CAP), "wide", split_axis=0, concat_axis=0, tiled=True
        )
        rows = rows.reshape(slot_count, channels)
        cells = cells.reshape(slot_count)
        units = 3
        unit_rows = slot_count
        row_live = cells >= 0
        row_x = jnp.where(row_live, wide_at * tile_x + cells // tile_y, 0)
        row_y = cells % tile_y

    cells = grid_state.reshape(-1, channels)
    cotangent = mesh_cotangent.reshape(-1, channels)
    mask = g2m_mask.transpose(1, 2, 0).reshape(-1, 36)
    place = jnp.stack([wide_at, narrow_at])
    struct = jax.ShapeDtypeStruct
    long = struct((shape.halo + 2 * shape.edge + unit_rows + 16, channels), BF16)
    plain = struct((shape.halo + 2 * shape.edge, channels), BF16)
    short = struct((unit_rows + 16, channels), BF16)
    (place,) = call(
        open_kernel,
        [struct((2,), jnp.int32)],
        [place],
        spaces="s",
        out_space=pltpu.SMEM,
        flops=LONG,
    )
    if whole_column:
        first, second, third, fourth, mesh, own_rows = call(
            functools.partial(pack_kernel, shape, units),
            [long, plain, short, short, struct((2 * shape.own_nodes, channels), BF16), short],
            [
                place,
                cells,
                cotangent,
                mask,
                rows,
                target_x.reshape(1, -1),
                target_y.reshape(1, -1),
                row_count.reshape(1, 1),
            ],
            spaces="s",
            flops=LONG,
        )
        third = swapped(third, "wide", 2)
        fourth = swapped(fourth, "wide", 3)
        first_in = swapped(first, "wide", 1)
        arrived = [first_in, swapped_between(second, "wide"), third, fourth]
    else:

        def with_meta(slot):
            return [rows, meta_rows(row_live, row_x, row_y, tile_x, unit_rows, slot, units)]

        mask = jnp.pad(mask.astype(BF16), ((0, 0), (0, channels - 36)))
        mesh = jnp.concatenate([cotangent, mask])
        own_rows = jnp.concatenate(with_meta(0))
        edge = shape.edge
        to_prev = [cells[: shape.halo], cotangent[:edge], mask[:edge]]
        to_next = [cells[-shape.halo :], cotangent[-edge:], mask[-edge:]]
        to_prev, to_next = jnp.concatenate(to_prev), jnp.concatenate(to_next)
        upward = wide_at % 2 == 0
        first = jnp.concatenate([jnp.where(upward, to_next, to_prev)] + with_meta(1))
        second = jnp.concatenate([jnp.where(upward, to_prev, to_next)] + with_meta(2))
        arrived = [swapped(first, "wide", 1), swapped_between(second, "wide")]

    total_rows = unit_rows * units
    stack_rows = 4 * shape.edge + 2 * shape.own_nodes
    payload = struct((shape.side + 2 * shape.side_nodes, channels), BF16)
    blended, first, second, stack, all_rows, keys = call(
        functools.partial(blend_kernel, shape, units, unit_rows),
        [
            struct((shape.center, channels), BF16),
            payload,
            payload,
            struct((stack_rows, channels), BF16),
            struct((total_rows, channels), BF16),
            struct((8, total_rows), jnp.int32),
        ],
        [place, cells, mesh, w_force, table["to_side"], own_rows] + arrived,
        scratch=[pltpu.VMEM((total_rows, channels), BF16)],
        spaces="s",
        flops=2 * shape.center * total_rows * channels,
    )
    second = swapped_between(second, "narrow")
    first = swapped(first, "narrow", 1)
    message, latent, embed_slope, message_slope = call(
        functools.partial(forward_kernel, shape),
        [
            struct((shape.center, channels), BF16),
            struct((shape.cells, channels), BF16),
            struct((shape.cells, channels), F32),
            struct((shape.cells, channels), F32),
        ],
        [blended, w_embed, w_message],
        flops=4 * shape.center * channels * channels,
    )
    grad_rows_total = 5 * channels
    grad_state, back, sent, kept = call(
        functools.partial(backward_kernel, shape, total_rows),
        [
            struct((shape.cells, channels), BF16),
            struct((total_rows, channels), BF16),
            struct((grad_rows_total // 2, channels), BF16),
            struct((grad_rows_total // 2, channels), F32),
        ],
        [
            narrow_at.reshape(1),
            second,
            first,
            stack,
            blended,
            message,
            latent,
            embed_slope,
            message_slope,
            all_rows,
            keys,
            table["place"],
            table["spread"],
            table["match"],
            table["quad"],
            w_force,
            w_embed,
            w_message,
            w_level_one,
            w_level_two,
        ],
        scratch=[
            pltpu.VMEM((shape.rows_x * shape.pitch, channels), BF16),
            pltpu.VMEM((shape.nodes, channels), BF16),
            pltpu.VMEM((shape.cells, 2 * shape.nodes), BF16),
            pltpu.VMEM((shape.cells, channels), BF16),
            pltpu.VMEM((shape.cells, channels), BF16),
            pltpu.VMEM((grad_rows_total, channels), F32),
        ],
        spaces="s",
        flops=12 * shape.cells * channels * channels,
    )

    piece = kept + swapped(sent, "narrow", 1).astype(F32)
    back_blocks = back.reshape(units, unit_rows, channels)
    row_back = back_blocks[0].astype(F32)
    bits = [1 << k for k in range(1, narrow_count.bit_length() - 1)]
    for bit in bits:
        half = piece.shape[0] // 2
        upper = (narrow_at // bit) % 2
        sent = lax.dynamic_slice_in_dim(piece, (1 - upper) * half, half).astype(BF16)
        kept = lax.dynamic_slice_in_dim(piece, upper * half, half)
        piece = kept + swapped(sent, "narrow", bit).astype(F32)
    part = piece.shape[0] // wide_count
    rounded = piece.astype(BF16).reshape(wide_count, part, channels)
    if whole_column:
        ordered = [
            lax.dynamic_slice_in_dim(back_blocks, wide_at ^ k, 1) for k in range(wide_count)
        ]
        rounded = jnp.concatenate([rounded, jnp.concatenate(ordered)], axis=1)
    got = lax.all_to_all(rounded, "wide", split_axis=0, concat_axis=0, tiled=True)
    got = got.astype(F32).sum(axis=0)
    if whole_column:
        row_back = got[part:]
    own = got[:part].astype(BF16)
    copies = jnp.broadcast_to(own, (wide_count, part, channels))
    gathered = lax.all_to_all(copies, "wide", split_axis=0, concat_axis=0, tiled=True)
    gathered = gathered.reshape(wide_count * part, channels)
    for bit in reversed(bits):
        upper = (narrow_at // bit) % 2
        other = swapped(gathered, "narrow", bit)
        gathered = jnp.where(
            upper == 0,
            jnp.concatenate([gathered, other]),
            jnp.concatenate([other, gathered]),
        )
    other = swapped(gathered, "narrow", 1)
    if whole_column:
        row_back = row_back.astype(BF16)
    else:
        returned = lax.all_to_all(
            back_blocks[0].reshape(wide_count, CAP, channels),
            "wide",
            split_axis=0,
            concat_axis=0,
            tiled=True,
        )
        row_back = jnp.take(
            returned.reshape(-1, channels), send_slot, axis=0, mode="fill", fill_value=0
        )
    cell_total = shape.cells * wide_count * narrow_count
    row_total = held_rows * wide_count * narrow_count
    sizes = [row_total, cell_total, cell_total, cell_total // 16, cell_total // 64]
    scales = np.array([1.0 / math.sqrt(size) for size in sizes], np.float32)
    totals = jnp.where(
        narrow_at % 2 == 0,
        jnp.concatenate([gathered, other]),
        jnp.concatenate([other, gathered]),
    )
    weight_grads = totals.reshape(5, channels, channels).astype(F32) * scales[:, None, None]
    return (grad_state.reshape(tile_x, tile_y, channels), row_back, weight_grads)


def solution(mesh):
    in_specs = (
        P(("groups", "wide"), "narrow", None),
        P(("groups", "wide", "narrow"), None),
        P(("groups", "wide", "narrow")),
        P(("groups", "wide", "narrow")),
        P(("groups", "wide", "narrow")),
        P(None, ("groups", "wide"), "narrow"),
        P(("groups", "wide"), "narrow", None),
        P(),
        P(),
        P(),
        P(),
        P(),
    )
    out_specs = (
        P(("groups", "wide"), "narrow", None),
        P(("groups", "wide", "narrow"), None),
        P("groups", None, None),
    )
    return jax.shard_map(local, mesh=mesh, in_specs=in_specs, out_specs=out_specs, check_vma=False)
```

```python
import functools
import math

import jax
import jax.numpy as jnp
import numpy as np
from jax import lax
from jax.experimental import pallas as pl
from jax.experimental.pallas import tpu as pltpu
from jax.sharding import PartitionSpec as P

CAP = 16
REACH = 9
NODES_OUT = 2
SIDE = 16
SLOTS = 16
LANES = 256
LONG = 10**10
VMEM_LIMIT = 48 * 1024 * 1024
F32 = jnp.float32
BF16 = jnp.bfloat16


def swapped(block, axis, bits):
    count = lax.axis_size(axis)
    return lax.ppermute(block, axis, [(i, i ^ bits) for i in range(count)])


def shifted(block, axis, step):
    count = lax.axis_size(axis)
    return lax.ppermute(block, axis, [(i, (i + step) % count) for i in range(count)])


def swapped_between(block, axis):
    count = lax.axis_size(axis)
    pairs = [(i, i + 1) for i in range(1, count - 1, 2)]
    return lax.ppermute(block, axis, pairs + [(j, i) for i, j in pairs])


def dot(left, right):
    return jnp.dot(left, right, preferred_element_type=F32)


def dot_right_t(left, right):
    return lax.dot_general(left, right, (((1,), (1,)), ((), ())), preferred_element_type=F32)


def dot_left_t(left, right):
    return lax.dot_general(left, right, (((0,), (0,)), ((), ())), preferred_element_type=F32)


def sigmoid(value):
    return 0.5 * jnp.tanh(0.5 * value) + 0.5


def silu_and_slope(value):
    logistic = sigmoid(value)
    return value * logistic, logistic * (1.0 + value * (1.0 - logistic))


def silu(value):
    return value * sigmoid(value)


def pieces(start, stop, size):
    return [(at, min(size, stop - at)) for at in range(start, stop, size)]


def two_halves(value):
    high = value.astype(BF16)
    low = (value - high.astype(F32)).astype(BF16)
    return jnp.concatenate([high, low], axis=0)


class Shape:
    def __init__(self, tile_x, tile_y):
        self.tile_x = tile_x
        self.tile_y = tile_y
        self.cells = tile_x * tile_y
        self.rows_x = tile_x + 2 * REACH
        self.halo = REACH * tile_y
        self.center = self.rows_x * tile_y
        self.side = self.rows_x * SIDE
        self.pitch = tile_y + 2 * SIDE
        self.node_x = tile_x // 4
        self.node_y = tile_y // 4
        self.out_x = self.node_x + 2 * NODES_OUT
        self.nodes = self.out_x * SLOTS
        self.edge = NODES_OUT * self.node_y
        self.own_nodes = self.node_x * self.node_y
        self.window = 6 * self.pitch
        self.side_nodes = NODES_OUT * self.out_x

    def center_row(self, at_x, at_y, kind):
        edge, own = self.edge, self.own_nodes
        if at_x < NODES_OUT:
            return kind * edge + at_x * self.node_y + at_y
        at_x -= NODES_OUT
        if at_x < self.node_x:
            return 2 * edge + kind * own + at_x * self.node_y + at_y
        at_x -= self.node_x
        return 2 * edge + 2 * own + kind * edge + at_x * self.node_y + at_y

    def tables(self):
        stack = 4 * self.edge + 2 * self.own_nodes
        side = self.side_nodes
        to_left = np.zeros((2 * side, stack), np.float32)
        to_right = np.zeros((2 * side, stack), np.float32)
        for kind in range(2):
            for at_x in range(self.out_x):
                for k in range(NODES_OUT):
                    row = kind * side + at_x * NODES_OUT + k
                    to_left[row, self.center_row(at_x, k, kind)] = 1
                    last = self.node_y - NODES_OUT + k
                    to_right[row, self.center_row(at_x, last, kind)] = 1
        place = np.zeros((2, self.nodes, stack + 4 * side), np.float32)
        for kind in range(2):
            for at_x in range(self.out_x):
                for slot in range(self.node_y + 2 * NODES_OUT):
                    at_y = slot - NODES_OUT
                    if at_y < 0:
                        column = stack + kind * side + at_x * NODES_OUT + slot
                    elif at_y < self.node_y:
                        column = self.center_row(at_x, at_y, kind)
                    else:
                        k = at_y - self.node_y
                        column = stack + 2 * side + kind * side + at_x * NODES_OUT + k
                    place[kind, at_x * SLOTS + slot, column] = 1
        spread = np.zeros((2, 128, self.window), np.float32)
        match = np.zeros((2, SLOTS, self.window), np.float32)
        for dx in range(6):
            for at in range(self.pitch):
                if at < self.tile_y:
                    y = at
                elif at < self.tile_y + SIDE:
                    y = at - self.tile_y - SIDE
                else:
                    y = at - SIDE
                quotient, rest = (y + REACH) // 4, (y + REACH) % 4
                lane = dx * self.pitch + at
                spread[0, dx * 6 + rest, lane] = 1
                if 0 <= quotient < SLOTS:
                    match[0, quotient, lane] = 1
                if rest < 2:
                    spread[1, dx * 6 + rest + 4, lane] = 1
                    if 0 <= quotient - 1 < SLOTS:
                        match[1, quotient - 1, lane] = 1
        node = np.arange(self.nodes)
        quad = node // SLOTS // 2 * SLOTS + node % SLOTS // 2
        same = (quad[:, None] == quad[None, :]).astype(np.float32)
        return {
            "to_side": np.stack([to_left, to_right]),
            "place": place,
            "spread": spread,
            "match": match,
            "quad": np.concatenate([same, same], axis=1),
        }


def open_kernel(place_ref, out_ref):
    out_ref[0] = place_ref[0]
    out_ref[1] = place_ref[1]


def pack_kernel(
    shape,
    units,
    place_ref,
    own_ref,
    cotangent_ref,
    mask_ref,
    rows_ref,
    target_x_ref,
    target_y_ref,
    count_ref,
    first_ref,
    second_ref,
    third_ref,
    fourth_ref,
    mesh_ref,
    own_rows_ref,
):
    edge, own_nodes, halo = shape.edge, shape.own_nodes, shape.halo
    held = rows_ref.shape[0]
    even = place_ref[0] % 2 == 0
    odd = jnp.logical_not(even)
    target_x = target_x_ref[...]
    column = target_y_ref[...] - place_ref[1] * shape.tile_y
    slot = lax.broadcasted_iota(jnp.int32, (1, held), 1)
    column = jnp.where(slot < count_ref[...], column, LANES - 1)
    line = lax.broadcasted_iota(jnp.int32, (16, held), 0)
    fields = jnp.where(line == 0, target_x // shape.tile_x, 0)
    fields = fields + jnp.where(line == 1, target_x % shape.tile_x, 0)
    fields = fields + jnp.where(line == 2, column, 0)
    lane = lax.broadcasted_iota(jnp.int32, (held, LANES), 1)
    repeat = lane % held == lax.broadcasted_iota(jnp.int32, (held, LANES), 0)
    spread = dot(fields.astype(F32).astype(BF16), jnp.where(repeat, 1.0, 0.0).astype(BF16))
    lane = lax.broadcasted_iota(jnp.int32, (16, LANES), 1)
    for number, ref in enumerate((own_rows_ref, first_ref, third_ref, fourth_ref)):
        at = ref.shape[0] - held - 16
        ref[at : at + held] = rows_ref[...]
        ref[at + held :] = jnp.where(lane // held == number, spread, 0.0).astype(BF16)

    mesh_ref[:own_nodes] = cotangent_ref[...]
    mesh_ref[own_nodes:] = jnp.zeros((own_nodes, mesh_ref.shape[1]), BF16)
    mesh_ref[own_nodes:, : mask_ref.shape[1]] = mask_ref[...].astype(F32).astype(BF16)
    for ref, upward in ((first_ref, even), (second_ref, odd)):
        start = pl.multiple_of(jnp.where(upward, shape.cells - halo, 0), shape.tile_y)
        ref[:halo] = own_ref[pl.ds(start, halo)]
        start = pl.multiple_of(jnp.where(upward, own_nodes - edge, 0), 16)
        ref[halo : halo + edge] = mesh_ref[pl.ds(start, edge)]
        start = pl.multiple_of(jnp.where(upward, 2 * own_nodes - edge, own_nodes), 16)
        ref[halo + edge : halo + 2 * edge] = mesh_ref[pl.ds(start, edge)]


def blend_kernel(shape, units, unit_rows, *refs):
    (place_ref, own_ref, mesh_ref, w_force_ref, side_ref, own_rows_ref) = refs[:6]
    count = units if units > 3 else 2
    arrived = refs[6 : 6 + count]
    (blended_ref, first_ref, second_ref, stack_ref, rows_ref, key_ref) = refs[6 + count : 12 + count]
    (projected_ref,) = refs[12 + count :]
    wide_at = place_ref[0]
    even = wide_at % 2 == 0
    near, between = arrived[0], arrived[1]
    mesh = 2 * shape.edge
    first_row = shape.halo + mesh

    def held(k, at, n):
        if k == 0:
            return own_rows_ref[at : at + n]
        if k == 1 or units == 3:
            return arrived[k - 1][first_row + at : first_row + at + n]
        return arrived[k][at : at + n]

    total = unit_rows * units
    for k in range(units):
        rows_ref[k * unit_rows : (k + 1) * unit_rows] = held(k, 0, unit_rows)
    blocks = []
    if total <= LANES:
        metas = [held(k, unit_rows, 16).astype(F32) for k in range(units)]
        blocks.append(functools.reduce(lambda a, b: a + b, metas)[:, :total])
    else:
        for k in range(units):
            for part in range(unit_rows // LANES):
                blocks.append(held(k, unit_rows + 16 * part, 16).astype(F32))
    keys = []
    for block in blocks:
        whole = block.astype(jnp.int32)
        at_x = whole[0:1] * shape.tile_x + whole[1:2] - wide_at * shape.tile_x + REACH
        at_y = whole[2:3]
        inside = (at_x >= 0) & (at_x < shape.rows_x) & (at_y < shape.tile_y)
        keys.append(jnp.where(inside, at_x * shape.tile_y + at_y, -1))
    width = keys[0].shape[1]
    for k, key in enumerate(keys):
        key_ref[:, k * width : (k + 1) * width] = jnp.broadcast_to(key, (8, width))
    projected_ref[...] = dot(rows_ref[...], w_force_ref[...]).astype(BF16)

    def facing(at, n, forward):
        one, other = near[at : at + n], between[at : at + n]
        return jnp.where(even, one, other) if forward else jnp.where(even, other, one)

    stack = jnp.concatenate(
        [facing(shape.halo, mesh, False), mesh_ref[...], facing(shape.halo, mesh, True)], axis=0
    )
    stack_ref[...] = stack
    narrow_even = place_ref[1] % 2 == 0
    to_left = dot(side_ref[0], stack).astype(BF16)
    to_right = dot(side_ref[1], stack).astype(BF16)
    first_ref[shape.side :] = jnp.where(narrow_even, to_right, to_left)
    second_ref[shape.side :] = jnp.where(narrow_even, to_left, to_right)

    tile_y = shape.tile_y
    inner = shape.halo + shape.cells
    jobs = [(0, at, n) for at, n in pieces(0, shape.halo, 3 * tile_y)]
    jobs += [(shape.halo, at, n) for at, n in pieces(0, shape.cells, 4 * tile_y)]
    jobs += [(inner, at, n) for at, n in pieces(0, shape.halo, 3 * tile_y)]
    for base, at, n in jobs:
        first = base + at
        if base == shape.halo:
            value = own_ref[at : at + n].astype(F32)
        else:
            value = facing(at, n, base == inner).astype(F32)
        cell = lax.broadcasted_iota(jnp.int32, (n, width), 0) + first
        for k, key in enumerate(keys):
            hit = jnp.where(cell == key, 1.0, 0.0).astype(BF16)
            value = value + dot(hit, projected_ref[k * width : (k + 1) * width])
        value = value.astype(BF16)
        blended_ref[first : first + n] = value
        for t in range(n // tile_y):
            row = first // tile_y + t
            target = slice(row * SIDE, (row + 1) * SIDE)
            low = value[t * tile_y : t * tile_y + SIDE]
            high = value[(t + 1) * tile_y - SIDE : (t + 1) * tile_y]
            first_ref[target] = jnp.where(narrow_even, high, low)
            second_ref[target] = jnp.where(narrow_even, low, high)


def forward_kernel(
    shape, blended_ref, w_embed_ref, w_message_ref, message_ref, latent_ref, embed_ref, slope_ref
):
    inner = shape.halo + shape.cells
    jobs = pieces(0, shape.halo, 96) + pieces(shape.halo, inner, 128)
    jobs += pieces(inner, shape.center, 96)
    for at, n in jobs:
        blended = blended_ref[at : at + n]
        pre_embed = dot(blended, w_embed_ref[...])
        value, slope = silu_and_slope(pre_embed)
        latent = (blended.astype(F32) + value).astype(BF16)
        pre_message = dot(latent, w_message_ref[...])
        message, message_slope = silu_and_slope(pre_message)
        message_ref[at : at + n] = message.astype(BF16)
        if shape.halo <= at < inner:
            own = at - shape.halo
            latent_ref[own : own + n] = latent
            embed_ref[own : own + n] = slope
            slope_ref[own : own + n] = message_slope


def backward_kernel(shape, total_rows, *refs):
    (
        narrow_ref,
        second_ref,
        first_ref,
        stack_ref,
        blended_ref,
        message_ref,
        latent_ref,
        embed_ref,
        slope_ref,
        rows_ref,
        key_ref,
        place_ref,
        spread_ref,
        match_ref,
        quad_ref,
        w_force_ref,
        w_embed_ref,
        w_message_ref,
        w_one_ref,
        w_two_ref,
        state_ref,
        back_ref,
        sent_ref,
        kept_ref,
        padded_ref,
        level_ref,
        cover_ref,
        pmb_ref,
        peb_ref,
        grads_ref,
    ) = refs
    tile_y, pitch = shape.tile_y, shape.pitch
    channels = blended_ref.shape[1]

    even = narrow_ref[0] % 2 == 0
    first_at = pl.multiple_of(tile_y + jnp.where(even, SIDE, 0), SIDE)
    second_at = pl.multiple_of(tile_y + jnp.where(even, 0, SIDE), SIDE)
    for ref, offset in ((first_ref, first_at), (second_ref, second_at)):
        for at, n in pieces(0, shape.side, 8 * SIDE):
            blended = ref[at : at + n]
            latent = (blended.astype(F32) + silu(dot(blended, w_embed_ref[...]))).astype(BF16)
            message = silu(dot(latent, w_message_ref[...])).astype(BF16)
            for t in range(n // SIDE):
                row = (at // SIDE + t) * pitch + offset
                padded_ref[pl.ds(row, SIDE)] = message[t * SIDE : (t + 1) * SIDE]
    for row in range(shape.rows_x):
        padded_ref[row * pitch : row * pitch + tile_y] = message_ref[
            row * tile_y : (row + 1) * tile_y
        ]

    first, second = first_ref[shape.side :], second_ref[shape.side :]
    stack = jnp.concatenate(
        [stack_ref[...], jnp.where(even, second, first), jnp.where(even, first, second)], axis=0
    )
    cotangent = dot(place_ref[0], stack)
    mask = dot(place_ref[1], stack[:, :128]).astype(BF16)
    near = dot(mask, spread_ref[0])
    far = dot(mask, spread_ref[1])
    windows = []
    for at_x in range(shape.out_x):
        rows = slice(at_x * SLOTS, (at_x + 1) * SLOTS)
        windows.append(near[rows] * match_ref[0] + far[rows] * match_ref[1])
        level_ref[rows] = (
            dot(
                windows[-1].astype(BF16),
                padded_ref[4 * at_x * pitch : 4 * at_x * pitch + shape.window],
            )
            / 6.0
        ).astype(BF16)
    turned = jnp.concatenate(windows, axis=0).T
    node_x = lax.broadcasted_iota(jnp.int32, (tile_y, shape.nodes), 1) // SLOTS
    for at_x in range(shape.tile_x):
        quotient, rest = (at_x + REACH) // 4, (at_x + REACH) % 4
        cover = jnp.where(node_x == quotient, turned[rest * pitch : rest * pitch + tile_y], 0.0)
        if rest < 2:
            again = (rest + 4) * pitch
            cover = cover + jnp.where(
                node_x == quotient - 1, turned[again : again + tile_y], 0.0
            )
        cover = cover.astype(BF16)
        cover_ref[at_x * tile_y : (at_x + 1) * tile_y] = jnp.concatenate([cover, cover], axis=1)

    level_one = level_ref[...]
    pre_one = dot(level_one, w_one_ref[...])
    value, slope_one = silu_and_slope(pre_one)
    state_one = level_one.astype(F32) + value
    level_two = (0.25 * dot(quad_ref[...], two_halves(state_one))).astype(BF16)
    pre_two = dot(level_two, w_two_ref[...])
    two_bar = dot(quad_ref[:, : shape.nodes], cotangent.astype(BF16))
    pre_two_bar = (two_bar * silu_and_slope(pre_two)[1]).astype(BF16)
    pooled_bar = two_bar + dot_right_t(pre_two_bar, w_two_ref[...])
    one_bar = cotangent + 0.25 * pooled_bar
    pre_one_bar = (one_bar * slope_one).astype(BF16)
    level_bar = one_bar + dot_right_t(pre_one_bar, w_one_ref[...])

    node = lax.broadcasted_iota(jnp.int32, (shape.nodes, channels), 0)
    at_x, at_y = node // SLOTS, node % SLOTS
    owned = (at_x >= NODES_OUT) & (at_x < NODES_OUT + shape.node_x)
    owned = owned & (at_y >= NODES_OUT) & (at_y < NODES_OUT + shape.node_y)
    first = owned & (at_x % 2 == 0) & (at_y % 2 == 0)
    grads_ref[3 * channels : 4 * channels] = dot_left_t(
        level_one, jnp.where(owned, pre_one_bar.astype(F32), 0.0).astype(BF16)
    )
    grads_ref[4 * channels :] = dot_left_t(
        level_two, jnp.where(first, pre_two_bar.astype(F32), 0.0).astype(BF16)
    )

    both = two_halves(level_bar)
    for at, n in pieces(0, shape.cells, 128):
        rows = slice(at, at + n)
        message_bar = dot(cover_ref[rows], both) / 6.0
        pre_message_bar = (message_bar * slope_ref[rows]).astype(BF16)
        pmb_ref[rows] = pre_message_bar
        latent_bar = dot_right_t(pre_message_bar, w_message_ref[...])
        pre_embed_bar = (latent_bar * embed_ref[rows]).astype(BF16)
        peb_ref[rows] = pre_embed_bar
        state_ref[rows] = (latent_bar + dot_right_t(pre_embed_bar, w_embed_ref[...])).astype(BF16)
    own = slice(shape.halo, shape.halo + shape.cells)
    grads_ref[channels : 2 * channels] = dot_left_t(blended_ref[own], peb_ref[...])
    grads_ref[2 * channels : 3 * channels] = dot_left_t(latent_ref[...], pmb_ref[...])

    width = min(total_rows, LANES)
    cell = lax.broadcasted_iota(jnp.int32, (shape.cells, width), 0) + shape.halo
    grad_force = None
    for at in range(0, total_rows, width):
        rows = slice(at, at + width)
        hit = jnp.where(cell == key_ref[0:1, rows], 1.0, 0.0).astype(BF16)
        slot_bar = dot_left_t(hit, state_ref[...]).astype(BF16)
        back_ref[rows] = dot_right_t(slot_bar, w_force_ref[...]).astype(BF16)
        term = dot_left_t(rows_ref[rows], slot_bar)
        grad_force = term if grad_force is None else grad_force + term
    grads_ref[:channels] = grad_force

    half = sent_ref.shape[0]
    upper = narrow_ref[0] % 2
    kept_at = pl.multiple_of(upper * half, half)
    sent_at = pl.multiple_of((1 - upper) * half, half)
    sent_ref[...] = grads_ref[pl.ds(sent_at, half)].astype(BF16)
    kept_ref[...] = grads_ref[pl.ds(kept_at, half)]


def call(kernel, out_shapes, operands, scratch=(), spaces="", out_space=pltpu.VMEM, flops=0):
    kinds = {"s": pltpu.SMEM, "v": pltpu.VMEM}
    spaces = spaces + "v" * (len(operands) - len(spaces))
    moved = sum(math.prod(o.shape) * o.dtype.itemsize for o in list(operands) + list(out_shapes))
    return pl.pallas_call(
        kernel,
        out_shape=tuple(out_shapes),
        in_specs=[pl.BlockSpec(memory_space=kinds[space]) for space in spaces],
        out_specs=tuple(pl.BlockSpec(memory_space=out_space) for _ in out_shapes),
        scratch_shapes=list(scratch),
        compiler_params=pltpu.CompilerParams(vmem_limit_bytes=VMEM_LIMIT),
        cost_estimate=pl.CostEstimate(flops=flops, bytes_accessed=moved, transcendentals=0),
    )(*operands)


def meta_rows(live, target_x, target_y, tile_x, unit_rows, slot, units):
    high = target_x // tile_x
    low = target_x % tile_x
    column = jnp.where(live, target_y, LANES - 1)
    fields = jnp.stack([high, low, column]).astype(F32)
    if unit_rows * units <= LANES:
        before = slot * unit_rows
        after = LANES - before - unit_rows
        return jnp.pad(fields, ((0, 13), (before, after))).astype(BF16)
    blocks = unit_rows // LANES
    fields = fields.reshape(3, blocks, LANES).transpose(1, 0, 2)
    return jnp.pad(fields, ((0, 0), (0, 13), (0, 0))).reshape(16 * blocks, LANES).astype(BF16)


def local(
    grid_state,
    boundary_rows,
    row_count,
    target_x,
    target_y,
    g2m_mask,
    mesh_cotangent,
    w_force,
    w_embed,
    w_message,
    w_level_one,
    w_level_two,
):
    tile_x, tile_y, channels = grid_state.shape
    wide_count = lax.axis_size("wide")
    narrow_count = lax.axis_size("narrow")
    wide_at = lax.axis_index("wide")
    narrow_at = lax.axis_index("narrow")
    held_rows = boundary_rows.shape[0]
    shape = Shape(tile_x, tile_y)
    table = shape.tables()
    table = {
        name: jnp.asarray(value, F32 if name == "match" else BF16)
        for name, value in table.items()
    }

    live = jnp.arange(held_rows) < row_count[0]
    column = target_y - narrow_at * tile_y
    whole_column = wide_count == 4 and held_rows * wide_count <= LANES
    if whole_column:
        units = wide_count
        unit_rows = held_rows
        rows, row_live, row_x, row_y = boundary_rows, live, target_x, column
    else:
        slot_count = wide_count * CAP
        destination = target_x // tile_x
        matches = (destination[:, None] == jnp.arange(wide_count)[None, :]) & live[:, None]
        running = jnp.cumsum(matches.astype(jnp.int32), axis=0) - 1
        slot_index = jnp.sum(jnp.where(matches, running, 0), axis=1)
        send_slot = jnp.where(live, destination * CAP + slot_index, slot_count)
        cells = jnp.full((slot_count,), -1, jnp.int32)
        cells = cells.at[send_slot].set(target_x % tile_x * tile_y + column, mode="drop")
        outgoing = jnp.zeros((slot_count, channels), BF16)
        outgoing = outgoing.at[send_slot].set(boundary_rows, mode="drop")
        outgoing = outgoing.reshape(wide_count, CAP, channels)
        rows = lax.all_to_all(outgoing, "wide", split_axis=0, concat_axis=0, tiled=True)
        cells = lax.all_to_all(
            cells.reshape(wide_count, CAP), "wide", split_axis=0, concat_axis=0, tiled=True
        )
        rows = rows.reshape(slot_count, channels)
        cells = cells.reshape(slot_count)
        units = 3
        unit_rows = slot_count
        row_live = cells >= 0
        row_x = jnp.where(row_live, wide_at * tile_x + cells // tile_y, 0)
        row_y = cells % tile_y

    cells = grid_state.reshape(-1, channels)
    cotangent = mesh_cotangent.reshape(-1, channels)
    mask = g2m_mask.transpose(1, 2, 0).reshape(-1, 36)
    place = jnp.stack([wide_at, narrow_at])
    struct = jax.ShapeDtypeStruct
    long = struct((shape.halo + 2 * shape.edge + unit_rows + 16, channels), BF16)
    plain = struct((shape.halo + 2 * shape.edge, channels), BF16)
    short = struct((unit_rows + 16, channels), BF16)
    (place,) = call(
        open_kernel,
        [struct((2,), jnp.int32)],
        [place],
        spaces="s",
        out_space=pltpu.SMEM,
        flops=LONG,
    )
    if whole_column:
        first, second, third, fourth, mesh, own_rows = call(
            functools.partial(pack_kernel, shape, units),
            [long, plain, short, short, struct((2 * shape.own_nodes, channels), BF16), short],
            [
                place,
                cells,
                cotangent,
                mask,
                rows,
                target_x.reshape(1, -1),
                target_y.reshape(1, -1),
                row_count.reshape(1, 1),
            ],
            spaces="s",
            flops=LONG,
        )
        third = swapped(third, "wide", 2)
        fourth = swapped(fourth, "wide", 3)
        first_in = swapped(first, "wide", 1)
        arrived = [first_in, swapped_between(second, "wide"), third, fourth]
    else:

        def with_meta(slot):
            return [rows, meta_rows(row_live, row_x, row_y, tile_x, unit_rows, slot, units)]

        mask = jnp.pad(mask.astype(BF16), ((0, 0), (0, channels - 36)))
        mesh = jnp.concatenate([cotangent, mask])
        own_rows = jnp.concatenate(with_meta(0))
        edge = shape.edge
        to_prev = [cells[: shape.halo], cotangent[:edge], mask[:edge]]
        to_next = [cells[-shape.halo :], cotangent[-edge:], mask[-edge:]]
        to_prev, to_next = jnp.concatenate(to_prev), jnp.concatenate(to_next)
        upward = wide_at % 2 == 0
        first = jnp.concatenate([jnp.where(upward, to_next, to_prev)] + with_meta(1))
        second = jnp.concatenate([jnp.where(upward, to_prev, to_next)] + with_meta(2))
        arrived = [swapped(first, "wide", 1), swapped_between(second, "wide")]

    total_rows = unit_rows * units
    stack_rows = 4 * shape.edge + 2 * shape.own_nodes
    payload = struct((shape.side + 2 * shape.side_nodes, channels), BF16)
    blended, first, second, stack, all_rows, keys = call(
        functools.partial(blend_kernel, shape, units, unit_rows),
        [
            struct((shape.center, channels), BF16),
            payload,
            payload,
            struct((stack_rows, channels), BF16),
            struct((total_rows, channels), BF16),
            struct((8, total_rows), jnp.int32),
        ],
        [place, cells, mesh, w_force, table["to_side"], own_rows] + arrived,
        scratch=[pltpu.VMEM((total_rows, channels), BF16)],
        spaces="s",
        flops=2 * shape.center * total_rows * channels,
    )
    second = swapped_between(second, "narrow")
    first = swapped(first, "narrow", 1)
    message, latent, embed_slope, message_slope = call(
        functools.partial(forward_kernel, shape),
        [
            struct((shape.center, channels), BF16),
            struct((shape.cells, channels), BF16),
            struct((shape.cells, channels), F32),
            struct((shape.cells, channels), F32),
        ],
        [blended, w_embed, w_message],
        flops=4 * shape.center * channels * channels,
    )
    grad_rows_total = 5 * channels
    grad_state, back, sent, kept = call(
        functools.partial(backward_kernel, shape, total_rows),
        [
            struct((shape.cells, channels), BF16),
            struct((total_rows, channels), BF16),
            struct((grad_rows_total // 2, channels), BF16),
            struct((grad_rows_total // 2, channels), F32),
        ],
        [
            narrow_at.reshape(1),
            second,
            first,
            stack,
            blended,
            message,
            latent,
            embed_slope,
            message_slope,
            all_rows,
            keys,
            table["place"],
            table["spread"],
            table["match"],
            table["quad"],
            w_force,
            w_embed,
            w_message,
            w_level_one,
            w_level_two,
        ],
        scratch=[
            pltpu.VMEM((shape.rows_x * shape.pitch, channels), BF16),
            pltpu.VMEM((shape.nodes, channels), BF16),
            pltpu.VMEM((shape.cells, 2 * shape.nodes), BF16),
            pltpu.VMEM((shape.cells, channels), BF16),
            pltpu.VMEM((shape.cells, channels), BF16),
            pltpu.VMEM((grad_rows_total, channels), F32),
        ],
        spaces="s",
        flops=12 * shape.cells * channels * channels,
    )

    piece = kept + swapped(sent, "narrow", 1).astype(F32)
    back_blocks = back.reshape(units, unit_rows, channels)
    row_back = back_blocks[0].astype(F32)
    bits = [1 << k for k in range(1, narrow_count.bit_length() - 1)]
    for bit in bits:
        half = piece.shape[0] // 2
        upper = (narrow_at // bit) % 2
        sent = lax.dynamic_slice_in_dim(piece, (1 - upper) * half, half).astype(BF16)
        kept = lax.dynamic_slice_in_dim(piece, upper * half, half)
        piece = kept + swapped(sent, "narrow", bit).astype(F32)
    part = piece.shape[0] // wide_count
    rounded = piece.astype(BF16)
    own = lax.dynamic_slice_in_dim(piece, wide_at * part, part)
    for k in range(1, wide_count):
        target = (wide_at + k) % wide_count
        sent = lax.dynamic_slice_in_dim(rounded, target * part, part)
        if whole_column:
            block = lax.dynamic_slice_in_dim(back_blocks, target ^ wide_at, 1)
            sent = jnp.concatenate([sent, block[0]])
        got = shifted(sent, "wide", k).astype(F32)
        own = own + got[:part]
        if whole_column:
            row_back = row_back + got[part:]
    own = own.astype(BF16)
    gathered = jnp.zeros((wide_count * part, channels), BF16)
    gathered = lax.dynamic_update_slice_in_dim(gathered, own, wide_at * part, 0)
    for k in range(1, wide_count):
        source = (wide_at - k) % wide_count
        got = shifted(own, "wide", k)
        gathered = lax.dynamic_update_slice_in_dim(gathered, got, source * part, 0)
    for bit in reversed(bits):
        upper = (narrow_at // bit) % 2
        other = swapped(gathered, "narrow", bit)
        gathered = jnp.where(
            upper == 0,
            jnp.concatenate([gathered, other]),
            jnp.concatenate([other, gathered]),
        )
    other = swapped(gathered, "narrow", 1)
    if whole_column:
        row_back = row_back.astype(BF16)
    else:
        returned = lax.all_to_all(
            back_blocks[0].reshape(wide_count, CAP, channels),
            "wide",
            split_axis=0,
            concat_axis=0,
            tiled=True,
        )
        row_back = jnp.take(
            returned.reshape(-1, channels), send_slot, axis=0, mode="fill", fill_value=0
        )
    cell_total = shape.cells * wide_count * narrow_count
    row_total = held_rows * wide_count * narrow_count
    sizes = [row_total, cell_total, cell_total, cell_total // 16, cell_total // 64]
    scales = np.array([1.0 / math.sqrt(size) for size in sizes], np.float32)
    totals = jnp.where(
        narrow_at % 2 == 0,
        jnp.concatenate([gathered, other]),
        jnp.concatenate([other, gathered]),
    )
    weight_grads = totals.reshape(5, channels, channels).astype(F32) * scales[:, None, None]
    return (grad_state.reshape(tile_x, tile_y, channels), row_back, weight_grads)


def solution(mesh):
    in_specs = (
        P(("groups", "wide"), "narrow", None),
        P(("groups", "wide", "narrow"), None),
        P(("groups", "wide", "narrow")),
        P(("groups", "wide", "narrow")),
        P(("groups", "wide", "narrow")),
        P(None, ("groups", "wide"), "narrow"),
        P(("groups", "wide"), "narrow", None),
        P(),
        P(),
        P(),
        P(),
        P(),
    )
    out_specs = (
        P(("groups", "wide"), "narrow", None),
        P(("groups", "wide", "narrow"), None),
        P("groups", None, None),
    )
    return jax.shard_map(local, mesh=mesh, in_specs=in_specs, out_specs=out_specs, check_vma=False)
```

```python
import functools
import math

import jax
import jax.numpy as jnp
import numpy as np
from jax import lax
from jax.experimental import pallas as pl
from jax.experimental.pallas import tpu as pltpu
from jax.sharding import PartitionSpec as P

CAP = 16
REACH = 9
NODES_OUT = 2
SIDE = 16
SLOTS = 16
LANES = 256
LONG = 10**10
VMEM_LIMIT = 48 * 1024 * 1024
F32 = jnp.float32
BF16 = jnp.bfloat16


def swapped(block, axis, bits):
    count = lax.axis_size(axis)
    return lax.ppermute(block, axis, [(i, i ^ bits) for i in range(count)])


def shifted(block, axis, step):
    count = lax.axis_size(axis)
    return lax.ppermute(block, axis, [(i, (i + step) % count) for i in range(count)])


def swapped_between(block, axis):
    count = lax.axis_size(axis)
    pairs = [(i, i + 1) for i in range(1, count - 1, 2)]
    return lax.ppermute(block, axis, pairs + [(j, i) for i, j in pairs])


def dot(left, right):
    return jnp.dot(left, right, preferred_element_type=F32)


def dot_right_t(left, right):
    return lax.dot_general(left, right, (((1,), (1,)), ((), ())), preferred_element_type=F32)


def dot_left_t(left, right):
    return lax.dot_general(left, right, (((0,), (0,)), ((), ())), preferred_element_type=F32)


def sigmoid(value):
    return 0.5 * jnp.tanh(0.5 * value) + 0.5


def silu_and_slope(value):
    logistic = sigmoid(value)
    return value * logistic, logistic * (1.0 + value * (1.0 - logistic))


def silu(value):
    return value * sigmoid(value)


def pieces(start, stop, size):
    return [(at, min(size, stop - at)) for at in range(start, stop, size)]


def two_halves(value):
    high = value.astype(BF16)
    low = (value - high.astype(F32)).astype(BF16)
    return jnp.concatenate([high, low], axis=0)


class Shape:
    def __init__(self, tile_x, tile_y):
        self.tile_x = tile_x
        self.tile_y = tile_y
        self.cells = tile_x * tile_y
        self.rows_x = tile_x + 2 * REACH
        self.halo = REACH * tile_y
        self.center = self.rows_x * tile_y
        self.side = self.rows_x * SIDE
        self.pitch = tile_y + 2 * SIDE
        self.node_x = tile_x // 4
        self.node_y = tile_y // 4
        self.out_x = self.node_x + 2 * NODES_OUT
        self.nodes = self.out_x * SLOTS
        self.edge = NODES_OUT * self.node_y
        self.own_nodes = self.node_x * self.node_y
        self.window = 6 * self.pitch
        self.side_nodes = NODES_OUT * self.out_x

    def center_row(self, at_x, at_y, kind):
        edge, own = self.edge, self.own_nodes
        if at_x < NODES_OUT:
            return kind * edge + at_x * self.node_y + at_y
        at_x -= NODES_OUT
        if at_x < self.node_x:
            return 2 * edge + kind * own + at_x * self.node_y + at_y
        at_x -= self.node_x
        return 2 * edge + 2 * own + kind * edge + at_x * self.node_y + at_y

    def tables(self):
        stack = 4 * self.edge + 2 * self.own_nodes
        side = self.side_nodes
        to_left = np.zeros((2 * side, stack), np.float32)
        to_right = np.zeros((2 * side, stack), np.float32)
        for kind in range(2):
            for at_x in range(self.out_x):
                for k in range(NODES_OUT):
                    row = kind * side + at_x * NODES_OUT + k
                    to_left[row, self.center_row(at_x, k, kind)] = 1
                    last = self.node_y - NODES_OUT + k
                    to_right[row, self.center_row(at_x, last, kind)] = 1
        place = np.zeros((2, self.nodes, stack + 4 * side), np.float32)
        for kind in range(2):
            for at_x in range(self.out_x):
                for slot in range(self.node_y + 2 * NODES_OUT):
                    at_y = slot - NODES_OUT
                    if at_y < 0:
                        column = stack + kind * side + at_x * NODES_OUT + slot
                    elif at_y < self.node_y:
                        column = self.center_row(at_x, at_y, kind)
                    else:
                        k = at_y - self.node_y
                        column = stack + 2 * side + kind * side + at_x * NODES_OUT + k
                    place[kind, at_x * SLOTS + slot, column] = 1
        spread = np.zeros((2, 128, self.window), np.float32)
        match = np.zeros((2, SLOTS, self.window), np.float32)
        for dx in range(6):
            for at in range(self.pitch):
                if at < self.tile_y:
                    y = at
                elif at < self.tile_y + SIDE:
                    y = at - self.tile_y - SIDE
                else:
                    y = at - SIDE
                quotient, rest = (y + REACH) // 4, (y + REACH) % 4
                lane = dx * self.pitch + at
                spread[0, dx * 6 + rest, lane] = 1
                if 0 <= quotient < SLOTS:
                    match[0, quotient, lane] = 1
                if rest < 2:
                    spread[1, dx * 6 + rest + 4, lane] = 1
                    if 0 <= quotient - 1 < SLOTS:
                        match[1, quotient - 1, lane] = 1
        node = np.arange(self.nodes)
        quad = node // SLOTS // 2 * SLOTS + node % SLOTS // 2
        same = (quad[:, None] == quad[None, :]).astype(np.float32)
        return {
            "to_side": np.stack([to_left, to_right]),
            "place": place,
            "spread": spread,
            "match": match,
            "quad": np.concatenate([same, same], axis=1),
        }


def open_kernel(out_ref):
    out_ref[...] = jnp.zeros(out_ref.shape, jnp.int32)


def pack_kernel(
    shape,
    units,
    place_ref,
    own_ref,
    cotangent_ref,
    mask_ref,
    rows_ref,
    target_x_ref,
    target_y_ref,
    count_ref,
    zero_ref,
    first_ref,
    second_ref,
    third_ref,
    fourth_ref,
    mesh_ref,
    own_rows_ref,
):
    edge, own_nodes, halo = shape.edge, shape.own_nodes, shape.halo
    held = rows_ref.shape[0]
    even = place_ref[0] % 2 == 0
    odd = jnp.logical_not(even)
    target_x = target_x_ref[...]
    column = target_y_ref[...] - place_ref[1] * shape.tile_y
    slot = lax.broadcasted_iota(jnp.int32, (1, held), 1)
    column = jnp.where(slot < count_ref[...] + zero_ref[0:1, 0:1], column, LANES - 1)
    line = lax.broadcasted_iota(jnp.int32, (16, held), 0)
    fields = jnp.where(line == 0, target_x // shape.tile_x, 0)
    fields = fields + jnp.where(line == 1, target_x % shape.tile_x, 0)
    fields = fields + jnp.where(line == 2, column, 0)
    lane = lax.broadcasted_iota(jnp.int32, (held, LANES), 1)
    repeat = lane % held == lax.broadcasted_iota(jnp.int32, (held, LANES), 0)
    spread = dot(fields.astype(F32).astype(BF16), jnp.where(repeat, 1.0, 0.0).astype(BF16))
    lane = lax.broadcasted_iota(jnp.int32, (16, LANES), 1)
    for number, ref in enumerate((own_rows_ref, first_ref, third_ref, fourth_ref)):
        at = ref.shape[0] - held - 16
        ref[at : at + held] = rows_ref[...]
        ref[at + held :] = jnp.where(lane // held == number, spread, 0.0).astype(BF16)

    mesh_ref[:own_nodes] = cotangent_ref[...]
    mesh_ref[own_nodes:] = jnp.zeros((own_nodes, mesh_ref.shape[1]), BF16)
    mesh_ref[own_nodes:, : mask_ref.shape[1]] = mask_ref[...].astype(F32).astype(BF16)
    for ref, upward in ((first_ref, even), (second_ref, odd)):
        start = pl.multiple_of(jnp.where(upward, shape.cells - halo, 0), shape.tile_y)
        ref[:halo] = own_ref[pl.ds(start, halo)]
        start = pl.multiple_of(jnp.where(upward, own_nodes - edge, 0), 16)
        ref[halo : halo + edge] = mesh_ref[pl.ds(start, edge)]
        start = pl.multiple_of(jnp.where(upward, 2 * own_nodes - edge, own_nodes), 16)
        ref[halo + edge : halo + 2 * edge] = mesh_ref[pl.ds(start, edge)]


def blend_kernel(shape, units, unit_rows, *refs):
    (place_ref, own_ref, mesh_ref, w_force_ref, side_ref, own_rows_ref) = refs[:6]
    count = units if units > 3 else 2
    arrived = refs[6 : 6 + count]
    (blended_ref, first_ref, second_ref, stack_ref, rows_ref, key_ref) = refs[6 + count : 12 + count]
    (projected_ref,) = refs[12 + count :]
    wide_at = place_ref[0]
    even = wide_at % 2 == 0
    near, between = arrived[0], arrived[1]
    mesh = 2 * shape.edge
    first_row = shape.halo + mesh

    def held(k, at, n):
        if k == 0:
            return own_rows_ref[at : at + n]
        if k == 1 or units == 3:
            return arrived[k - 1][first_row + at : first_row + at + n]
        return arrived[k][at : at + n]

    total = unit_rows * units
    for k in range(units):
        rows_ref[k * unit_rows : (k + 1) * unit_rows] = held(k, 0, unit_rows)
    blocks = []
    if total <= LANES:
        metas = [held(k, unit_rows, 16).astype(F32) for k in range(units)]
        blocks.append(functools.reduce(lambda a, b: a + b, metas)[:, :total])
    else:
        for k in range(units):
            for part in range(unit_rows // LANES):
                blocks.append(held(k, unit_rows + 16 * part, 16).astype(F32))
    keys = []
    for block in blocks:
        whole = block.astype(jnp.int32)
        at_x = whole[0:1] * shape.tile_x + whole[1:2] - wide_at * shape.tile_x + REACH
        at_y = whole[2:3]
        inside = (at_x >= 0) & (at_x < shape.rows_x) & (at_y < shape.tile_y)
        keys.append(jnp.where(inside, at_x * shape.tile_y + at_y, -1))
    width = keys[0].shape[1]
    for k, key in enumerate(keys):
        key_ref[:, k * width : (k + 1) * width] = jnp.broadcast_to(key, (8, width))
    projected_ref[...] = dot(rows_ref[...], w_force_ref[...]).astype(BF16)

    def facing(at, n, forward):
        one, other = near[at : at + n], between[at : at + n]
        return jnp.where(even, one, other) if forward else jnp.where(even, other, one)

    stack = jnp.concatenate(
        [facing(shape.halo, mesh, False), mesh_ref[...], facing(shape.halo, mesh, True)], axis=0
    )
    stack_ref[...] = stack
    narrow_even = place_ref[1] % 2 == 0
    to_left = dot(side_ref[0], stack).astype(BF16)
    to_right = dot(side_ref[1], stack).astype(BF16)
    first_ref[shape.side :] = jnp.where(narrow_even, to_right, to_left)
    second_ref[shape.side :] = jnp.where(narrow_even, to_left, to_right)

    tile_y = shape.tile_y
    inner = shape.halo + shape.cells
    jobs = [(0, at, n) for at, n in pieces(0, shape.halo, 3 * tile_y)]
    jobs += [(shape.halo, at, n) for at, n in pieces(0, shape.cells, 4 * tile_y)]
    jobs += [(inner, at, n) for at, n in pieces(0, shape.halo, 3 * tile_y)]
    for base, at, n in jobs:
        first = base + at
        if base == shape.halo:
            value = own_ref[at : at + n].astype(F32)
        else:
            value = facing(at, n, base == inner).astype(F32)
        cell = lax.broadcasted_iota(jnp.int32, (n, width), 0) + first
        for k, key in enumerate(keys):
            hit = jnp.where(cell == key, 1.0, 0.0).astype(BF16)
            value = value + dot(hit, projected_ref[k * width : (k + 1) * width])
        value = value.astype(BF16)
        blended_ref[first : first + n] = value
        for t in range(n // tile_y):
            row = first // tile_y + t
            target = slice(row * SIDE, (row + 1) * SIDE)
            low = value[t * tile_y : t * tile_y + SIDE]
            high = value[(t + 1) * tile_y - SIDE : (t + 1) * tile_y]
            first_ref[target] = jnp.where(narrow_even, high, low)
            second_ref[target] = jnp.where(narrow_even, low, high)


def forward_kernel(
    shape, blended_ref, w_embed_ref, w_message_ref, message_ref, latent_ref, embed_ref, slope_ref
):
    inner = shape.halo + shape.cells
    jobs = pieces(0, shape.halo, 96) + pieces(shape.halo, inner, 128)
    jobs += pieces(inner, shape.center, 96)
    for at, n in jobs:
        blended = blended_ref[at : at + n]
        pre_embed = dot(blended, w_embed_ref[...])
        value, slope = silu_and_slope(pre_embed)
        latent = (blended.astype(F32) + value).astype(BF16)
        pre_message = dot(latent, w_message_ref[...])
        message, message_slope = silu_and_slope(pre_message)
        message_ref[at : at + n] = message.astype(BF16)
        if shape.halo <= at < inner:
            own = at - shape.halo
            latent_ref[own : own + n] = latent
            embed_ref[own : own + n] = slope
            slope_ref[own : own + n] = message_slope


def backward_kernel(shape, total_rows, *refs):
    (
        narrow_ref,
        second_ref,
        first_ref,
        stack_ref,
        blended_ref,
        message_ref,
        latent_ref,
        embed_ref,
        slope_ref,
        rows_ref,
        key_ref,
        place_ref,
        spread_ref,
        match_ref,
        quad_ref,
        w_force_ref,
        w_embed_ref,
        w_message_ref,
        w_one_ref,
        w_two_ref,
        state_ref,
        back_ref,
        sent_ref,
        kept_ref,
        padded_ref,
        level_ref,
        cover_ref,
        pmb_ref,
        peb_ref,
        grads_ref,
    ) = refs
    tile_y, pitch = shape.tile_y, shape.pitch
    channels = blended_ref.shape[1]

    even = narrow_ref[0] % 2 == 0
    first_at = pl.multiple_of(tile_y + jnp.where(even, SIDE, 0), SIDE)
    second_at = pl.multiple_of(tile_y + jnp.where(even, 0, SIDE), SIDE)
    for ref, offset in ((first_ref, first_at), (second_ref, second_at)):
        for at, n in pieces(0, shape.side, 8 * SIDE):
            blended = ref[at : at + n]
            latent = (blended.astype(F32) + silu(dot(blended, w_embed_ref[...]))).astype(BF16)
            message = silu(dot(latent, w_message_ref[...])).astype(BF16)
            for t in range(n // SIDE):
                row = (at // SIDE + t) * pitch + offset
                padded_ref[pl.ds(row, SIDE)] = message[t * SIDE : (t + 1) * SIDE]
    for row in range(shape.rows_x):
        padded_ref[row * pitch : row * pitch + tile_y] = message_ref[
            row * tile_y : (row + 1) * tile_y
        ]

    first, second = first_ref[shape.side :], second_ref[shape.side :]
    stack = jnp.concatenate(
        [stack_ref[...], jnp.where(even, second, first), jnp.where(even, first, second)], axis=0
    )
    cotangent = dot(place_ref[0], stack)
    mask = dot(place_ref[1], stack[:, :128]).astype(BF16)
    near = dot(mask, spread_ref[0])
    far = dot(mask, spread_ref[1])
    windows = []
    for at_x in range(shape.out_x):
        rows = slice(at_x * SLOTS, (at_x + 1) * SLOTS)
        windows.append(near[rows] * match_ref[0] + far[rows] * match_ref[1])
        level_ref[rows] = (
            dot(
                windows[-1].astype(BF16),
                padded_ref[4 * at_x * pitch : 4 * at_x * pitch + shape.window],
            )
            / 6.0
        ).astype(BF16)
    turned = jnp.concatenate(windows, axis=0).T
    node_x = lax.broadcasted_iota(jnp.int32, (tile_y, shape.nodes), 1) // SLOTS
    for at_x in range(shape.tile_x):
        quotient, rest = (at_x + REACH) // 4, (at_x + REACH) % 4
        cover = jnp.where(node_x == quotient, turned[rest * pitch : rest * pitch + tile_y], 0.0)
        if rest < 2:
            again = (rest + 4) * pitch
            cover = cover + jnp.where(
                node_x == quotient - 1, turned[again : again + tile_y], 0.0
            )
        cover = cover.astype(BF16)
        cover_ref[at_x * tile_y : (at_x + 1) * tile_y] = jnp.concatenate([cover, cover], axis=1)

    level_one = level_ref[...]
    pre_one = dot(level_one, w_one_ref[...])
    value, slope_one = silu_and_slope(pre_one)
    state_one = level_one.astype(F32) + value
    level_two = (0.25 * dot(quad_ref[...], two_halves(state_one))).astype(BF16)
    pre_two = dot(level_two, w_two_ref[...])
    two_bar = dot(quad_ref[:, : shape.nodes], cotangent.astype(BF16))
    pre_two_bar = (two_bar * silu_and_slope(pre_two)[1]).astype(BF16)
    pooled_bar = two_bar + dot_right_t(pre_two_bar, w_two_ref[...])
    one_bar = cotangent + 0.25 * pooled_bar
    pre_one_bar = (one_bar * slope_one).astype(BF16)
    level_bar = one_bar + dot_right_t(pre_one_bar, w_one_ref[...])

    node = lax.broadcasted_iota(jnp.int32, (shape.nodes, channels), 0)
    at_x, at_y = node // SLOTS, node % SLOTS
    owned = (at_x >= NODES_OUT) & (at_x < NODES_OUT + shape.node_x)
    owned = owned & (at_y >= NODES_OUT) & (at_y < NODES_OUT + shape.node_y)
    first = owned & (at_x % 2 == 0) & (at_y % 2 == 0)
    grads_ref[3 * channels : 4 * channels] = dot_left_t(
        level_one, jnp.where(owned, pre_one_bar.astype(F32), 0.0).astype(BF16)
    )
    grads_ref[4 * channels :] = dot_left_t(
        level_two, jnp.where(first, pre_two_bar.astype(F32), 0.0).astype(BF16)
    )

    both = two_halves(level_bar)
    for at, n in pieces(0, shape.cells, 128):
        rows = slice(at, at + n)
        message_bar = dot(cover_ref[rows], both) / 6.0
        pre_message_bar = (message_bar * slope_ref[rows]).astype(BF16)
        pmb_ref[rows] = pre_message_bar
        latent_bar = dot_right_t(pre_message_bar, w_message_ref[...])
        pre_embed_bar = (latent_bar * embed_ref[rows]).astype(BF16)
        peb_ref[rows] = pre_embed_bar
        state_ref[rows] = (latent_bar + dot_right_t(pre_embed_bar, w_embed_ref[...])).astype(BF16)
    own = slice(shape.halo, shape.halo + shape.cells)
    grads_ref[channels : 2 * channels] = dot_left_t(blended_ref[own], peb_ref[...])
    grads_ref[2 * channels : 3 * channels] = dot_left_t(latent_ref[...], pmb_ref[...])

    width = min(total_rows, LANES)
    cell = lax.broadcasted_iota(jnp.int32, (shape.cells, width), 0) + shape.halo
    grad_force = None
    for at in range(0, total_rows, width):
        rows = slice(at, at + width)
        hit = jnp.where(cell == key_ref[0:1, rows], 1.0, 0.0).astype(BF16)
        slot_bar = dot_left_t(hit, state_ref[...]).astype(BF16)
        back_ref[rows] = dot_right_t(slot_bar, w_force_ref[...]).astype(BF16)
        term = dot_left_t(rows_ref[rows], slot_bar)
        grad_force = term if grad_force is None else grad_force + term
    grads_ref[:channels] = grad_force

    half = sent_ref.shape[0]
    upper = narrow_ref[0] % 2
    kept_at = pl.multiple_of(upper * half, half)
    sent_at = pl.multiple_of((1 - upper) * half, half)
    sent_ref[...] = grads_ref[pl.ds(sent_at, half)].astype(BF16)
    kept_ref[...] = grads_ref[pl.ds(kept_at, half)]


def call(kernel, out_shapes, operands, scratch=(), spaces="", out_space=pltpu.VMEM, flops=0):
    kinds = {"s": pltpu.SMEM, "v": pltpu.VMEM}
    spaces = spaces + "v" * (len(operands) - len(spaces))
    moved = sum(math.prod(o.shape) * o.dtype.itemsize for o in list(operands) + list(out_shapes))
    return pl.pallas_call(
        kernel,
        out_shape=tuple(out_shapes),
        in_specs=[pl.BlockSpec(memory_space=kinds[space]) for space in spaces],
        out_specs=tuple(pl.BlockSpec(memory_space=out_space) for _ in out_shapes),
        scratch_shapes=list(scratch),
        compiler_params=pltpu.CompilerParams(vmem_limit_bytes=VMEM_LIMIT),
        cost_estimate=pl.CostEstimate(flops=flops, bytes_accessed=moved, transcendentals=0),
    )(*operands)


def meta_rows(live, target_x, target_y, tile_x, unit_rows, slot, units):
    high = target_x // tile_x
    low = target_x % tile_x
    column = jnp.where(live, target_y, LANES - 1)
    fields = jnp.stack([high, low, column]).astype(F32)
    if unit_rows * units <= LANES:
        before = slot * unit_rows
        after = LANES - before - unit_rows
        return jnp.pad(fields, ((0, 13), (before, after))).astype(BF16)
    blocks = unit_rows // LANES
    fields = fields.reshape(3, blocks, LANES).transpose(1, 0, 2)
    return jnp.pad(fields, ((0, 0), (0, 13), (0, 0))).reshape(16 * blocks, LANES).astype(BF16)


def local(
    grid_state,
    boundary_rows,
    row_count,
    target_x,
    target_y,
    g2m_mask,
    mesh_cotangent,
    w_force,
    w_embed,
    w_message,
    w_level_one,
    w_level_two,
):
    tile_x, tile_y, channels = grid_state.shape
    wide_count = lax.axis_size("wide")
    narrow_count = lax.axis_size("narrow")
    wide_at = lax.axis_index("wide")
    narrow_at = lax.axis_index("narrow")
    held_rows = boundary_rows.shape[0]
    shape = Shape(tile_x, tile_y)
    table = shape.tables()
    table = {
        name: jnp.asarray(value, F32 if name == "match" else BF16)
        for name, value in table.items()
    }

    live = jnp.arange(held_rows) < row_count[0]
    column = target_y - narrow_at * tile_y
    whole_column = wide_count == 4 and held_rows * wide_count <= LANES
    if whole_column:
        units = wide_count
        unit_rows = held_rows
        rows, row_live, row_x, row_y = boundary_rows, live, target_x, column
    else:
        slot_count = wide_count * CAP
        destination = target_x // tile_x
        matches = (destination[:, None] == jnp.arange(wide_count)[None, :]) & live[:, None]
        running = jnp.cumsum(matches.astype(jnp.int32), axis=0) - 1
        slot_index = jnp.sum(jnp.where(matches, running, 0), axis=1)
        send_slot = jnp.where(live, destination * CAP + slot_index, slot_count)
        cells = jnp.full((slot_count,), -1, jnp.int32)
        cells = cells.at[send_slot].set(target_x % tile_x * tile_y + column, mode="drop")
        outgoing = jnp.zeros((slot_count, channels), BF16)
        outgoing = outgoing.at[send_slot].set(boundary_rows, mode="drop")
        outgoing = outgoing.reshape(wide_count, CAP, channels)
        rows = lax.all_to_all(outgoing, "wide", split_axis=0, concat_axis=0, tiled=True)
        cells = lax.all_to_all(
            cells.reshape(wide_count, CAP), "wide", split_axis=0, concat_axis=0, tiled=True
        )
        rows = rows.reshape(slot_count, channels)
        cells = cells.reshape(slot_count)
        units = 3
        unit_rows = slot_count
        row_live = cells >= 0
        row_x = jnp.where(row_live, wide_at * tile_x + cells // tile_y, 0)
        row_y = cells % tile_y

    cells = grid_state.reshape(-1, channels)
    cotangent = mesh_cotangent.reshape(-1, channels)
    mask = g2m_mask.transpose(1, 2, 0).reshape(-1, 36)
    place = jnp.stack([wide_at, narrow_at])
    struct = jax.ShapeDtypeStruct
    long = struct((shape.halo + 2 * shape.edge + unit_rows + 16, channels), BF16)
    plain = struct((shape.halo + 2 * shape.edge, channels), BF16)
    short = struct((unit_rows + 16, channels), BF16)
    (zero,) = call(open_kernel, [struct((8, 128), jnp.int32)], [], flops=LONG)
    if whole_column:
        first, second, third, fourth, mesh, own_rows = call(
            functools.partial(pack_kernel, shape, units),
            [long, plain, short, short, struct((2 * shape.own_nodes, channels), BF16), short],
            [
                place,
                cells,
                cotangent,
                mask,
                rows,
                target_x.reshape(1, -1),
                target_y.reshape(1, -1),
                row_count.reshape(1, 1),
                zero,
            ],
            spaces="s",
            flops=LONG,
        )
        third = swapped(third, "wide", 2)
        fourth = swapped(fourth, "wide", 3)
        first_in = swapped(first, "wide", 1)
        arrived = [first_in, swapped_between(second, "wide"), third, fourth]
    else:

        def with_meta(slot):
            return [rows, meta_rows(row_live, row_x, row_y, tile_x, unit_rows, slot, units)]

        mask = jnp.pad(mask.astype(BF16), ((0, 0), (0, channels - 36)))
        mesh = jnp.concatenate([cotangent, mask])
        own_rows = jnp.concatenate(with_meta(0))
        edge = shape.edge
        to_prev = [cells[: shape.halo], cotangent[:edge], mask[:edge]]
        to_next = [cells[-shape.halo :], cotangent[-edge:], mask[-edge:]]
        to_prev, to_next = jnp.concatenate(to_prev), jnp.concatenate(to_next)
        upward = wide_at % 2 == 0
        first = jnp.concatenate([jnp.where(upward, to_next, to_prev)] + with_meta(1))
        second = jnp.concatenate([jnp.where(upward, to_prev, to_next)] + with_meta(2))
        arrived = [swapped(first, "wide", 1), swapped_between(second, "wide")]

    total_rows = unit_rows * units
    stack_rows = 4 * shape.edge + 2 * shape.own_nodes
    payload = struct((shape.side + 2 * shape.side_nodes, channels), BF16)
    blended, first, second, stack, all_rows, keys = call(
        functools.partial(blend_kernel, shape, units, unit_rows),
        [
            struct((shape.center, channels), BF16),
            payload,
            payload,
            struct((stack_rows, channels), BF16),
            struct((total_rows, channels), BF16),
            struct((8, total_rows), jnp.int32),
        ],
        [place, cells, mesh, w_force, table["to_side"], own_rows] + arrived,
        scratch=[pltpu.VMEM((total_rows, channels), BF16)],
        spaces="s",
        flops=2 * shape.center * total_rows * channels,
    )
    second = swapped_between(second, "narrow")
    first = swapped(first, "narrow", 1)
    message, latent, embed_slope, message_slope = call(
        functools.partial(forward_kernel, shape),
        [
            struct((shape.center, channels), BF16),
            struct((shape.cells, channels), BF16),
            struct((shape.cells, channels), F32),
            struct((shape.cells, channels), F32),
        ],
        [blended, w_embed, w_message],
        flops=4 * shape.center * channels * channels,
    )
    grad_rows_total = 5 * channels
    grad_state, back, sent, kept = call(
        functools.partial(backward_kernel, shape, total_rows),
        [
            struct((shape.cells, channels), BF16),
            struct((total_rows, channels), BF16),
            struct((grad_rows_total // 2, channels), BF16),
            struct((grad_rows_total // 2, channels), F32),
        ],
        [
            narrow_at.reshape(1),
            second,
            first,
            stack,
            blended,
            message,
            latent,
            embed_slope,
            message_slope,
            all_rows,
            keys,
            table["place"],
            table["spread"],
            table["match"],
            table["quad"],
            w_force,
            w_embed,
            w_message,
            w_level_one,
            w_level_two,
        ],
        scratch=[
            pltpu.VMEM((shape.rows_x * shape.pitch, channels), BF16),
            pltpu.VMEM((shape.nodes, channels), BF16),
            pltpu.VMEM((shape.cells, 2 * shape.nodes), BF16),
            pltpu.VMEM((shape.cells, channels), BF16),
            pltpu.VMEM((shape.cells, channels), BF16),
            pltpu.VMEM((grad_rows_total, channels), F32),
        ],
        spaces="s",
        flops=12 * shape.cells * channels * channels,
    )

    piece = kept + swapped(sent, "narrow", 1).astype(F32)
    back_blocks = back.reshape(units, unit_rows, channels)
    row_back = back_blocks[0].astype(F32)
    bits = [1 << k for k in range(1, narrow_count.bit_length() - 1)]
    for bit in bits:
        half = piece.shape[0] // 2
        upper = (narrow_at // bit) % 2
        sent = lax.dynamic_slice_in_dim(piece, (1 - upper) * half, half).astype(BF16)
        kept = lax.dynamic_slice_in_dim(piece, upper * half, half)
        piece = kept + swapped(sent, "narrow", bit).astype(F32)
    part = piece.shape[0] // wide_count
    rounded = piece.astype(BF16)
    own = lax.dynamic_slice_in_dim(piece, wide_at * part, part)
    for k in range(1, wide_count):
        target = (wide_at + k) % wide_count
        sent = lax.dynamic_slice_in_dim(rounded, target * part, part)
        if whole_column:
            block = lax.dynamic_slice_in_dim(back_blocks, target ^ wide_at, 1)
            sent = jnp.concatenate([sent, block[0]])
        got = shifted(sent, "wide", k).astype(F32)
        own = own + got[:part]
        if whole_column:
            row_back = row_back + got[part:]
    own = own.astype(BF16)
    gathered = jnp.zeros((wide_count * part, channels), BF16)
    gathered = lax.dynamic_update_slice_in_dim(gathered, own, wide_at * part, 0)
    for k in range(1, wide_count):
        source = (wide_at - k) % wide_count
        got = shifted(own, "wide", k)
        gathered = lax.dynamic_update_slice_in_dim(gathered, got, source * part, 0)
    for bit in reversed(bits):
        upper = (narrow_at // bit) % 2
        other = swapped(gathered, "narrow", bit)
        gathered = jnp.where(
            upper == 0,
            jnp.concatenate([gathered, other]),
            jnp.concatenate([other, gathered]),
        )
    other = swapped(gathered, "narrow", 1)
    if whole_column:
        row_back = row_back.astype(BF16)
    else:
        returned = lax.all_to_all(
            back_blocks[0].reshape(wide_count, CAP, channels),
            "wide",
            split_axis=0,
            concat_axis=0,
            tiled=True,
        )
        row_back = jnp.take(
            returned.reshape(-1, channels), send_slot, axis=0, mode="fill", fill_value=0
        )
    cell_total = shape.cells * wide_count * narrow_count
    row_total = held_rows * wide_count * narrow_count
    sizes = [row_total, cell_total, cell_total, cell_total // 16, cell_total // 64]
    scales = np.array([1.0 / math.sqrt(size) for size in sizes], np.float32)
    totals = jnp.where(
        narrow_at % 2 == 0,
        jnp.concatenate([gathered, other]),
        jnp.concatenate([other, gathered]),
    )
    weight_grads = totals.reshape(5, channels, channels).astype(F32) * scales[:, None, None]
    return (grad_state.reshape(tile_x, tile_y, channels), row_back, weight_grads)


def solution(mesh):
    in_specs = (
        P(("groups", "wide"), "narrow", None),
        P(("groups", "wide", "narrow"), None),
        P(("groups", "wide", "narrow")),
        P(("groups", "wide", "narrow")),
        P(("groups", "wide", "narrow")),
        P(None, ("groups", "wide"), "narrow"),
        P(("groups", "wide"), "narrow", None),
        P(),
        P(),
        P(),
        P(),
        P(),
    )
    out_specs = (
        P(("groups", "wide"), "narrow", None),
        P(("groups", "wide", "narrow"), None),
        P("groups", None, None),
    )
    return jax.shard_map(local, mesh=mesh, in_specs=in_specs, out_specs=out_specs, check_vma=False)
```
